128 devices in a mesh: row: 8 (over x, core), col: 16 (over z, y).
Axes of the slice: x: 4, y: 4, z: 4, core: 2. Of those that a mesh axis runs over, the one named last changes fastest.
Arguments:
- right_side: float32 [1024, 2, 256], P(('row', 'col')), may hold values from -12 to 12
- anchor: float32 [1024, 256], P(('row', 'col')), may hold values from 0.3 to 3
- tiles: float32 [1024, 4, 256, 256], P(('row', 'col')), may hold values from 0 to 1, as said below
- neighbours: int32 [1024, 4], P(('row', 'col')), may hold values from 0 to 1023, as said below
- owners: int32 [262144, 1], P(('row', 'col')), may hold values from 0 to 127; in each aligned block of 2048 rows (0 to 2047, 2048 to 4095, ...) at most 32 rows name the same one
- row_offset: int32 [262144], P(('row', 'col')), may hold values from 0 to 2047
- col_offset: int32 [262144], P(('row', 'col')), may hold values from 0 to 511
- macro_density: float32 [16384, 8192], P('row', 'col'), may hold values from 0.05 to 1
Outputs:
- solution: float32 [1024, 2, 256], P(('row', 'col'))
- density: float32 [16384, 8192], P('row', 'col')
The draws below stay inside these ranges and needn't reach their ends.
Inputs may be any that keep to these rules, and one draw needn't show every extreme that they name: `owners`: at most 32 of the clusters of one device name the same owner; in every draw the clusters of some device name one owner exactly 32 times. `neighbours`: block b lies on device b // 8, and device d on mesh position (d // 16, d % 16) of row and col. Every tile names a block on the device of its own block row or on a device next to it along row, col or both (diagonals included). `tiles`: entries are positive.
All inputs are finite; a program needn't handle non-finite values.
Results may differ from the reference program's by a relative error of at most 0.0003.
Values sent between devices are 32-bit elements; how exact they have to be, the bound alone decides.
A program may use at most 128 MiB of HBM per device.

```python
import math
import jax
import jax.numpy as jnp
import numpy as np
from jax import lax

BS = 256
K = 4
ITERS = 3
STEPS = 4
NB_DEV = 8
GX_DEV = 2048
GY_DEV = 512
NBLK = 1024
CLU_DEV = 2048
CLUSTERS = 262144
CAP = 32
GROWS = 16384
GCOLS = 8192
N_ROW = 8
N_COL = 16


def draw_tiles(key, part):
    sample = jax.random.uniform(key, (NBLK, K, BS, BS), jnp.float32)
    weights = jnp.exp(jnp.log(0.02) - jnp.log(0.02) * sample)
    return weights * (2.0 / (K * BS))


def draw_right_side(key, part):
    rising = 1.0 + 2.0 * jnp.arange(NBLK, dtype=jnp.float32) / max(NBLK - 1, 1)
    values = jnp.clip(jax.random.normal(key, (NBLK, 2, BS), jnp.float32), -4.0, 4.0)
    return values * rising[:, None, None]


def draw_neighbours(key, part):
    first_key, second_key, third_key = jax.random.split(jax.random.fold_in(key, 17), 3)
    block_ids = jnp.arange(NBLK, dtype=jnp.int32)
    device_ids = block_ids // NB_DEV
    mesh_row = device_ids // N_COL
    mesh_col = device_ids % N_COL
    step_row = jax.random.randint(first_key, (NBLK, K), -1, 2, jnp.int32)
    step_col = jax.random.randint(second_key, (NBLK, K), -1, 2, jnp.int32)
    local_block = jax.random.randint(third_key, (NBLK, K), 0, NB_DEV, jnp.int32)
    near_row = jnp.clip(mesh_row[:, None] + step_row, 0, N_ROW - 1)
    near_col = jnp.clip(mesh_col[:, None] + step_col, 0, N_COL - 1)
    return ((near_row * N_COL + near_col) * NB_DEV + local_block).astype(jnp.int32)


def place_ends(drawn, rng, smallest, high):
    place = [jax.random.randint(jax.random.fold_in(rng, axis), (), 0, length) for axis, length in enumerate(drawn.shape)]
    widest = drawn.shape.index(max(drawn.shape))
    next_to = place[:widest] + [(place[widest] + 1) % drawn.shape[widest]] + place[widest + 1:]
    return drawn.at[tuple(place)].set(smallest).at[tuple(next_to)].set(high)


def block_levels(own_key, dims, cuts, least, largest):
    loudness, own = 1.0, jax.random.fold_in(own_key, 6)
    for dim, shards_of in cuts:
        heights = jnp.exp(jax.random.uniform(jax.random.fold_in(own, dim), (shards_of,), jnp.float32, least / len(cuts), largest / len(cuts)))
        loudness = loudness * jnp.repeat(heights, dims[dim] // shards_of).reshape([-1 if axis == dim else 1 for axis in range(len(dims))])
    return loudness


def routed_block(key, own, number, rows, count, top, most, lean):
    ranking = jax.random.permutation(key, count)
    packed, usual = shares(count, rows * top, most, lean, True), shares(count, rows * top, most, lean, False)
    places = jnp.arange(count)

    def named(tallies, turn):
        used = int((tallies > 0).sum())
        fixed = max(1, used // 4)
        passed = fixed + (places - fixed + turn * (used - fixed)) % max(1, count - fixed)
        return jnp.zeros((count,), jnp.int32).at[ranking[jnp.where(places < fixed, places, passed)]].set(jnp.asarray(tallies, jnp.int32))

    tallies = jnp.where(number % 4 == 0, named(packed, number // 4), named(usual, number - number // 4 - 1))
    mixed = jax.random.permutation(jax.random.fold_in(own, 3), count)
    giver, sink = mixed[0:count // 2 * 2:2], mixed[1:count // 2 * 2:2]
    slack = jnp.minimum(tallies[giver] - 1, most - tallies[sink]) // 2
    slack = jnp.where((giver == ranking[0]) | (sink == ranking[0]) | (tallies[sink] == 0), 0, jnp.maximum(slack, 0))
    passed = jax.random.randint(jax.random.fold_in(own, 4), (count // 2,), 0, 1 << 20) % (slack + 1)
    tallies = tallies.at[giver].add(-passed).at[sink].add(passed)
    items = jnp.searchsorted(jnp.cumsum(tallies), jnp.arange(rows * top), side="right").astype(jnp.int32)
    table = items.reshape(top, rows).T
    table = table[jax.random.permutation(jax.random.fold_in(own, 1), rows)]
    turn = jax.random.randint(jax.random.fold_in(own, 2), (rows, 1), 0, top)
    return jnp.take_along_axis(table, (jnp.arange(top)[None, :] + turn) % top, axis=1)


def shares(number_of, total, bound, lean, full):
    loads = [(1 << 20) // math.isqrt(grade ** lean) + 1 for grade in range(1, number_of + 1)]
    largest = bound if full else min(bound, max(-(-total // number_of), total * loads[0] // sum(loads)))
    least = 1 if total - largest >= number_of - 1 else 0
    holding, spare = [largest] + [least] * (number_of - 1), total - largest - least * (number_of - 1)
    while spare > 0:
        candidates = [i for i in range(1, number_of) if holding[i] < largest] or [i for i in range(1, number_of) if holding[i] < bound]
        mass, left = sum([loads[i] for i in candidates]), spare
        for i in candidates:
            extra = min(bound - holding[i], max(1, left * loads[i] // mass), spare)
            holding[i] = holding[i] + extra
            spare = spare - extra
    return np.array(holding)


def setup_inputs(seed: int = 0) -> dict:
    key_of = jax.random.split(jax.random.key(seed), 9)
    right_side = draw_right_side(jax.random.fold_in(key_of[8], 71), 0)
    anchor = jnp.clip(jnp.exp(math.log(3.0) - 2.3025851 * jax.random.uniform(key_of[1], (NBLK, BS), jnp.float32) ** block_levels(key_of[1], (NBLK, BS), ((0, 128),), -0.2, 0.2)), 0.3, 3.0)
    tiles = draw_tiles(jax.random.fold_in(key_of[8], 71), 0)
    neighbours = draw_neighbours(jax.random.fold_in(key_of[8], 71), 0)
    owners_keys = jax.random.split(jax.random.fold_in(key_of[4], 1), CLUSTERS // CLU_DEV)
    owners_turns = jax.random.permutation(jax.random.fold_in(key_of[4], 3), CLUSTERS // CLU_DEV)
    owners = jax.vmap(lambda own, number: routed_block(jax.random.fold_in(key_of[4], 2), own, number, CLU_DEV, N_ROW * N_COL, 1, CAP, 2))(owners_keys, owners_turns).reshape((CLUSTERS, 1))
    row_offset = place_ends(jax.random.randint(key_of[5], (CLUSTERS,), 0, GX_DEV), jax.random.fold_in(key_of[5], 1), 0, GX_DEV - 1).astype(jnp.int32)
    col_offset = place_ends(jax.random.randint(key_of[6], (CLUSTERS,), 0, GY_DEV), jax.random.fold_in(key_of[6], 1), 0, GY_DEV - 1).astype(jnp.int32)
    macro_density = jnp.clip(jnp.exp(math.log(1.0) - 2.9957323 * jax.random.uniform(key_of[7], (GROWS, GCOLS), jnp.float32) ** block_levels(key_of[7], (GROWS, GCOLS), ((0, 8), (1, 16)), -0.2, 0.2)), 0.05, 1.0)
    return dict(right_side=right_side, anchor=anchor, tiles=tiles, neighbours=neighbours, owners=owners, row_offset=row_offset, col_offset=col_offset, macro_density=macro_density)


HIGH = lax.Precision.HIGHEST
RATE = 0.2


def laplace_image(field, tiles, neighbours, anchor, row_sums, col_sums):
    remote = field[neighbours]
    direct = jnp.einsum('bkij,bkcj->bci', tiles, remote, precision=HIGH)
    backward = jnp.einsum('bkij,bci->bkcj', tiles, field, precision=HIGH)
    row_part = row_sums[:, None, :] * field - direct
    col_part = col_sums[:, :, None, :] * remote - backward
    scattered = jax.ops.segment_sum(col_part.reshape(-1, 2, BS), neighbours.reshape(-1), num_segments=NBLK)
    return anchor[:, None, :] * field + row_part + scattered


def window_bells(position, limit):
    start_cell = jnp.clip(jnp.floor(position).astype(jnp.int32) - 7, 0, limit - 16)
    cells = start_cell[:, None] + jnp.arange(16, dtype=jnp.int32)[None, :]
    offset = cells.astype(jnp.float32) - position[:, None]
    bells = jnp.exp(-0.5 * offset * offset).astype(jnp.bfloat16).astype(jnp.float32)
    return cells, bells


def reference(right_side, anchor, tiles, neighbours, owners, row_offset, col_offset, macro_density):
    row_sums = jnp.sum(jnp.sum(tiles, axis=3), axis=1)
    col_sums = jnp.sum(tiles, axis=2)
    solution = jnp.zeros_like(right_side)
    residual = right_side
    direction = right_side
    norm_now = jnp.sum(residual * residual, axis=(0, 2))
    for sweep in range(ITERS):
        image = laplace_image(direction, tiles, neighbours, anchor, row_sums, col_sums)
        alpha = norm_now / jnp.sum(direction * image, axis=(0, 2))
        solution = solution + alpha[None, :, None] * direction
        residual = residual - alpha[None, :, None] * image
        norm_next = jnp.sum(residual * residual, axis=(0, 2))
        direction = residual + (norm_next / norm_now)[None, :, None] * direction
        norm_now = norm_next
    pos_row = row_offset.astype(jnp.float32) + 3.0 * jnp.tanh(solution[:, 0, :].reshape(-1))
    pos_col = col_offset.astype(jnp.float32) + 3.0 * jnp.tanh(solution[:, 1, :].reshape(-1))
    owner = owners[:, 0]
    cells_row, bells_row = window_bells(pos_row, GX_DEV)
    cells_col, bells_col = window_bells(pos_col, GY_DEV)
    glob_row = (owner // N_COL * GX_DEV)[:, None] + cells_row
    glob_col = (owner % N_COL * GY_DEV)[:, None] + cells_col
    outer = bells_row[:, :, None] * bells_col[:, None, :]
    spread = jnp.zeros(macro_density.shape, jnp.float32).at[glob_row[:, :, None], glob_col[:, None, :]].add(outer)
    field = macro_density + spread
    for sweep in range(STEPS):
        padded = jnp.pad(field, 1)
        centre = padded[1:-1, 1:-1]
        field = centre + RATE * (padded[2:, 1:-1] + padded[:-2, 1:-1] + padded[1:-1, 2:] + padded[1:-1, :-2] - 4.0 * centre)
    return solution, field
```

```python
import functools

import jax
import jax.numpy as jnp
from jax import lax
from jax.experimental import pallas as pl
from jax.experimental.pallas import tpu as pltpu
from jax.sharding import PartitionSpec as P

MESH = pl.DeviceIdType.MESH
F32 = jnp.float32
BF16 = jnp.bfloat16
STEPS = 4
CAP = 32
NONE = -1000.0
AROUND = [(dr, dc) for dr in (-1, 0, 1) for dc in (-1, 0, 1)]


def nt_dot(a, b):
    return lax.dot_general(a, b, (((1,), (1,)), ((), ())), preferred_element_type=F32)


def nn_dot(a, b):
    return jnp.dot(a, b, preferred_element_type=F32)


def split3(x):
    hi = x.astype(BF16)
    rest = x - hi.astype(F32)
    mid = rest.astype(BF16)
    low = (rest - mid.astype(F32)).astype(BF16)
    return hi, mid, low


def iota(shape, dim):
    return lax.broadcasted_iota(jnp.int32, shape, dim)


def remote(src, dst, send, recv, row, col):
    return pltpu.make_async_remote_copy(
        src_ref=src, dst_ref=dst, send_sem=send, recv_sem=recv,
        device_id={"row": row, "col": col}, device_id_type=MESH,
    )


def solve_kernel(
    n_row, n_col,
    nbr_ref, rhs_ref, anchor_ref, owner_ref, roff_ref, coff_ref, tiles_ref,
    sol_ref, arrived_ref,
    stage, thi, tlo, xbuf, sel, spread_sel, gath, terms, back, recv,
    ar_row, ar_col, own_hot, rank_sc, out_rows, mid_rows,
    tile_sem, fs, fr, bs, br, rs, rr, cs, cr, away1, got, away2, land, keep_sem,
):
    n_blk, fan, side, _ = thi.shape
    rows = 2 * n_blk
    q_own = n_blk * fan * 8
    q_all = q_own + n_blk * 8
    n_dev = n_row * n_col
    me_r = lax.axis_index("row")
    me_c = lax.axis_index("col")

    for b in range(n_blk):
        pltpu.make_async_copy(tiles_ref.at[b], stage.at[b], tile_sem.at[b]).start()

    barrier = pltpu.get_barrier_semaphore()
    peers = [(d, 0) for d in range(1, n_row)] + [(0, d) for d in range(1, n_col)]
    peers += [(dr, dc) for dr, dc in AROUND if dr and dc]
    for dr, dc in peers:
        pl.semaphore_signal(
            barrier, inc=1,
            device_id={"row": lax.rem(me_r + dr + n_row, n_row), "col": lax.rem(me_c + dc + n_col, n_col)},
            device_id_type=MESH,
        )

    own_lo = 4 * rows
    below = iota((side - 9 * rows, side), 0)
    for it in range(3):
        xbuf[it, 9 * rows:side, :] = jnp.where(below == 0, 1.0, 0.0)
    for b in range(n_blk):
        xbuf[0, own_lo + 2 * b:own_lo + 2 * b + 2, :] = rhs_ref[b]

    pl.semaphore_wait(barrier, len(peers))

    def x_rows(it, g):
        return xbuf.at[it, pl.ds(g * rows, rows)]

    pending = []

    def forward(it):
        for g, (dr, dc) in enumerate(AROUND):
            if g == 4:
                continue
            copy = remote(
                x_rows(it, 4), x_rows(it, 8 - g), fs.at[it, g], fr.at[it, 8 - g],
                lax.rem(me_r + dr + n_row, n_row), lax.rem(me_c + dc + n_col, n_col),
            )
            copy.start()
            pending.append(copy)

    def forward_wait(it):
        for g in range(9):
            if g != 4:
                remote(x_rows(it, 4), x_rows(it, g), fs.at[it, g], fr.at[it, g], me_r, me_c).wait_recv()

    def backward(it):
        for g, (dr, dc) in enumerate(AROUND):
            if g == 4:
                continue
            copy = remote(
                back.at[it, pl.ds(g * rows, rows)], recv.at[it, 8 - g], bs.at[it, g], br.at[it, 8 - g],
                lax.rem(me_r + dr + n_row, n_row), lax.rem(me_c + dc + n_col, n_col),
            )
            copy.start()
            pending.append(copy)

    def backward_wait(it):
        for g in range(9):
            if g != 4:
                remote(back.at[it, pl.ds(g * rows, rows)], recv.at[it, g], bs.at[it, g], br.at[it, g], me_r, me_c).wait_recv()

    forward(0)

    ones_row = 9 * rows
    lane3 = iota((8, 3 * side), 1)
    part_row = iota((8, 1), 0)
    base_col = jnp.where(
        part_row < 6, (part_row // 2) * side + lax.rem(part_row, 2), jnp.where(part_row == 6, ones_row, -1)
    )
    moves = (part_row < 6).astype(jnp.int32)

    def select_row(q, slot):
        sel[q:q + 8, :] = (lane3 == base_col + moves * (2 * slot)).astype(F32).astype(BF16)

    for b in range(n_blk):
        for k in range(fan):
            named = nbr_ref[b, k]
            dev = named // n_blk
            slot = ((dev // n_col - me_r + 1) * 3 + (lax.rem(dev, n_col) - me_c + 1)) * n_blk + lax.rem(named, n_blk)
            select_row((b * fan + k) * 8, slot)
        select_row(q_own + b * 8, 4 * n_blk + b)
    sel_t = sel[:, 0:side].astype(F32) + sel[:, side:2 * side].astype(F32) + sel[:, 2 * side:].astype(F32)
    spread_sel[...] = jnp.transpose(jnp.concatenate([sel_t, jnp.zeros((384 - q_all, side), F32)], axis=0)).astype(BF16)
    terms[...] = jnp.zeros_like(terms)

    upper = (iota((side, side), 0) < iota((side, side), 1)).astype(F32).astype(BF16)

    count = jnp.zeros((n_dev, 1), F32)
    for b in range(n_blk):
        hot = (owner_ref[b:b + 1, :] == iota((n_dev, side), 0)).astype(F32)
        own_hot[b] = hot.astype(BF16)
        before = nn_dot(hot.astype(BF16), upper) + count
        rank_sc[b:b + 1, :] = jnp.sum(hot * before, axis=0, keepdims=True)
        count = count + jnp.sum(hot, axis=1, keepdims=True)

    def split_block(b, carry):
        pltpu.make_async_copy(tiles_ref.at[b], stage.at[b], tile_sem.at[b]).wait()
        for k in range(fan):
            t = stage[b, k]
            hi = t.astype(BF16)
            thi[b, k] = hi
            tlo[b, k] = (t - hi.astype(F32)).astype(BF16)
        return carry

    lax.fori_loop(0, n_blk, split_block, 0)

    def apply(it, after_forward=None):
        forward_wait(it)
        if after_forward is not None:
            after_forward()
        parts = jnp.concatenate(split3(xbuf[it]), axis=0)
        gath[...] = nn_dot(sel[...], parts)

        def one_block(b, carry):
            own = gath[pl.ds(pl.multiple_of(q_own + b * 8, 8), 8), :]
            own_b = own.astype(BF16)
            total = jnp.zeros((8, side), F32)
            for k in range(fan):
                q = pl.multiple_of((b * fan + k) * 8, 8)
                far = gath[pl.ds(q, 8), :]
                far_b = far.astype(BF16)
                total = total + nt_dot(far_b, thi[b, k]) + nt_dot(far_b, tlo[b, k])
                down = nn_dot(own_b, thi[b, k]) + nn_dot(own_b, tlo[b, k])
                terms[pl.ds(q, 8), :] = down[6:7, :] * far - down
            weight = total[6:7, :] + anchor_ref[pl.ds(b, 1), :]
            terms[pl.ds(pl.multiple_of(q_own + b * 8, 8), 8), :] = weight * own - total
            return carry

        lax.fori_loop(0, n_blk, one_block, 0)
        hi, mid, low = split3(terms[...])
        where_to = spread_sel[0:9 * rows, :]
        back[it] = nn_dot(where_to, hi) + nn_dot(where_to, mid) + nn_dot(where_to, low)
        backward(it)

    def applied(it):
        backward_wait(it)
        image = back[it, own_lo:own_lo + rows, :]
        for g in range(9):
            if g != 4:
                image = image + recv[it, g]
        return image

    def dots_start(it, pairs):
        lane = iota((8, 128), 1)
        tile = jnp.zeros((8, 128), F32)
        for d, (a, b) in enumerate(pairs):
            e = a * b
            e = e[0:8] + e[8:16]
            tile = jnp.where(lane == d, jnp.sum(e, axis=1, keepdims=True), tile)
        ar_row[it, me_r] = tile
        for d in range(1, n_row):
            copy = remote(
                ar_row.at[it, me_r], ar_row.at[it, me_r], rs.at[it, d], rr.at[it, me_r],
                lax.rem(me_r + d, n_row), me_c,
            )
            copy.start()
            pending.append(copy)

    def dots_middle(it):
        for d in range(1, n_row):
            far = lax.rem(me_r + d, n_row)
            remote(ar_row.at[it, far], ar_row.at[it, far], rs.at[it, d], rr.at[it, far], me_r, me_c).wait_recv()
        ar_col[it, me_c] = jnp.sum(ar_row[it], axis=0)
        for d in range(1, n_col):
            copy = remote(
                ar_col.at[it, me_c], ar_col.at[it, me_c], cs.at[it, d], cr.at[it, me_c],
                me_r, lax.rem(me_c + d, n_col),
            )
            copy.start()
            pending.append(copy)

    def dots_end(it, n):
        for d in range(1, n_col):
            far = lax.rem(me_c + d, n_col)
            remote(ar_col.at[it, far], ar_col.at[it, far], cs.at[it, d], cr.at[it, far], me_r, me_c).wait_recv()
        t = jnp.sum(ar_col[it], axis=0)
        t = t + pltpu.roll(t, 4, 0)
        t = t + pltpu.roll(t, 2, 0)
        return [t[:, d:d + 1] for d in range(n)]

    def times(c, v):
        return jnp.concatenate([c] * (rows // 8), axis=0) * v

    r0 = xbuf[0, own_lo:own_lo + rows, :]
    apply(0)
    w0 = applied(0)
    xbuf[1, own_lo:own_lo + rows, :] = w0
    forward(1)
    dots_start(0, [(r0, r0), (r0, w0)])
    apply(1, lambda: dots_middle(0))
    gamma0, curve0 = dots_end(0, 2)
    alpha0 = gamma0 / curve0
    z0 = applied(1)
    w1 = w0 - times(alpha0, z0)
    xbuf[2, own_lo:own_lo + rows, :] = w1
    forward(2)
    r1 = r0 - times(alpha0, w0)
    dots_start(1, [(r1, r1), (r1, w1), (r1, w0)])
    apply(2, lambda: dots_middle(1))
    gamma1, r1w1, r1w0 = dots_end(1, 3)
    beta0 = gamma1 / gamma0
    curve1 = r1w1 + 2.0 * beta0 * r1w0 + beta0 * beta0 * curve0
    alpha1 = gamma1 / curve1
    p1 = r1 + times(beta0, r0)
    s1 = w1 + times(beta0, w0)
    z1 = applied(2)
    q1 = z1 + times(beta0, z0)
    r2 = r1 - times(alpha1, s1)
    w2 = w1 - times(alpha1, q1)
    dots_start(2, [(r2, r2), (r2, w2), (r2, s1)])
    dots_middle(2)
    gamma2, r2w2, r2s1 = dots_end(2, 3)
    beta1 = gamma2 / gamma1
    curve2 = r2w2 + 2.0 * beta1 * r2s1 + beta1 * beta1 * curve1
    alpha2 = gamma2 / curve2
    x = times(alpha0, r0) + times(alpha1, p1) + times(alpha2, r2 + times(beta1, p1))
    for b in range(n_blk):
        sol_ref[b] = x[2 * b:2 * b + 2, :]

    moved = 3.0 * jnp.tanh(x)
    table = jnp.zeros((n_dev, 128), F32)
    lane_rank = iota((2 * CAP, side), 0)
    for b in range(n_blk):
        pos_row = roff_ref[b:b + 1, :].astype(F32) + moved[2 * b:2 * b + 1, :]
        pos_col = coff_ref[b:b + 1, :].astype(F32) + moved[2 * b + 1:2 * b + 2, :]
        rank = rank_sc[b:b + 1, :].astype(jnp.int32)
        placed = jnp.where(lane_rank == rank, pos_row, jnp.where(lane_rank == rank + CAP, pos_col, 0.0))
        placed = jnp.concatenate([placed, jnp.zeros((128 - 2 * CAP, side), F32)], axis=0)
        for part in split3(placed):
            table = table + nt_dot(own_hot[b], part)
    lane_of = lax.rem(iota((n_dev, 128), 1), CAP).astype(F32)
    table = jnp.where(lane_of < count, table, NONE)
    for o in range(n_dev):
        out_rows[o // n_col, o % n_col] = table[o:o + 1, :]

    keep = pltpu.make_async_copy(out_rows.at[me_r], mid_rows.at[:, me_r], keep_sem.at[0])
    keep.start()
    for d in range(1, n_row):
        far = lax.rem(me_r + d, n_row)
        copy = remote(out_rows.at[far], mid_rows.at[:, me_r], away1.at[d], got.at[me_r], far, me_c)
        copy.start()
        pending.append(copy)
    keep.wait()
    for d in range(1, n_row):
        far = lax.rem(me_r + d, n_row)
        remote(out_rows.at[far], mid_rows.at[:, far], away1.at[d], got.at[far], me_r, me_c).wait_recv()
    keep2 = pltpu.make_async_copy(mid_rows.at[me_c], arrived_ref.at[me_c], keep_sem.at[1])
    keep2.start()
    for d in range(1, n_col):
        far = lax.rem(me_c + d, n_col)
        copy = remote(mid_rows.at[far], arrived_ref.at[me_c], away2.at[d], land.at[me_c], me_r, far)
        copy.start()
        pending.append(copy)
    keep2.wait()
    for d in range(1, n_col):
        far = lax.rem(me_c + d, n_col)
        remote(mid_rows.at[far], arrived_ref.at[far], away2.at[d], land.at[far], me_r, me_c).wait_recv()
    for copy in pending:
        copy.wait_send()


def solve(n_row, n_col, neighbours, right_side, anchor, owners, row_offset, col_offset, tiles):
    n_blk, fan, side, _ = tiles.shape
    rows = 2 * n_blk
    q_all = n_blk * fan * 8 + n_blk * 8
    vmem = pl.BlockSpec(memory_space=pltpu.VMEM)
    dma = pltpu.SemaphoreType.DMA
    return pl.pallas_call(
        functools.partial(solve_kernel, n_row, n_col),
        name="solve_and_route",
        out_shape=(
            jax.ShapeDtypeStruct(right_side.shape, F32),
            jax.ShapeDtypeStruct((n_col, n_row, 1, 128), F32),
        ),
        in_specs=[pl.BlockSpec(memory_space=pltpu.SMEM)] + [vmem] * 5 + [pl.BlockSpec(memory_space=pl.ANY)],
        out_specs=(vmem, vmem),
        scratch_shapes=[
            pltpu.VMEM(tiles.shape, F32),
            pltpu.VMEM(tiles.shape, BF16),
            pltpu.VMEM(tiles.shape, BF16),
            pltpu.VMEM((3, side, side), F32),
            pltpu.VMEM((q_all, 3 * side), BF16),
            pltpu.VMEM((side, 384), BF16),
            pltpu.VMEM((q_all, side), F32),
            pltpu.VMEM((384, side), F32),
            pltpu.VMEM((3, 9 * rows, side), F32),
            pltpu.VMEM((3, 9, rows, side), F32),
            pltpu.VMEM((3, n_row, 8, 128), F32),
            pltpu.VMEM((3, n_col, 8, 128), F32),
            pltpu.VMEM((n_blk, n_row * n_col, side), BF16),
            pltpu.VMEM((n_blk, side), F32),
            pltpu.VMEM((n_row, n_col, 1, 128), F32),
            pltpu.VMEM((n_col, n_row, 1, 128), F32),
            dma((n_blk,)),
            dma((3, 9)), dma((3, 9)), dma((3, 9)), dma((3, 9)),
            dma((3, n_row)), dma((3, n_row)), dma((3, n_col)), dma((3, n_col)),
            dma((n_row,)), dma((n_row,)), dma((n_col,)), dma((n_col,)), dma((2,)),
        ],
        compiler_params=pltpu.CompilerParams(
            collective_id=0, has_side_effects=True, vmem_limit_bytes=48 * 2**20
        ),
        cost_estimate=pl.CostEstimate(flops=10**9, bytes_accessed=2**23, transcendentals=0),
    )(neighbours, right_side, anchor, owners, row_offset, col_offset, tiles)


def edge_kernel(n_row, n_col, top_ref, bottom_ref, left_ref, right_ref, up_ref, down_ref, west_ref, east_ref, ss, rs):
    me_r = lax.axis_index("row")
    me_c = lax.axis_index("col")
    barrier = pltpu.get_barrier_semaphore()

    def at(dr, dc):
        return lax.rem(me_r + dr + n_row, n_row), lax.rem(me_c + dc + n_col, n_col)

    for g, (dr, dc) in enumerate(AROUND):
        if g != 4:
            row, col = at(dr, dc)
            pl.semaphore_signal(barrier, inc=1, device_id={"row": row, "col": col}, device_id_type=MESH)
    pl.semaphore_wait(barrier, 8)
    length = left_ref.shape[1]
    first = (slice(None), pl.ds(0, 128))
    last = (slice(None), pl.ds(length - 128, 128))
    inner = (slice(None), pl.ds(128, length))
    above = (slice(None), pl.ds(0, 128))
    below = (slice(None), pl.ds(length + 128, 128))
    plan = {
        (-1, 0): (top_ref, down_ref),
        (1, 0): (bottom_ref, up_ref),
        (0, -1): (left_ref, east_ref.at[inner]),
        (0, 1): (right_ref, west_ref.at[inner]),
        (-1, -1): (left_ref.at[first], east_ref.at[below]),
        (-1, 1): (right_ref.at[first], west_ref.at[below]),
        (1, -1): (left_ref.at[last], east_ref.at[above]),
        (1, 1): (right_ref.at[last], west_ref.at[above]),
    }
    copies = []
    for g, side in enumerate(AROUND):
        if g != 4:
            src, dst = plan[side]
            row, col = at(*side)
            copy = remote(src, dst, ss.at[g], rs.at[g], row, col)
            copy.start()
            copies.append(copy)
    for copy in copies:
        copy.wait_recv()
    for copy in copies:
        copy.wait_send()


def exchange_edges(n_row, n_col, top, bottom, left, right):
    vmem = pl.BlockSpec(memory_space=pltpu.VMEM)
    length, width = left.shape[1], top.shape[1]
    return pl.pallas_call(
        functools.partial(edge_kernel, n_row, n_col),
        name="grid_edges",
        out_shape=(
            jax.ShapeDtypeStruct((8, width), F32),
            jax.ShapeDtypeStruct((8, width), F32),
            jax.ShapeDtypeStruct((8, length + 256), F32),
            jax.ShapeDtypeStruct((8, length + 256), F32),
        ),
        in_specs=[vmem] * 4,
        out_specs=(vmem,) * 4,
        scratch_shapes=[pltpu.SemaphoreType.DMA((9,)), pltpu.SemaphoreType.DMA((9,))],
        compiler_params=pltpu.CompilerParams(collective_id=1, has_side_effects=True),
    )(top, bottom, left, right)


CHUNK = 128
STRIP = 64


def diffuse_kernel(n_row, n_col, field_ref, up_ref, down_ref, west_ref, east_ref, out_ref, one, two, in_sem, out_sem):
    length, width = field_ref.shape
    wide = width + 128
    n_chunk = length // CHUNK
    me_r = lax.axis_index("row")
    me_c = lax.axis_index("col")

    def load(i):
        return pltpu.make_async_copy(
            field_ref.at[pl.ds(i * CHUNK, CHUNK)], one.at[pl.ds(8 + i * CHUNK, CHUNK), pl.ds(0, width)], in_sem.at[i]
        )

    for i in range(n_chunk):
        load(i).start()
    not_first_row = (me_r > 0).astype(F32)
    not_last_row = (me_r < n_row - 1).astype(F32)
    not_first_col = (me_c > 0).astype(F32)
    not_last_col = (me_c < n_col - 1).astype(F32)
    lane = iota((1, 128), 1)
    keep_lane = jnp.where(lane < 8, not_last_col, jnp.where(lane >= 120, not_first_col, 0.0))
    one[0:8, 0:width] = up_ref[...] * not_first_row
    one[length + 8:length + 16, 0:width] = down_ref[...] * not_last_row
    gap = jnp.zeros((112, 128), F32)
    for i in range(length // 128 + 2):
        here = pl.ds(i * 128, 128)
        tile = jnp.transpose(jnp.concatenate([east_ref[:, here], gap, west_ref[:, here]], axis=0)) * keep_lane
        if i == 0:
            one[0:8, width:wide] = tile[120:128] * not_first_row
        elif i == length // 128 + 1:
            one[length + 8:length + 16, width:wide] = tile[0:8] * not_last_row
        else:
            one[8 + (i - 1) * 128:8 + i * 128, width:wide] = tile
    for i in range(n_chunk):
        load(i).wait()

    keep_cols = jnp.concatenate([jnp.ones((1, width), F32), keep_lane], axis=1)

    def summed(src, start, n):
        window = src[pl.ds(pl.multiple_of(start - 8, 8), n + 16), :]
        centre = window[8:8 + n]
        above = window[7:7 + n]
        below = window[9:9 + n]
        return (centre + above) + (below + pltpu.roll(centre, 1, 1)) + pltpu.roll(centre, wide - 1, 1)

    def edge(src, dst):
        for start, keep in ((0, not_first_row), (length + 8, not_last_row)):
            c = src[start:start + 8, :]
            if start == 0:
                above = pltpu.roll(c, 1, 0)
                below = src[1:9, :]
            else:
                above = src[start - 1:start + 7, :]
                below = pltpu.roll(c, 7, 0)
            total = c + above + below + pltpu.roll(c, 1, 1) + pltpu.roll(c, wide - 1, 1)
            dst[start:start + 8, :] = total * keep_cols * keep

    src, dst = one, two
    for step in range(STEPS):
        if step < STEPS - 1:
            edge(src, dst)

            def strip(i, carry, src=src, dst=dst):
                start = pl.multiple_of(8 + i * STRIP, 8)
                total = summed(src, start, STRIP)
                dst[pl.ds(start, STRIP), 0:width] = total[:, 0:width]
                dst[pl.ds(start, STRIP), width:wide] = total[:, width:wide] * keep_lane
                return carry

            lax.fori_loop(0, length // STRIP, strip, 0)
        else:

            def strip(i, carry, src=src, dst=dst):
                start = pl.multiple_of(8 + i * STRIP, 8)
                total = summed(src, start, STRIP)
                dst[pl.ds(start, STRIP), 0:width] = total[:, 0:width] * (0.2 ** STEPS)
                return carry

            for i in range(n_chunk):
                lax.fori_loop(i * (CHUNK // STRIP), (i + 1) * (CHUNK // STRIP), strip, 0)
                store_chunk(dst, out_ref, out_sem, i, width).start()
        src, dst = dst, src
    for i in range(n_chunk):
        store_chunk(src, out_ref, out_sem, i, width).wait()


def store_chunk(buf, out_ref, out_sem, i, width):
    return pltpu.make_async_copy(
        buf.at[pl.ds(8 + i * CHUNK, CHUNK), pl.ds(0, width)], out_ref.at[pl.ds(i * CHUNK, CHUNK)], out_sem.at[i]
    )


def diffuse(n_row, n_col, field, up, down, west, east):
    length, width = field.shape
    vmem = pl.BlockSpec(memory_space=pltpu.VMEM)
    hbm = pl.BlockSpec(memory_space=pl.ANY)
    n_chunk = length // CHUNK
    return pl.pallas_call(
        functools.partial(diffuse_kernel, n_row, n_col),
        name="diffuse",
        out_shape=jax.ShapeDtypeStruct(field.shape, F32),
        in_specs=[hbm] + [vmem] * 4,
        out_specs=hbm,
        scratch_shapes=[
            pltpu.VMEM((length + 16, width + 128), F32),
            pltpu.VMEM((length + 16, width + 128), F32),
            pltpu.SemaphoreType.DMA((n_chunk,)),
            pltpu.SemaphoreType.DMA((n_chunk,)),
        ],
        compiler_params=pltpu.CompilerParams(vmem_limit_bytes=32 * 2**20),
        cost_estimate=pl.CostEstimate(flops=4 * 5 * length * width, bytes_accessed=8 * length * width, transcendentals=0),
    )(field, up, down, west, east)


def per_device(right_side, anchor, tiles, neighbours, owners, row_offset, col_offset, macro_density):
    n_blk, _, side, _ = tiles.shape[0], tiles.shape[1], tiles.shape[2], tiles.shape[3]
    n_row, n_col = lax.axis_size("row"), lax.axis_size("col")
    solution, arrived = solve(
        n_row, n_col, neighbours, right_side, anchor, owners.reshape(n_blk, side),
        row_offset.reshape(n_blk, side), col_offset.reshape(n_blk, side), tiles,
    )
    arrived = arrived.reshape(n_row * n_col, 128)
    at_row = arrived[:, :CAP].reshape(-1)
    at_col = arrived[:, CAP:2 * CAP].reshape(-1)
    grid_rows, grid_cols = macro_density.shape

    def window_of(position, limit):
        start_cell = jnp.clip(jnp.floor(position).astype(jnp.int32) - 7, 0, limit - 16)
        cells = lax.iota(jnp.int32, limit)[None, :]
        inside = ((cells >= start_cell[:, None]) & (cells < start_cell[:, None] + 16)).astype(F32)
        offset = cells.astype(F32) - position[:, None]
        return (jnp.exp(-0.5 * offset * offset) * inside).astype(BF16)

    spread = lax.dot_general(
        window_of(at_row, grid_rows), window_of(at_col, grid_cols), (((0,), (0,)), ((), ())), preferred_element_type=F32
    )
    field = macro_density + spread
    edges = exchange_edges(
        n_row, n_col, field[:8], field[-8:], field[:, :8].T, field[:, -8:].T
    )
    return solution, diffuse(n_row, n_col, field, *edges)


def solution(mesh):
    blocks = P(("row", "col"))
    return jax.shard_map(
        per_device,
        mesh=mesh,
        in_specs=(
            P(("row", "col"), None, None),
            P(("row", "col"), None),
            P(("row", "col"), None, None, None),
            P(("row", "col"), None),
            P(("row", "col"), None),
            blocks,
            blocks,
            P("row", "col"),
        ),
        out_specs=(P(("row", "col"), None, None), P("row", "col")),
        check_vma=False,
    )
```

```python
import functools

import jax
import jax.numpy as jnp
from jax import lax
from jax.experimental import pallas as pl
from jax.experimental.pallas import tpu as pltpu
from jax.sharding import PartitionSpec as P

MESH = pl.DeviceIdType.MESH
F32 = jnp.float32
BF16 = jnp.bfloat16
STEPS = 4
CAP = 32
NONE = -1000.0
AROUND = [(dr, dc) for dr in (-1, 0, 1) for dc in (-1, 0, 1)]


def nt_dot(a, b):
    return lax.dot_general(a, b, (((1,), (1,)), ((), ())), preferred_element_type=F32)


def nn_dot(a, b):
    return jnp.dot(a, b, preferred_element_type=F32)


def split3(x):
    hi = x.astype(BF16)
    rest = x - hi.astype(F32)
    mid = rest.astype(BF16)
    low = (rest - mid.astype(F32)).astype(BF16)
    return hi, mid, low


def iota(shape, dim):
    return lax.broadcasted_iota(jnp.int32, shape, dim)


def remote(src, dst, send, recv, row, col):
    return pltpu.make_async_remote_copy(
        src_ref=src, dst_ref=dst, send_sem=send, recv_sem=recv,
        device_id={"row": row, "col": col}, device_id_type=MESH,
    )


def solve_kernel(
    n_row, n_col,
    nbr_ref, rhs_ref, anchor_ref, owner_ref, roff_ref, coff_ref, tiles_ref,
    sol_ref, pos_ref,
    stage, thi, tlo, xbuf, sel, spread_sel, gath, terms, back, recv,
    ar_row, ar_col, own_hot, rank_sc, weight_sc, out_rows, mid_rows, end_rows, table_sc,
    tile_sem, fs, fr, bs, br, rs, rr, cs, cr, away1, got, away2, land, keep_sem,
):
    n_blk, fan, side, _ = thi.shape
    rows = 2 * n_blk
    q_own = n_blk * fan * 8
    q_all = q_own + n_blk * 8
    n_dev = n_row * n_col
    me_r = lax.axis_index("row")
    me_c = lax.axis_index("col")
    row_order = sorted(range(1, n_row), key=lambda d: -min(d, n_row - d))
    col_order = sorted(range(1, n_col), key=lambda d: -(min(d // 4, 4 - d // 4) + min(d % 4, 4 - d % 4)))
    around = sorted((g for g in range(9) if g != 4), key=lambda g: -abs(AROUND[g][0]) - 2 * abs(AROUND[g][1]))

    for b in range(n_blk):
        pltpu.make_async_copy(tiles_ref.at[b], stage.at[b], tile_sem.at[b]).start()

    barrier = pltpu.get_barrier_semaphore()
    peers = [AROUND[g] for g in around if AROUND[g][0] and AROUND[g][1]]
    peers += [(0, d) for d in col_order] + [(d, 0) for d in row_order]
    for dr, dc in peers:
        pl.semaphore_signal(
            barrier, inc=1,
            device_id={"row": lax.rem(me_r + dr + n_row, n_row), "col": lax.rem(me_c + dc + n_col, n_col)},
            device_id_type=MESH,
        )

    own_lo = 4 * rows
    below = iota((side - 9 * rows, side), 0)
    for it in range(3):
        xbuf[it, 9 * rows:side, :] = jnp.where(below == 0, 1.0, 0.0)
    for b in range(n_blk):
        xbuf[0, own_lo + 2 * b:own_lo + 2 * b + 2, :] = rhs_ref[b]

    upper = (iota((side, side), 0) < iota((side, side), 1)).astype(F32).astype(BF16)
    count = jnp.zeros((n_dev, 1), F32)
    held = jnp.zeros((1, n_dev), F32)
    for b in range(n_blk):
        hot = (owner_ref[b:b + 1, :] == iota((n_dev, side), 0)).astype(F32)
        before = nn_dot(hot.astype(BF16), upper) + count
        rank_sc[b:b + 1, :] = jnp.sum(hot * before, axis=0, keepdims=True)
        count = count + jnp.sum(hot, axis=1, keepdims=True)
        turned = jnp.transpose(hot)
        own_hot[b] = turned.astype(BF16)
        held = held + jnp.sum(turned, axis=0, keepdims=True)

    pl.semaphore_wait(barrier, len(peers))

    def x_rows(it, g):
        return xbuf.at[it, pl.ds(g * rows, rows)]

    pending = []

    def forward(it):
        for g in around:
            dr, dc = AROUND[g]
            copy = remote(
                x_rows(it, 4), x_rows(it, 8 - g), fs.at[it, g], fr.at[it, 8 - g],
                lax.rem(me_r + dr + n_row, n_row), lax.rem(me_c + dc + n_col, n_col),
            )
            copy.start()
            pending.append(copy)

    def forward_wait(it):
        for g in around:
            remote(x_rows(it, 4), x_rows(it, g), fs.at[it, g], fr.at[it, g], me_r, me_c).wait_recv()

    def backward(it):
        for g in around:
            dr, dc = AROUND[g]
            copy = remote(
                back.at[it, pl.ds(g * rows, rows)], recv.at[it, 8 - g], bs.at[it, g], br.at[it, 8 - g],
                lax.rem(me_r + dr + n_row, n_row), lax.rem(me_c + dc + n_col, n_col),
            )
            copy.start()
            pending.append(copy)

    def backward_wait(it):
        for g in around:
            remote(back.at[it, pl.ds(g * rows, rows)], recv.at[it, g], bs.at[it, g], br.at[it, g], me_r, me_c).wait_recv()

    forward(0)

    ones_row = 9 * rows
    lane3 = iota((8, 3 * side), 1)
    part_row = iota((8, 1), 0)
    base_col = jnp.where(
        part_row < 6, (part_row // 2) * side + lax.rem(part_row, 2), jnp.where(part_row == 6, ones_row, -1)
    )
    moves = (part_row < 6).astype(jnp.int32)

    def select_row(q, slot):
        sel[q:q + 8, :] = (lane3 == base_col + moves * (2 * slot)).astype(F32).astype(BF16)

    for b in range(n_blk):
        for k in range(fan):
            named = nbr_ref[b, k]
            dev = named // n_blk
            slot = ((dev // n_col - me_r + 1) * 3 + (lax.rem(dev, n_col) - me_c + 1)) * n_blk + lax.rem(named, n_blk)
            select_row((b * fan + k) * 8, slot)
        select_row(q_own + b * 8, 4 * n_blk + b)
    sel_t = sel[:, 0:side].astype(F32) + sel[:, side:2 * side].astype(F32) + sel[:, 2 * side:].astype(F32)
    spread_sel[...] = jnp.transpose(jnp.concatenate([sel_t, jnp.zeros((384 - q_all, side), F32)], axis=0)).astype(BF16)
    terms[...] = jnp.zeros_like(terms)

    def split_block(b, carry):
        pltpu.make_async_copy(tiles_ref.at[b], stage.at[b], tile_sem.at[b]).wait()
        for k in range(fan):
            t = stage[b, k]
            hi = t.astype(BF16)
            thi[b, k] = hi
            tlo[b, k] = (t - hi.astype(F32)).astype(BF16)
        return carry

    lax.fori_loop(0, n_blk, split_block, 0)

    def apply(it, after_forward=None):
        forward_wait(it)
        if after_forward is not None:
            after_forward()
        parts = jnp.concatenate(split3(xbuf[it]), axis=0)
        gath[...] = nn_dot(sel[...], parts)

        def one_block(b, carry):
            own = gath[pl.ds(pl.multiple_of(q_own + b * 8, 8), 8), :]
            own_b = own.astype(BF16)
            total = jnp.zeros((8, side), F32)
            for k in range(fan):
                q = pl.multiple_of((b * fan + k) * 8, 8)
                far = gath[pl.ds(q, 8), :]
                far_b = far.astype(BF16)
                total = total + nt_dot(far_b, thi[b, k]) + nt_dot(far_b, tlo[b, k])
                down = nn_dot(own_b, thi[b, k]) + nn_dot(own_b, tlo[b, k])
                terms[pl.ds(q, 8), :] = down[6:7, :] * far - down
            weight = total[6:7, :] + anchor_ref[pl.ds(b, 1), :]
            if it == 0:
                weight_sc[pl.ds(b, 1), :] = weight
            terms[pl.ds(pl.multiple_of(q_own + b * 8, 8), 8), :] = weight * own - total
            return carry

        lax.fori_loop(0, n_blk, one_block, 0)
        hi, mid, low = split3(terms[...])
        where_to = spread_sel[0:9 * rows, :]
        back[it] = nn_dot(where_to, hi) + nn_dot(where_to, mid) + nn_dot(where_to, low)
        backward(it)

    def applied(it):
        backward_wait(it)
        image = back[it, own_lo:own_lo + rows, :]
        for g in range(9):
            if g != 4:
                image = image + recv[it, g]
        return image

    def dots_start(it, pairs, more=None):
        lane = iota((8, 128), 1)
        tile = jnp.zeros((8, 128), F32)
        for d, (a, b) in enumerate(pairs):
            e = a * b
            e = e[0:8] + e[8:16]
            if d == 0 and more is not None:
                e = e + more
            tile = jnp.where(lane == d, jnp.sum(e, axis=1, keepdims=True), tile)
        ar_row[it, me_r] = tile
        for d in row_order:
            copy = remote(
                ar_row.at[it, me_r], ar_row.at[it, me_r], rs.at[it, d], rr.at[it, me_r],
                lax.rem(me_r + d, n_row), me_c,
            )
            copy.start()
            pending.append(copy)

    def dots_middle(it):
        for d in row_order:
            far = lax.rem(me_r + d, n_row)
            remote(ar_row.at[it, far], ar_row.at[it, far], rs.at[it, d], rr.at[it, far], me_r, me_c).wait_recv()
        ar_col[it, me_c] = jnp.sum(ar_row[it], axis=0)
        for d in col_order:
            copy = remote(
                ar_col.at[it, me_c], ar_col.at[it, me_c], cs.at[it, d], cr.at[it, me_c],
                me_r, lax.rem(me_c + d, n_col),
            )
            copy.start()
            pending.append(copy)

    def dots_end(it, n):
        for d in col_order:
            far = lax.rem(me_c + d, n_col)
            remote(ar_col.at[it, far], ar_col.at[it, far], cs.at[it, d], cr.at[it, far], me_r, me_c).wait_recv()
        t = jnp.sum(ar_col[it], axis=0)
        t = t + pltpu.roll(t, 4, 0)
        t = t + pltpu.roll(t, 2, 0)
        return [t[:, d:d + 1] for d in range(n)]

    def times(c, v):
        return jnp.concatenate([c] * (v.shape[0] // 8), axis=0) * v

    r0 = xbuf[0, own_lo:own_lo + rows, :]
    apply(0)
    w0 = applied(0)
    xbuf[1, own_lo:own_lo + rows, :] = w0
    forward(1)
    dots_start(0, [(r0, r0), (r0, w0)])
    apply(1, lambda: dots_middle(0))
    gamma0, curve0 = dots_end(0, 2)
    alpha0 = gamma0 / curve0
    z0 = applied(1)
    w1 = w0 - times(alpha0, z0)
    xbuf[2, own_lo:own_lo + rows, :] = w1
    forward(2)
    r1 = r0 - times(alpha0, w0)
    dots_start(1, [(r1, r1), (r1, w1), (r1, w0)])

    rank_of = iota((CAP, side), 0)
    table = jnp.zeros((8 * CAP, n_dev), F32)
    for b in range(n_blk):
        mine = rank_of == rank_sc[b:b + 1, :].astype(jnp.int32)
        values = [v[2 * b + c:2 * b + c + 1, :] for v in (r0, w0, w1) for c in (0, 1)]
        values += [roff_ref[b:b + 1, :].astype(F32), coff_ref[b:b + 1, :].astype(F32)]
        placed = jnp.concatenate([jnp.where(mine, v, 0.0) for v in values], axis=0)
        for part in split3(placed):
            table = table + nn_dot(part, own_hot[b])
    empty = iota((CAP, n_dev), 0).astype(F32) >= held
    table = jnp.concatenate(
        [table[0:6 * CAP], jnp.where(empty, NONE, table[6 * CAP:7 * CAP]), table[7 * CAP:]], axis=0
    )
    table = jnp.transpose(table)
    for o in range(n_dev):
        out_rows[o // n_col, o % n_col] = table[o:o + 1, :]
    keep = pltpu.make_async_copy(out_rows.at[me_r], mid_rows.at[:, me_r], keep_sem.at[0])
    keep.start()
    for d in row_order:
        far = lax.rem(me_r + d, n_row)
        copy = remote(out_rows.at[far], mid_rows.at[:, me_r], away1.at[d], got.at[me_r], far, me_c)
        copy.start()
        pending.append(copy)

    dots_middle(1)

    keep.wait()
    for d in row_order:
        far = lax.rem(me_r + d, n_row)
        remote(out_rows.at[far], mid_rows.at[:, far], away1.at[d], got.at[far], me_r, me_c).wait_recv()
    keep2 = pltpu.make_async_copy(mid_rows.at[me_c], end_rows.at[me_c], keep_sem.at[1])
    keep2.start()
    for d in col_order:
        far = lax.rem(me_c + d, n_col)
        copy = remote(mid_rows.at[far], end_rows.at[me_c], away2.at[d], land.at[me_c], me_r, far)
        copy.start()
        pending.append(copy)

    forward_wait(2)
    gamma1, r1w1, r1w0 = dots_end(1, 3)
    beta0 = gamma1 / gamma0
    curve1 = r1w1 + 2.0 * beta0 * r1w0 + beta0 * beta0 * curve0
    alpha1 = gamma1 / curve1
    p1 = r1 + times(beta0, r0)
    s1 = w1 + times(beta0, w0)
    r2 = r1 - times(alpha1, s1)

    near_w0 = xbuf[1, 0:9 * rows, :]
    near_r1 = xbuf[0, 0:9 * rows, :] - times(alpha0, near_w0)
    near_r2 = near_r1 - times(alpha1, xbuf[2, 0:9 * rows, :] + times(beta0, near_w0))
    near_r2 = jnp.concatenate([near_r2, jnp.where(below == 0, 1.0, 0.0)], axis=0)
    gath[...] = nn_dot(sel[...], jnp.concatenate(split3(near_r2), axis=0))

    def energy_block(b, carry):
        own_b = gath[pl.ds(pl.multiple_of(q_own + b * 8, 8), 8), :].astype(BF16)
        for k in range(fan):
            q = pl.multiple_of((b * fan + k) * 8, 8)
            down = nn_dot(own_b, thi[b, k]) + nn_dot(own_b, tlo[b, k])
            terms[pl.ds(q, 8), :] = down[6:7, :] * gath[pl.ds(q, 8), :] - 2.0 * down
        return carry

    lax.fori_loop(0, n_blk, energy_block, 0)

    def over_parts(v):
        return v + pltpu.roll(v, q_own - 2, 0) + pltpu.roll(v, q_own - 4, 0)

    cross = over_parts(terms[0:q_own, :]) * over_parts(gath[0:q_own, :])
    cross = jnp.sum(cross.reshape(q_own // 8, 8, side), axis=0)
    cross = jnp.where(iota((8, side), 0) < 2, cross, 0.0)
    weights = weight_sc[...]
    weights = jnp.concatenate([weights[b:b + 1] for b in range(n_blk) for _ in (0, 1)], axis=0)
    dots_start(2, [(r2, weights * r2), (r2, r2), (r2, s1)], more=cross)

    keep2.wait()
    for d in col_order:
        far = lax.rem(me_c + d, n_col)
        remote(mid_rows.at[far], end_rows.at[far], away2.at[d], land.at[far], me_r, me_c).wait_recv()
    dots_middle(2)
    for o in range(n_dev):
        table_sc[o:o + 1, :] = end_rows[o // n_row, o % n_row]
    curve_r2, gamma2, r2s1 = dots_end(2, 3)
    beta1 = gamma2 / gamma1
    curve2 = curve_r2 + 2.0 * beta1 * r2s1 + beta1 * beta1 * curve1
    alpha2 = gamma2 / curve2

    of_b = alpha0 + alpha1 * (1.0 + beta0) + alpha2 * (1.0 + beta1 * (1.0 + beta0))
    of_w0 = -alpha1 * alpha0 - alpha2 * (alpha0 + alpha1 * beta0 + beta1 * alpha0)
    of_w1 = -alpha2 * alpha1
    lane = iota((1, 128), 1)

    def by_lane(first, second):
        return jnp.where(
            lane < CAP, first[0:1], jnp.where(lane < 2 * CAP, first[1:2], jnp.where(lane < 3 * CAP, second[0:1], second[1:2]))
        )

    near = table_sc[:, 0:128] * by_lane(of_b, of_w0)
    far = table_sc[:, 128:256]
    moved = near + pltpu.roll(near, 64, 1) + far * by_lane(of_w1, of_w1)
    pos_ref[...] = pltpu.roll(far, 64, 1) + 3.0 * jnp.tanh(moved)

    x = times(alpha0, r0) + times(alpha1, p1) + times(alpha2, r2 + times(beta1, p1))
    for b in range(n_blk):
        sol_ref[b] = x[2 * b:2 * b + 2, :]
    for copy in pending:
        copy.wait_send()


def solve(n_row, n_col, neighbours, right_side, anchor, owners, row_offset, col_offset, tiles):
    n_blk, fan, side, _ = tiles.shape
    rows = 2 * n_blk
    n_dev = n_row * n_col
    q_all = n_blk * fan * 8 + n_blk * 8
    vmem = pl.BlockSpec(memory_space=pltpu.VMEM)
    dma = pltpu.SemaphoreType.DMA
    return pl.pallas_call(
        functools.partial(solve_kernel, n_row, n_col),
        name="solve_and_route",
        out_shape=(
            jax.ShapeDtypeStruct(right_side.shape, F32),
            jax.ShapeDtypeStruct((n_dev, 128), F32),
        ),
        in_specs=[pl.BlockSpec(memory_space=pltpu.SMEM)] + [vmem] * 5 + [pl.BlockSpec(memory_space=pl.ANY)],
        out_specs=(vmem, vmem),
        scratch_shapes=[
            pltpu.VMEM(tiles.shape, F32),
            pltpu.VMEM(tiles.shape, BF16),
            pltpu.VMEM(tiles.shape, BF16),
            pltpu.VMEM((3, side, side), F32),
            pltpu.VMEM((q_all, 3 * side), BF16),
            pltpu.VMEM((side, 384), BF16),
            pltpu.VMEM((q_all, side), F32),
            pltpu.VMEM((384, side), F32),
            pltpu.VMEM((2, 9 * rows, side), F32),
            pltpu.VMEM((2, 9, rows, side), F32),
            pltpu.VMEM((3, n_row, 8, 128), F32),
            pltpu.VMEM((3, n_col, 8, 128), F32),
            pltpu.VMEM((n_blk, side, n_dev), BF16),
            pltpu.VMEM((n_blk, side), F32),
            pltpu.VMEM((n_blk, side), F32),
            pltpu.VMEM((n_row, n_col, 1, 8 * CAP), F32),
            pltpu.VMEM((n_col, n_row, 1, 8 * CAP), F32),
            pltpu.VMEM((n_col, n_row, 1, 8 * CAP), F32),
            pltpu.VMEM((n_dev, 8 * CAP), F32),
            dma((n_blk,)),
            dma((3, 9)), dma((3, 9)), dma((3, 9)), dma((3, 9)),
            dma((3, n_row)), dma((3, n_row)), dma((3, n_col)), dma((3, n_col)),
            dma((n_row,)), dma((n_row,)), dma((n_col,)), dma((n_col,)), dma((2,)),
        ],
        compiler_params=pltpu.CompilerParams(
            collective_id=0, has_side_effects=True, vmem_limit_bytes=48 * 2**20
        ),
        cost_estimate=pl.CostEstimate(flops=10**9, bytes_accessed=2**23, transcendentals=0),
    )(neighbours, right_side, anchor, owners, row_offset, col_offset, tiles)


def edge_kernel(n_row, n_col, top_ref, bottom_ref, left_ref, right_ref, up_ref, down_ref, west_ref, east_ref, ss, rs):
    me_r = lax.axis_index("row")
    me_c = lax.axis_index("col")
    barrier = pltpu.get_barrier_semaphore()

    def at(dr, dc):
        return lax.rem(me_r + dr + n_row, n_row), lax.rem(me_c + dc + n_col, n_col)

    for g, (dr, dc) in enumerate(AROUND):
        if g != 4:
            row, col = at(dr, dc)
            pl.semaphore_signal(barrier, inc=1, device_id={"row": row, "col": col}, device_id_type=MESH)
    pl.semaphore_wait(barrier, 8)
    length = left_ref.shape[1]
    first = (slice(None), pl.ds(0, 128))
    last = (slice(None), pl.ds(length - 128, 128))
    inner = (slice(None), pl.ds(128, length))
    above = (slice(None), pl.ds(0, 128))
    below = (slice(None), pl.ds(length + 128, 128))
    plan = {
        (-1, 0): (top_ref, down_ref),
        (1, 0): (bottom_ref, up_ref),
        (0, -1): (left_ref, east_ref.at[inner]),
        (0, 1): (right_ref, west_ref.at[inner]),
        (-1, -1): (left_ref.at[first], east_ref.at[below]),
        (-1, 1): (right_ref.at[first], west_ref.at[below]),
        (1, -1): (left_ref.at[last], east_ref.at[above]),
        (1, 1): (right_ref.at[last], west_ref.at[above]),
    }
    copies = []
    for g, side in enumerate(AROUND):
        if g != 4:
            src, dst = plan[side]
            row, col = at(*side)
            copy = remote(src, dst, ss.at[g], rs.at[g], row, col)
            copy.start()
            copies.append(copy)
    for copy in copies:
        copy.wait_recv()
    for copy in copies:
        copy.wait_send()


def exchange_edges(n_row, n_col, top, bottom, left, right):
    vmem = pl.BlockSpec(memory_space=pltpu.VMEM)
    length, width = left.shape[1], top.shape[1]
    return pl.pallas_call(
        functools.partial(edge_kernel, n_row, n_col),
        name="grid_edges",
        out_shape=(
            jax.ShapeDtypeStruct((8, width), F32),
            jax.ShapeDtypeStruct((8, width), F32),
            jax.ShapeDtypeStruct((8, length + 256), F32),
            jax.ShapeDtypeStruct((8, length + 256), F32),
        ),
        in_specs=[vmem] * 4,
        out_specs=(vmem,) * 4,
        scratch_shapes=[pltpu.SemaphoreType.DMA((9,)), pltpu.SemaphoreType.DMA((9,))],
        compiler_params=pltpu.CompilerParams(collective_id=1, has_side_effects=True),
    )(top, bottom, left, right)


CHUNK = 128
STRIP = 64


def diffuse_kernel(n_row, n_col, field_ref, up_ref, down_ref, west_ref, east_ref, out_ref, one, two, in_sem, out_sem):
    length, width = field_ref.shape
    wide = width + 128
    n_chunk = length // CHUNK
    me_r = lax.axis_index("row")
    me_c = lax.axis_index("col")

    def load(i):
        return pltpu.make_async_copy(
            field_ref.at[pl.ds(i * CHUNK, CHUNK)], one.at[pl.ds(8 + i * CHUNK, CHUNK), pl.ds(0, width)], in_sem.at[i]
        )

    for i in range(n_chunk):
        load(i).start()
    not_first_row = (me_r > 0).astype(F32)
    not_last_row = (me_r < n_row - 1).astype(F32)
    not_first_col = (me_c > 0).astype(F32)
    not_last_col = (me_c < n_col - 1).astype(F32)
    lane = iota((1, 128), 1)
    keep_lane = jnp.where(lane < 8, not_last_col, jnp.where(lane >= 120, not_first_col, 0.0))
    one[0:8, 0:width] = up_ref[...] * not_first_row
    one[length + 8:length + 16, 0:width] = down_ref[...] * not_last_row
    gap = jnp.zeros((112, 128), F32)
    for i in range(length // 128 + 2):
        here = pl.ds(i * 128, 128)
        tile = jnp.transpose(jnp.concatenate([east_ref[:, here], gap, west_ref[:, here]], axis=0)) * keep_lane
        if i == 0:
            one[0:8, width:wide] = tile[120:128] * not_first_row
        elif i == length // 128 + 1:
            one[length + 8:length + 16, width:wide] = tile[0:8] * not_last_row
        else:
            one[8 + (i - 1) * 128:8 + i * 128, width:wide] = tile
    for i in range(n_chunk):
        load(i).wait()

    keep_cols = jnp.concatenate([jnp.ones((1, width), F32), keep_lane], axis=1)

    def summed(src, start, n):
        window = src[pl.ds(pl.multiple_of(start - 8, 8), n + 16), :]
        centre = window[8:8 + n]
        above = window[7:7 + n]
        below = window[9:9 + n]
        return (centre + above) + (below + pltpu.roll(centre, 1, 1)) + pltpu.roll(centre, wide - 1, 1)

    def edge(src, dst):
        for start, keep in ((0, not_first_row), (length + 8, not_last_row)):
            c = src[start:start + 8, :]
            if start == 0:
                above = pltpu.roll(c, 1, 0)
                below = src[1:9, :]
            else:
                above = src[start - 1:start + 7, :]
                below = pltpu.roll(c, 7, 0)
            total = c + above + below + pltpu.roll(c, 1, 1) + pltpu.roll(c, wide - 1, 1)
            dst[start:start + 8, :] = total * keep_cols * keep

    src, dst = one, two
    for step in range(STEPS):
        if step < STEPS - 1:
            edge(src, dst)

            def strip(i, carry, src=src, dst=dst):
                start = pl.multiple_of(8 + i * STRIP, 8)
                total = summed(src, start, STRIP)
                dst[pl.ds(start, STRIP), 0:width] = total[:, 0:width]
                dst[pl.ds(start, STRIP), width:wide] = total[:, width:wide] * keep_lane
                return carry

            lax.fori_loop(0, length // STRIP, strip, 0)
        else:

            def strip(i, carry, src=src, dst=dst):
                start = pl.multiple_of(8 + i * STRIP, 8)
                total = summed(src, start, STRIP)
                dst[pl.ds(start, STRIP), 0:width] = total[:, 0:width] * (0.2 ** STEPS)
                return carry

            for i in range(n_chunk):
                lax.fori_loop(i * (CHUNK // STRIP), (i + 1) * (CHUNK // STRIP), strip, 0)
                store_chunk(dst, out_ref, out_sem, i, width).start()
        src, dst = dst, src
    for i in range(n_chunk):
        store_chunk(src, out_ref, out_sem, i, width).wait()


def store_chunk(buf, out_ref, out_sem, i, width):
    return pltpu.make_async_copy(
        buf.at[pl.ds(8 + i * CHUNK, CHUNK), pl.ds(0, width)], out_ref.at[pl.ds(i * CHUNK, CHUNK)], out_sem.at[i]
    )


def diffuse(n_row, n_col, field, up, down, west, east):
    length, width = field.shape
    vmem = pl.BlockSpec(memory_space=pltpu.VMEM)
    hbm = pl.BlockSpec(memory_space=pl.ANY)
    n_chunk = length // CHUNK
    return pl.pallas_call(
        functools.partial(diffuse_kernel, n_row, n_col),
        name="diffuse",
        out_shape=jax.ShapeDtypeStruct(field.shape, F32),
        in_specs=[hbm] + [vmem] * 4,
        out_specs=hbm,
        scratch_shapes=[
            pltpu.VMEM((length + 16, width + 128), F32),
            pltpu.VMEM((length + 16, width + 128), F32),
            pltpu.SemaphoreType.DMA((n_chunk,)),
            pltpu.SemaphoreType.DMA((n_chunk,)),
        ],
        compiler_params=pltpu.CompilerParams(vmem_limit_bytes=32 * 2**20),
        cost_estimate=pl.CostEstimate(flops=4 * 5 * length * width, bytes_accessed=8 * length * width, transcendentals=0),
    )(field, up, down, west, east)


def per_device(right_side, anchor, tiles, neighbours, owners, row_offset, col_offset, macro_density):
    n_blk, _, side, _ = tiles.shape[0], tiles.shape[1], tiles.shape[2], tiles.shape[3]
    n_row, n_col = lax.axis_size("row"), lax.axis_size("col")
    solution, arrived = solve(
        n_row, n_col, neighbours, right_side, anchor, owners.reshape(n_blk, side),
        row_offset.reshape(n_blk, side), col_offset.reshape(n_blk, side), tiles,
    )
    at_row = arrived[:, :CAP].reshape(-1)
    at_col = arrived[:, CAP:2 * CAP].reshape(-1)
    grid_rows, grid_cols = macro_density.shape

    def window_of(position, limit):
        start_cell = jnp.clip(jnp.floor(position).astype(jnp.int32) - 7, 0, limit - 16)
        cells = lax.iota(jnp.int32, limit)[None, :]
        inside = ((cells >= start_cell[:, None]) & (cells < start_cell[:, None] + 16)).astype(F32)
        offset = cells.astype(F32) - position[:, None]
        return (jnp.exp(-0.5 * offset * offset) * inside).astype(BF16)

    spread = lax.dot_general(
        window_of(at_row, grid_rows), window_of(at_col, grid_cols), (((0,), (0,)), ((), ())), preferred_element_type=F32
    )
    field = macro_density + spread
    edges = exchange_edges(
        n_row, n_col, field[:8], field[-8:], field[:, :8].T, field[:, -8:].T
    )
    return solution, diffuse(n_row, n_col, field, *edges)


def solution(mesh):
    blocks = P(("row", "col"))
    return jax.shard_map(
        per_device,
        mesh=mesh,
        in_specs=(
            P(("row", "col"), None, None),
            P(("row", "col"), None),
            P(("row", "col"), None, None, None),
            P(("row", "col"), None),
            P(("row", "col"), None),
            blocks,
            blocks,
            P("row", "col"),
        ),
        out_specs=(P(("row", "col"), None, None), P("row", "col")),
        check_vma=False,
    )
```

```python
import functools

import jax
import jax.numpy as jnp
from jax import lax
from jax.experimental import pallas as pl
from jax.experimental.pallas import tpu as pltpu
from jax.sharding import PartitionSpec as P

MESH = pl.DeviceIdType.MESH
F32 = jnp.float32
BF16 = jnp.bfloat16
STEPS = 4
CAP = 32
NONE = -1000.0
AROUND = [(dr, dc) for dr in (-1, 0, 1) for dc in (-1, 0, 1)]


def nt_dot(a, b):
    return lax.dot_general(a, b, (((1,), (1,)), ((), ())), preferred_element_type=F32)


def nn_dot(a, b):
    return jnp.dot(a, b, preferred_element_type=F32)


def split3(x):
    hi = x.astype(BF16)
    rest = x - hi.astype(F32)
    mid = rest.astype(BF16)
    low = (rest - mid.astype(F32)).astype(BF16)
    return hi, mid, low


def iota(shape, dim):
    return lax.broadcasted_iota(jnp.int32, shape, dim)


def remote(src, dst, send, recv, row, col):
    return pltpu.make_async_remote_copy(
        src_ref=src, dst_ref=dst, send_sem=send, recv_sem=recv,
        device_id={"row": row, "col": col}, device_id_type=MESH,
    )


def solve_kernel(
    n_row, n_col,
    nbr_ref, rhs_ref, anchor_ref, owner_ref, roff_ref, coff_ref, tiles_ref,
    sol_ref, pos_ref,
    stage, thi, tlo, xbuf, sel, spread_sel, gath, terms, back, recv,
    ar_row, ar_col, own_hot, rank_sc, weight_sc, out_rows, mid_rows, end_rows, table_sc,
    tile_sem, fs, fr, bs, br, rs, rr, cs, cr, away1, got, away2, land, keep_sem,
):
    n_blk, fan, side, _ = thi.shape
    rows = 2 * n_blk
    q_own = n_blk * fan * 8
    q_all = q_own + n_blk * 8
    n_dev = n_row * n_col
    me_r = lax.axis_index("row")
    me_c = lax.axis_index("col")
    row_order = sorted(range(1, n_row), key=lambda d: -min(d, n_row - d))
    col_order = sorted(range(1, n_col), key=lambda d: -(min(d // 4, 4 - d // 4) + min(d % 4, 4 - d % 4)))
    around = sorted((g for g in range(9) if g != 4), key=lambda g: -abs(AROUND[g][0]) - 2 * abs(AROUND[g][1]))

    for b in range(n_blk):
        pltpu.make_async_copy(tiles_ref.at[b], stage.at[b], tile_sem.at[b]).start()

    barrier = pltpu.get_barrier_semaphore()
    peers = [AROUND[g] for g in around if AROUND[g][0] and AROUND[g][1]]
    peers += [(0, d) for d in col_order] + [(d, 0) for d in row_order]
    for dr, dc in peers:
        pl.semaphore_signal(
            barrier, inc=1,
            device_id={"row": lax.rem(me_r + dr + n_row, n_row), "col": lax.rem(me_c + dc + n_col, n_col)},
            device_id_type=MESH,
        )

    own_lo = 4 * rows
    below = iota((side - 9 * rows, side), 0)
    for it in range(3):
        xbuf[it, 9 * rows:side, :] = jnp.where(below == 0, 1.0, 0.0)
    for b in range(n_blk):
        xbuf[0, own_lo + 2 * b:own_lo + 2 * b + 2, :] = rhs_ref[b]

    upper = (iota((side, side), 0) < iota((side, side), 1)).astype(F32).astype(BF16)
    count = jnp.zeros((n_dev, 1), F32)
    held = jnp.zeros((1, n_dev), F32)
    for b in range(n_blk):
        hot = (owner_ref[b:b + 1, :] == iota((n_dev, side), 0)).astype(F32)
        before = nn_dot(hot.astype(BF16), upper) + count
        rank_sc[b:b + 1, :] = jnp.sum(hot * before, axis=0, keepdims=True)
        count = count + jnp.sum(hot, axis=1, keepdims=True)
        turned = jnp.transpose(hot)
        own_hot[b] = turned.astype(BF16)
        held = held + jnp.sum(turned, axis=0, keepdims=True)

    pl.semaphore_wait(barrier, len(peers))

    def x_rows(it, g):
        return xbuf.at[it, pl.ds(g * rows, rows)]

    pending = []

    def forward(it):
        for g in around:
            dr, dc = AROUND[g]
            copy = remote(
                x_rows(it, 4), x_rows(it, 8 - g), fs.at[it, g], fr.at[it, 8 - g],
                lax.rem(me_r + dr + n_row, n_row), lax.rem(me_c + dc + n_col, n_col),
            )
            copy.start()
            pending.append(copy)

    def forward_wait(it):
        for g in around:
            remote(x_rows(it, 4), x_rows(it, g), fs.at[it, g], fr.at[it, g], me_r, me_c).wait_recv()

    def backward(it):
        for g in around:
            dr, dc = AROUND[g]
            copy = remote(
                back.at[it, pl.ds(g * rows, rows)], recv.at[it, 8 - g], bs.at[it, g], br.at[it, 8 - g],
                lax.rem(me_r + dr + n_row, n_row), lax.rem(me_c + dc + n_col, n_col),
            )
            copy.start()
            pending.append(copy)

    def backward_wait(it):
        for g in around:
            remote(back.at[it, pl.ds(g * rows, rows)], recv.at[it, g], bs.at[it, g], br.at[it, g], me_r, me_c).wait_recv()

    forward(0)

    ones_row = 9 * rows
    lane3 = iota((8, 3 * side), 1)
    part_row = iota((8, 1), 0)
    base_col = jnp.where(
        part_row < 6, (part_row // 2) * side + lax.rem(part_row, 2), jnp.where(part_row == 6, ones_row, -1)
    )
    moves = (part_row < 6).astype(jnp.int32)

    def select_row(q, slot):
        sel[q:q + 8, :] = (lane3 == base_col + moves * (2 * slot)).astype(F32).astype(BF16)

    for b in range(n_blk):
        for k in range(fan):
            named = nbr_ref[b, k]
            dev = named // n_blk
            slot = ((dev // n_col - me_r + 1) * 3 + (lax.rem(dev, n_col) - me_c + 1)) * n_blk + lax.rem(named, n_blk)
            select_row((b * fan + k) * 8, slot)
        select_row(q_own + b * 8, 4 * n_blk + b)
    sel_t = sel[:, 0:side].astype(F32) + sel[:, side:2 * side].astype(F32) + sel[:, 2 * side:].astype(F32)
    spread_sel[...] = jnp.transpose(jnp.concatenate([sel_t, jnp.zeros((384 - q_all, side), F32)], axis=0)).astype(BF16)
    terms[...] = jnp.zeros_like(terms)

    def split_block(b, carry):
        pltpu.make_async_copy(tiles_ref.at[b], stage.at[b], tile_sem.at[b]).wait()
        for k in range(fan):
            t = stage[b, k]
            hi = t.astype(BF16)
            thi[b, k] = hi
            tlo[b, k] = (t - hi.astype(F32)).astype(BF16)
        return carry

    lax.fori_loop(0, n_blk, split_block, 0)

    def apply(it, after_forward=None):
        forward_wait(it)
        if after_forward is not None:
            after_forward()
        parts = jnp.concatenate(split3(xbuf[it]), axis=0)
        gath[...] = nn_dot(sel[...], parts)

        def one_block(b, carry):
            own = gath[pl.ds(pl.multiple_of(q_own + b * 8, 8), 8), :]
            own_b = own.astype(BF16)
            total = jnp.zeros((8, side), F32)
            for k in range(fan):
                q = pl.multiple_of((b * fan + k) * 8, 8)
                far = gath[pl.ds(q, 8), :]
                far_b = far.astype(BF16)
                total = total + nt_dot(far_b, thi[b, k]) + nt_dot(far_b, tlo[b, k])
                down = nn_dot(own_b, thi[b, k]) + nn_dot(own_b, tlo[b, k])
                terms[pl.ds(q, 8), :] = down[6:7, :] * far - down
            weight = total[6:7, :] + anchor_ref[pl.ds(b, 1), :]
            if it == 0:
                weight_sc[pl.ds(b, 1), :] = weight
            terms[pl.ds(pl.multiple_of(q_own + b * 8, 8), 8), :] = weight * own - total
            return carry

        lax.fori_loop(0, n_blk, one_block, 0)
        hi, mid, low = split3(terms[...])
        where_to = spread_sel[0:9 * rows, :]
        back[it] = nn_dot(where_to, hi) + nn_dot(where_to, mid) + nn_dot(where_to, low)
        backward(it)

    def applied(it):
        backward_wait(it)
        image = back[it, own_lo:own_lo + rows, :]
        for g in range(9):
            if g != 4:
                image = image + recv[it, g]
        return image

    def dots_start(it, pairs, more=None):
        lane = iota((8, 128), 1)
        tile = jnp.zeros((8, 128), F32)
        for d, (a, b) in enumerate(pairs):
            e = a * b
            e = e[0:8] + e[8:16]
            if d == 0 and more is not None:
                e = e + more
            tile = jnp.where(lane == d, jnp.sum(e, axis=1, keepdims=True), tile)
        ar_row[it, me_r] = tile
        for d in row_order:
            copy = remote(
                ar_row.at[it, me_r], ar_row.at[it, me_r], rs.at[it, d], rr.at[it, me_r],
                lax.rem(me_r + d, n_row), me_c,
            )
            copy.start()
            pending.append(copy)

    def dots_middle(it):
        for d in row_order:
            far = lax.rem(me_r + d, n_row)
            remote(ar_row.at[it, far], ar_row.at[it, far], rs.at[it, d], rr.at[it, far], me_r, me_c).wait_recv()
        ar_col[it, me_c] = jnp.sum(ar_row[it], axis=0)
        for d in col_order:
            copy = remote(
                ar_col.at[it, me_c], ar_col.at[it, me_c], cs.at[it, d], cr.at[it, me_c],
                me_r, lax.rem(me_c + d, n_col),
            )
            copy.start()
            pending.append(copy)

    def dots_end(it, n):
        for d in col_order:
            far = lax.rem(me_c + d, n_col)
            remote(ar_col.at[it, far], ar_col.at[it, far], cs.at[it, d], cr.at[it, far], me_r, me_c).wait_recv()
        t = jnp.sum(ar_col[it], axis=0)
        t = t + pltpu.roll(t, 4, 0)
        t = t + pltpu.roll(t, 2, 0)
        return [t[:, d:d + 1] for d in range(n)]

    def times(c, v):
        return jnp.concatenate([c] * (v.shape[0] // 8), axis=0) * v

    r0 = xbuf[0, own_lo:own_lo + rows, :]
    apply(0)
    w0 = applied(0)
    xbuf[1, own_lo:own_lo + rows, :] = w0
    forward(1)
    dots_start(0, [(r0, r0), (r0, w0)])
    apply(1, lambda: dots_middle(0))
    gamma0, curve0 = dots_end(0, 2)
    alpha0 = gamma0 / curve0
    z0 = applied(1)
    w1 = w0 - times(alpha0, z0)
    xbuf[2, own_lo:own_lo + rows, :] = w1
    forward(2)
    r1 = r0 - times(alpha0, w0)
    dots_start(1, [(r1, r1), (r1, w1), (r1, w0)])

    rank_of = iota((CAP, side), 0)
    table = jnp.zeros((8 * CAP, n_dev), F32)
    for b in range(n_blk):
        mine = rank_of == rank_sc[b:b + 1, :].astype(jnp.int32)
        values = [v[2 * b + c:2 * b + c + 1, :] for v in (r0, w0, w1) for c in (0, 1)]
        values += [roff_ref[b:b + 1, :].astype(F32), coff_ref[b:b + 1, :].astype(F32)]
        placed = jnp.concatenate([jnp.where(mine, v, 0.0) for v in values], axis=0)
        for part in split3(placed):
            table = table + nn_dot(part, own_hot[b])
    empty = iota((CAP, n_dev), 0).astype(F32) >= held
    table = jnp.concatenate(
        [table[0:6 * CAP], jnp.where(empty, NONE, table[6 * CAP:7 * CAP]), table[7 * CAP:]], axis=0
    )
    table = jnp.transpose(table)
    for o in range(n_dev):
        out_rows[o // n_col, o % n_col] = table[o:o + 1, :]
    keep = pltpu.make_async_copy(out_rows.at[me_r], mid_rows.at[:, me_r], keep_sem.at[0])
    keep.start()
    for d in row_order:
        far = lax.rem(me_r + d, n_row)
        copy = remote(out_rows.at[far], mid_rows.at[:, me_r], away1.at[d], got.at[me_r], far, me_c)
        copy.start()
        pending.append(copy)

    dots_middle(1)

    keep.wait()
    for d in row_order:
        far = lax.rem(me_r + d, n_row)
        remote(out_rows.at[far], mid_rows.at[:, far], away1.at[d], got.at[far], me_r, me_c).wait_recv()
    keep2 = pltpu.make_async_copy(mid_rows.at[me_c], end_rows.at[me_c], keep_sem.at[1])
    keep2.start()
    for d in col_order:
        far = lax.rem(me_c + d, n_col)
        copy = remote(mid_rows.at[far], end_rows.at[me_c], away2.at[d], land.at[me_c], me_r, far)
        copy.start()
        pending.append(copy)

    forward_wait(2)
    gamma1, r1w1, r1w0 = dots_end(1, 3)
    beta0 = gamma1 / gamma0
    curve1 = r1w1 + 2.0 * beta0 * r1w0 + beta0 * beta0 * curve0
    alpha1 = gamma1 / curve1
    p1 = r1 + times(beta0, r0)
    s1 = w1 + times(beta0, w0)
    r2 = r1 - times(alpha1, s1)

    near_w0 = xbuf[1, 0:9 * rows, :]
    near_r1 = xbuf[0, 0:9 * rows, :] - times(alpha0, near_w0)
    near_r2 = near_r1 - times(alpha1, xbuf[2, 0:9 * rows, :] + times(beta0, near_w0))
    near_r2 = jnp.concatenate([near_r2, jnp.where(below == 0, 1.0, 0.0)], axis=0)
    gath[...] = nn_dot(sel[...], jnp.concatenate(split3(near_r2), axis=0))

    def energy_block(b, carry):
        own_b = gath[pl.ds(pl.multiple_of(q_own + b * 8, 8), 8), :].astype(BF16)
        for k in range(fan):
            q = pl.multiple_of((b * fan + k) * 8, 8)
            down = nn_dot(own_b, thi[b, k]) + nn_dot(own_b, tlo[b, k])
            terms[pl.ds(q, 8), :] = down[6:7, :] * gath[pl.ds(q, 8), :] - 2.0 * down
        return carry

    lax.fori_loop(0, n_blk, energy_block, 0)

    def over_parts(v):
        return v + pltpu.roll(v, q_own - 2, 0) + pltpu.roll(v, q_own - 4, 0)

    cross = over_parts(terms[0:q_own, :]) * over_parts(gath[0:q_own, :])
    cross = jnp.sum(cross.reshape(q_own // 8, 8, side), axis=0)
    cross = jnp.where(iota((8, side), 0) < 2, cross, 0.0)
    weights = weight_sc[...]
    weights = jnp.concatenate([weights[b:b + 1] for b in range(n_blk) for _ in (0, 1)], axis=0)
    dots_start(2, [(r2, weights * r2), (r2, r2), (r2, s1)], more=cross)

    keep2.wait()
    for d in col_order:
        far = lax.rem(me_c + d, n_col)
        remote(mid_rows.at[far], end_rows.at[far], away2.at[d], land.at[far], me_r, me_c).wait_recv()
    dots_middle(2)
    for o in range(n_dev):
        table_sc[o:o + 1, :] = end_rows[o // n_row, o % n_row]
    curve_r2, gamma2, r2s1 = dots_end(2, 3)
    beta1 = gamma2 / gamma1
    curve2 = curve_r2 + 2.0 * beta1 * r2s1 + beta1 * beta1 * curve1
    alpha2 = gamma2 / curve2

    of_b = alpha0 + alpha1 * (1.0 + beta0) + alpha2 * (1.0 + beta1 * (1.0 + beta0))
    of_w0 = -alpha1 * alpha0 - alpha2 * (alpha0 + alpha1 * beta0 + beta1 * alpha0)
    of_w1 = -alpha2 * alpha1
    lane = iota((1, 128), 1)

    def by_lane(first, second):
        return jnp.where(
            lane < CAP, first[0:1], jnp.where(lane < 2 * CAP, first[1:2], jnp.where(lane < 3 * CAP, second[0:1], second[1:2]))
        )

    near = table_sc[:, 0:128] * by_lane(of_b, of_w0)
    far = table_sc[:, 128:256]
    moved = near + pltpu.roll(near, 64, 1) + far * by_lane(of_w1, of_w1)
    pos_ref[...] = pltpu.roll(far, 64, 1) + 3.0 * jnp.tanh(moved)

    x = times(alpha0, r0) + times(alpha1, p1) + times(alpha2, r2 + times(beta1, p1))
    for b in range(n_blk):
        sol_ref[b] = x[2 * b:2 * b + 2, :]
    for copy in pending:
        copy.wait_send()


def solve(n_row, n_col, neighbours, right_side, anchor, owners, row_offset, col_offset, tiles):
    n_blk, fan, side, _ = tiles.shape
    rows = 2 * n_blk
    n_dev = n_row * n_col
    q_all = n_blk * fan * 8 + n_blk * 8
    vmem = pl.BlockSpec(memory_space=pltpu.VMEM)
    dma = pltpu.SemaphoreType.DMA
    return pl.pallas_call(
        functools.partial(solve_kernel, n_row, n_col),
        name="solve_and_route",
        out_shape=(
            jax.ShapeDtypeStruct(right_side.shape, F32),
            jax.ShapeDtypeStruct((n_dev, 128), F32),
        ),
        in_specs=[pl.BlockSpec(memory_space=pltpu.SMEM)] + [vmem] * 5 + [pl.BlockSpec(memory_space=pl.ANY)],
        out_specs=(vmem, vmem),
        scratch_shapes=[
            pltpu.VMEM(tiles.shape, F32),
            pltpu.VMEM(tiles.shape, BF16),
            pltpu.VMEM(tiles.shape, BF16),
            pltpu.VMEM((3, side, side), F32),
            pltpu.VMEM((q_all, 3 * side), BF16),
            pltpu.VMEM((side, 384), BF16),
            pltpu.VMEM((q_all, side), F32),
            pltpu.VMEM((384, side), F32),
            pltpu.VMEM((2, 9 * rows, side), F32),
            pltpu.VMEM((2, 9, rows, side), F32),
            pltpu.VMEM((3, n_row, 8, 128), F32),
            pltpu.VMEM((3, n_col, 8, 128), F32),
            pltpu.VMEM((n_blk, side, n_dev), BF16),
            pltpu.VMEM((n_blk, side), F32),
            pltpu.VMEM((n_blk, side), F32),
            pltpu.VMEM((n_row, n_col, 1, 8 * CAP), F32),
            pltpu.VMEM((n_col, n_row, 1, 8 * CAP), F32),
            pltpu.VMEM((n_col, n_row, 1, 8 * CAP), F32),
            pltpu.VMEM((n_dev, 8 * CAP), F32),
            dma((n_blk,)),
            dma((3, 9)), dma((3, 9)), dma((3, 9)), dma((3, 9)),
            dma((3, n_row)), dma((3, n_row)), dma((3, n_col)), dma((3, n_col)),
            dma((n_row,)), dma((n_row,)), dma((n_col,)), dma((n_col,)), dma((2,)),
        ],
        compiler_params=pltpu.CompilerParams(
            collective_id=0, has_side_effects=True, vmem_limit_bytes=48 * 2**20
        ),
        cost_estimate=pl.CostEstimate(flops=10**9, bytes_accessed=2**23, transcendentals=0),
    )(neighbours, right_side, anchor, owners, row_offset, col_offset, tiles)


def grid_kernel(
    n_row, n_col,
    pos_ref, macro_ref, out_ref,
    one, two, bell_col, left_sel, right_sel, low_part, high_part, place,
    top_s, bottom_s, west_s, east_s, up_r, down_r, west_r, east_r, keep_top, keep_bottom, side,
    in_sem, out_sem, ss, rs,
):
    length, width = macro_ref.shape
    n_dev = n_row * n_col
    n_slot = bell_col.shape[0]
    n_chunk = length // CHUNK
    me_r = lax.axis_index("row")
    me_c = lax.axis_index("col")
    log2e = 1.4426950408889634

    def at(dr, dc):
        return lax.rem(me_r + dr + n_row, n_row), lax.rem(me_c + dc + n_col, n_col)

    def load(i):
        return pltpu.make_async_copy(
            macro_ref.at[pl.ds(i * BAND, BAND)], one.at[pl.ds(8 + i * BAND, BAND)], in_sem.at[i]
        )

    def store(buf, i):
        return pltpu.make_async_copy(
            buf.at[pl.ds(8 + i * CHUNK, CHUNK)], out_ref.at[pl.ds(i * CHUNK, CHUNK)], out_sem.at[i]
        )

    barrier = pltpu.get_barrier_semaphore()
    around = sorted((g for g in range(9) if g != 4), key=lambda g: -abs(AROUND[g][0]) - 2 * abs(AROUND[g][1]))
    for g in around:
        row, col = at(*AROUND[g])
        pl.semaphore_signal(barrier, inc=1, device_id={"row": row, "col": col}, device_id_type=MESH)
    for i in range(length // BAND):
        load(i).start()
    rim = jnp.zeros((8, width), F32)
    for buf in (one, two):
        buf[0:8, :] = rim
        buf[length + 8:length + 16, :] = rim

    turned = jnp.transpose(pos_ref[...])
    at_row = turned[0:CAP]
    start = jnp.clip(jnp.floor(at_row) - 7.0, 0.0, length - 16.0)
    block = jnp.floor(start * (1.0 / 32.0))
    rows48 = iota((48, n_dev), 0).astype(F32)
    for j in range(CAP):
        u = rows48 + 32.0 * block[j:j + 1]
        d = u - at_row[j:j + 1]
        inside = jnp.abs(u - (start[j:j + 1] + 7.5)) < 8.0
        bell = jnp.where(inside, jnp.exp2(d * d * (-0.5 * log2e)), 0.0).astype(BF16)
        here = slice(j * n_dev, (j + 1) * n_dev)
        low_part[:, here] = bell[0:32]
        high_part[:, here] = jnp.concatenate([bell[32:48], jnp.zeros((16, n_dev), BF16)], axis=0)
        place[:, here] = jnp.broadcast_to(block[j:j + 1], (32, n_dev)).astype(BF16)

    all_pos = pos_ref[...]
    at_col = pltpu.roll(all_pos, 128 - CAP, 1)
    middle = jnp.clip(jnp.floor(at_col) - 7.0, 0.0, width - 16.0) + 7.5
    v = iota((1, width), 1).astype(F32)

    def some_columns(i, carry):
        p, m = carry
        for k in range(4):
            d = v - p[:, k:k + 1]
            inside = jnp.abs(v - m[:, k:k + 1]) < 8.0
            bell = jnp.where(inside, jnp.exp2(d * d * (-0.5 * log2e)), 0.0)
            bell_col[pl.ds(pl.multiple_of((i * 4 + k) * n_dev, n_dev), n_dev), :] = bell.astype(BF16)
        return pltpu.roll(p, 124, 1), pltpu.roll(m, 124, 1)

    lax.fori_loop(0, CAP // 4, some_columns, (at_col, middle))

    def build(dst, band):
        for sub in range(BAND // 32):
            block_id = (band * (BAND // 32) + sub).astype(F32)
            first = place[...] == jnp.full((32, n_slot), block_id, F32).astype(BF16)
            second = place[...] == jnp.full((32, n_slot), block_id - 1.0, F32).astype(BF16)
            zero = jnp.zeros((32, n_slot), BF16)
            dst[sub * 32:(sub + 1) * 32, :] = jnp.where(
                first, low_part[...], jnp.where(second, high_part[...], zero)
            )

    def product(src, band):
        load(band).wait()
        here = pl.ds(pl.multiple_of(8 + band * BAND, 8), BAND)
        one[here, :] = one[here, :] + nn_dot(src[...], bell_col[...])

    build(left_sel, jnp.int32(0))

    def two_bands(i, carry):
        build(right_sel, 2 * i + 1)
        product(left_sel, 2 * i)
        build(left_sel, jnp.minimum(2 * i + 2, length // BAND - 1))
        product(right_sel, 2 * i + 1)
        return carry

    lax.fori_loop(0, length // BAND // 2, two_bands, 0)

    top_s[...] = one[8:16, :]
    bottom_s[...] = one[length:length + 8, :]
    keep_top[...] = one[8:24, :]
    keep_bottom[...] = one[length - 8:length + 8, :]
    lane = iota((1, 128), 1)
    for i in range(length // 128):
        here = slice(8 + i * 128, 8 + (i + 1) * 128)
        tile = jnp.transpose(jnp.where(lane < 64, one[here, 0:128], one[here, width - 128:width]))
        west_s[:, i * 128:(i + 1) * 128] = tile[0:8]
        east_s[:, i * 128:(i + 1) * 128] = tile[120:128]

    pl.semaphore_wait(barrier, 8)
    first = (slice(None), pl.ds(0, 128))
    last = (slice(None), pl.ds(length - 128, 128))
    inner = (slice(None), pl.ds(128, length))
    above = (slice(None), pl.ds(0, 128))
    below = (slice(None), pl.ds(length + 128, 128))
    plan = {
        (-1, 0): (top_s, down_r),
        (1, 0): (bottom_s, up_r),
        (0, -1): (west_s, east_r.at[inner]),
        (0, 1): (east_s, west_r.at[inner]),
        (-1, -1): (west_s.at[first], east_r.at[below]),
        (-1, 1): (east_s.at[first], west_r.at[below]),
        (1, -1): (west_s.at[last], east_r.at[above]),
        (1, 1): (east_s.at[last], west_r.at[above]),
    }
    copies = []
    for g in around:
        src, dst = plan[AROUND[g]]
        row, col = at(*AROUND[g])
        copy = remote(src, dst, ss.at[g], rs.at[g], row, col)
        copy.start()
        copies.append(copy)

    def summed(src, begin, n):
        window = src[pl.ds(pl.multiple_of(begin - 8, 8), n + 16), :]
        centre = window[8:8 + n]
        return (
            (centre + window[7:7 + n]) + (window[9:9 + n] + pltpu.roll(centre, 1, 1)) + pltpu.roll(centre, width - 1, 1)
        )

    for src, dst in ((one, two), (two, one), (one, two)):

        def strip(i, carry, src=src, dst=dst):
            begin = pl.multiple_of(8 + i * CHUNK, 8)
            dst[pl.ds(begin, CHUNK), :] = summed(src, begin, CHUNK)
            return carry

        lax.fori_loop(0, n_chunk, strip, 0)

    for copy in copies:
        copy.wait_recv()
    not_first_row = (me_r > 0).astype(F32)
    not_last_row = (me_r < n_row - 1).astype(F32)
    not_first_col = (me_c > 0).astype(F32)
    not_last_col = (me_c < n_col - 1).astype(F32)
    scale = 0.2 ** STEPS

    def cross(t):
        n, m = t.shape
        return (t + pltpu.roll(t, 1, 0)) + (pltpu.roll(t, n - 1, 0) + pltpu.roll(t, 1, 1)) + pltpu.roll(t, m - 1, 1)

    pad = jnp.zeros((120, 128), F32)
    corners = []
    for halo, order in ((up_r, 0), (down_r, 1)):
        for part in (halo[:, 0:128], halo[:, width - 128:width]):
            corners.append(jnp.transpose(jnp.concatenate([pad, part] if order == 0 else [part, pad], axis=0)))
    own_west = jnp.concatenate([corners[0][0:8], west_s[...], corners[2][0:8]], axis=1)
    own_east = jnp.concatenate([corners[1][120:128], east_s[...], corners[3][120:128]], axis=1)
    t = jnp.concatenate([west_r[...], own_west, own_east, east_r[...]], axis=0)
    down32 = iota((32, 1), 0)
    along = iota((1, length + 256), 1)
    mask = jnp.where(down32 < 8, not_first_col, jnp.where(down32 >= 24, not_last_col, 1.0)) * jnp.where(
        along < 128, jnp.where(along >= 120, not_first_row, 0.0),
        jnp.where(along >= length + 128, jnp.where(along < length + 136, not_last_row, 0.0), 1.0),
    )
    t = t * mask
    for step in range(STEPS):
        t = cross(t)
        if step < STEPS - 1:
            t = t * mask
    side[...] = t * scale

    def rim_rows(halo, kept, keep, at_top):
        r = jnp.concatenate([halo * keep, kept] if at_top else [kept, halo * keep], axis=0)
        near = iota((24, 1), 0)
        flag = jnp.where((near < 8) if at_top else (near >= 16), keep, 1.0)
        for step in range(STEPS):
            r = cross(r)
            if step < STEPS - 1:
                r = r * flag
        return (r[8:16] if at_top else r[8:16]) * scale

    zero112 = jnp.zeros((112, 128), F32)

    def side_tile(i):
        here = pl.ds(pl.multiple_of((i + 1) * 128, 128), 128)
        return jnp.transpose(jnp.concatenate([side[8:16, here], zero112, side[16:24, here]], axis=0))

    def finish(i, carry):
        begin = pl.multiple_of(8 + i * CHUNK, 8)
        total = summed(two, begin, CHUNK) * scale
        for h in range(CHUNK // 128):
            rows_h = slice(h * 128, (h + 1) * 128)
            tile = side_tile(i * (CHUNK // 128) + h)
            here = pl.ds(pl.multiple_of(begin + h * 128, 8), 128)
            one[here, 0:128] = jnp.where(lane < 4, tile, total[rows_h, 0:128])
            one[here, 128:width - 128] = total[rows_h, 128:width - 128]
            one[here, width - 128:width] = jnp.where(lane >= 124, tile, total[rows_h, width - 128:width])
        return carry

    def start_store(i, carry):
        finish(i, carry)
        store(one, i).start()
        return carry

    lax.fori_loop(1, n_chunk - 1, start_store, 0)
    for i, at_row8, rim8 in (
        (0, 8, rim_rows(up_r[...], keep_top[...], not_first_row, True)),
        (n_chunk - 1, length, rim_rows(down_r[...], keep_bottom[...], not_last_row, False)),
    ):
        finish(jnp.int32(i), 0)
        one[at_row8:at_row8 + 8, 0:128] = jnp.where(lane < 4, one[at_row8:at_row8 + 8, 0:128], rim8[:, 0:128])
        one[at_row8:at_row8 + 8, 128:width - 128] = rim8[:, 128:width - 128]
        one[at_row8:at_row8 + 8, width - 128:width] = jnp.where(
            lane >= 124, one[at_row8:at_row8 + 8, width - 128:width], rim8[:, width - 128:width]
        )
        store(one, i).start()

    def finish_store(i, carry):
        store(one, i).wait()
        return carry

    lax.fori_loop(0, n_chunk, finish_store, 0)
    for copy in copies:
        copy.wait_send()


CHUNK = 128
BAND = 256


def spread_and_diffuse(n_row, n_col, positions, macro):
    length, width = macro.shape
    n_slot = n_row * n_col * CAP
    any_space = pl.BlockSpec(memory_space=pl.ANY)
    dma = pltpu.SemaphoreType.DMA
    return pl.pallas_call(
        functools.partial(grid_kernel, n_row, n_col),
        name="spread_and_diffuse",
        out_shape=jax.ShapeDtypeStruct(macro.shape, F32),
        in_specs=[pl.BlockSpec(memory_space=pltpu.VMEM), any_space],
        out_specs=any_space,
        scratch_shapes=[
            pltpu.VMEM((length + 16, width), F32),
            pltpu.VMEM((length + 16, width), F32),
            pltpu.VMEM((n_slot, width), BF16),
            pltpu.VMEM((BAND, n_slot), BF16),
            pltpu.VMEM((BAND, n_slot), BF16),
            pltpu.VMEM((32, n_slot), BF16),
            pltpu.VMEM((32, n_slot), BF16),
            pltpu.VMEM((32, n_slot), BF16),
            pltpu.VMEM((8, width), F32),
            pltpu.VMEM((8, width), F32),
            pltpu.VMEM((8, length), F32),
            pltpu.VMEM((8, length), F32),
            pltpu.VMEM((8, width), F32),
            pltpu.VMEM((8, width), F32),
            pltpu.VMEM((8, length + 256), F32),
            pltpu.VMEM((8, length + 256), F32),
            pltpu.VMEM((16, width), F32),
            pltpu.VMEM((16, width), F32),
            pltpu.VMEM((32, length + 256), F32),
            dma((length // BAND,)),
            dma((length // CHUNK,)),
            dma((9,)),
            dma((9,)),
        ],
        compiler_params=pltpu.CompilerParams(
            collective_id=1, has_side_effects=True, vmem_limit_bytes=48 * 2**20
        ),
        cost_estimate=pl.CostEstimate(flops=10**10, bytes_accessed=8 * length * width, transcendentals=0),
    )(positions, macro)


def per_device(right_side, anchor, tiles, neighbours, owners, row_offset, col_offset, macro_density):
    n_blk, _, side, _ = tiles.shape[0], tiles.shape[1], tiles.shape[2], tiles.shape[3]
    n_row, n_col = lax.axis_size("row"), lax.axis_size("col")
    solution, arrived = solve(
        n_row, n_col, neighbours, right_side, anchor, owners.reshape(n_blk, side),
        row_offset.reshape(n_blk, side), col_offset.reshape(n_blk, side), tiles,
    )
    return solution, spread_and_diffuse(n_row, n_col, arrived, macro_density)


def solution(mesh):
    blocks = P(("row", "col"))
    return jax.shard_map(
        per_device,
        mesh=mesh,
        in_specs=(
            P(("row", "col"), None, None),
            P(("row", "col"), None),
            P(("row", "col"), None, None, None),
            P(("row", "col"), None),
            P(("row", "col"), None),
            blocks,
            blocks,
            P("row", "col"),
        ),
        out_specs=(P(("row", "col"), None, None), P("row", "col")),
        check_vma=False,
    )
```

```python
import functools

import jax
import jax.numpy as jnp
from jax import lax
from jax.experimental import pallas as pl
from jax.experimental.pallas import tpu as pltpu
from jax.sharding import PartitionSpec as P

MESH = pl.DeviceIdType.MESH
F32 = jnp.float32
BF16 = jnp.bfloat16
STEPS = 4
CAP = 32
NONE = -1000.0
AROUND = [(dr, dc) for dr in (-1, 0, 1) for dc in (-1, 0, 1)]


def nt_dot(a, b):
    return lax.dot_general(a, b, (((1,), (1,)), ((), ())), preferred_element_type=F32)


def nn_dot(a, b):
    return jnp.dot(a, b, preferred_element_type=F32)


def split3(x):
    hi = x.astype(BF16)
    rest = x - hi.astype(F32)
    mid = rest.astype(BF16)
    low = (rest - mid.astype(F32)).astype(BF16)
    return hi, mid, low


def iota(shape, dim):
    return lax.broadcasted_iota(jnp.int32, shape, dim)


def remote(src, dst, send, recv, row, col):
    return pltpu.make_async_remote_copy(
        src_ref=src, dst_ref=dst, send_sem=send, recv_sem=recv,
        device_id={"row": row, "col": col}, device_id_type=MESH,
    )


def solve_kernel(
    n_row, n_col,
    nbr_hbm, rhs_hbm, anchor_hbm, owner_hbm, roff_hbm, coff_hbm, tiles_ref,
    sol_ref, pos_ref,
    stage, thi, tlo, xbuf, sel, spread_sel, gath, terms, back, recv,
    ar_row, ar_col, own_hot, rank_sc, weight_sc, out_rows, mid_rows, end_rows, table_sc,
    own_sel, own_g, down_sc, sums_sc, far_sum, down_sum, nbr_sc, rhs_ref, anchor_ref, owner_ref, roff_ref, coff_ref, small_sem,
    tile_sem, fs, fr, bs, br, rs, rr, cs, cr, away1, got, away2, land, keep_sem,
):
    n_blk, fan, side, _ = thi.shape
    rows = 2 * n_blk
    q_own = n_blk * fan * 8
    q_all = q_own + n_blk * 8
    n_dev = n_row * n_col
    me_r = lax.axis_index("row")
    me_c = lax.axis_index("col")
    row_order = sorted(range(1, n_row), key=lambda d: -min(d, n_row - d))
    col_order = sorted(range(1, n_col), key=lambda d: -(min(d // 4, 4 - d // 4) + min(d % 4, 4 - d % 4)))
    around = sorted((g for g in range(9) if g != 4), key=lambda g: -abs(AROUND[g][0]) - 2 * abs(AROUND[g][1]))

    small = [
        pltpu.make_async_copy(src, dst, small_sem.at[i])
        for i, (src, dst) in enumerate((
            (rhs_hbm, rhs_ref), (owner_hbm, owner_ref), (nbr_hbm, nbr_sc),
            (anchor_hbm, anchor_ref), (roff_hbm, roff_ref), (coff_hbm, coff_ref),
        ))
    ]
    for copy in small:
        copy.start()
    for b in range(n_blk):
        pltpu.make_async_copy(tiles_ref.at[b], stage.at[b], tile_sem.at[b]).start()

    barrier = pltpu.get_barrier_semaphore()
    peers = [AROUND[g] for g in around if AROUND[g][0] and AROUND[g][1]]
    peers += [(0, d) for d in col_order] + [(d, 0) for d in row_order]
    for dr, dc in peers:
        pl.semaphore_signal(
            barrier, inc=1,
            device_id={"row": lax.rem(me_r + dr + n_row, n_row), "col": lax.rem(me_c + dc + n_col, n_col)},
            device_id_type=MESH,
        )

    own_lo = 4 * rows
    below = iota((side - 9 * rows, side), 0)
    for it in range(3):
        xbuf[it, 9 * rows:side, :] = jnp.where(below == 0, 1.0, 0.0)
    for copy in small[:2]:
        copy.wait()
    for b in range(n_blk):
        xbuf[0, own_lo + 2 * b:own_lo + 2 * b + 2, :] = rhs_ref[b]

    upper = (iota((side, side), 0) < iota((side, side), 1)).astype(F32).astype(BF16)
    count = jnp.zeros((n_dev, 1), F32)
    held = jnp.zeros((1, n_dev), F32)
    for b in range(n_blk):
        hot = (owner_ref[0:1, b * side:(b + 1) * side] == iota((n_dev, side), 0)).astype(F32)
        before = nn_dot(hot.astype(BF16), upper) + count
        rank_sc[b:b + 1, :] = jnp.sum(hot * before, axis=0, keepdims=True)
        count = count + jnp.sum(hot, axis=1, keepdims=True)
        turned = jnp.transpose(hot)
        own_hot[b] = turned.astype(BF16)
        held = held + jnp.sum(turned, axis=0, keepdims=True)

    pl.semaphore_wait(barrier, len(peers))

    def x_rows(it, g):
        return xbuf.at[it, pl.ds(g * rows, rows)]

    pending = []

    def forward(it):
        for g in around:
            dr, dc = AROUND[g]
            copy = remote(
                x_rows(it, 4), x_rows(it, 8 - g), fs.at[it, g], fr.at[it, 8 - g],
                lax.rem(me_r + dr + n_row, n_row), lax.rem(me_c + dc + n_col, n_col),
            )
            copy.start()
            pending.append(copy)

    def forward_wait(it):
        for g in around:
            remote(x_rows(it, 4), x_rows(it, g), fs.at[it, g], fr.at[it, g], me_r, me_c).wait_recv()

    def backward(it):
        for g in around:
            dr, dc = AROUND[g]
            copy = remote(
                back.at[it, pl.ds(g * rows, rows)], recv.at[it, 8 - g], bs.at[it, g], br.at[it, 8 - g],
                lax.rem(me_r + dr + n_row, n_row), lax.rem(me_c + dc + n_col, n_col),
            )
            copy.start()
            pending.append(copy)

    def backward_wait(it):
        for g in around:
            remote(back.at[it, pl.ds(g * rows, rows)], recv.at[it, g], bs.at[it, g], br.at[it, g], me_r, me_c).wait_recv()

    forward(0)

    ones_row = 9 * rows
    lane3 = iota((8, 3 * side), 1)
    part_row = iota((8, 1), 0)
    base_col = jnp.where(
        part_row < 6, (part_row // 2) * side + lax.rem(part_row, 2), jnp.where(part_row == 6, ones_row, -1)
    )
    moves = (part_row < 6).astype(jnp.int32)

    lane_own = iota((8, 4 * rows), 1)
    own_col = jnp.where(
        part_row < 6, (part_row // 2) * rows + lax.rem(part_row, 2), jnp.where(part_row == 6, 3 * rows, -1)
    )

    def select_row(q, slot):
        sel[q:q + 8, :] = (lane3 == base_col + moves * (2 * slot)).astype(F32).astype(BF16)

    for copy in small[2:]:
        copy.wait()
    for b in range(n_blk):
        for k in range(fan):
            named = nbr_sc[k, b]
            dev = named // n_blk
            slot = ((dev // n_col - me_r + 1) * 3 + (lax.rem(dev, n_col) - me_c + 1)) * n_blk + lax.rem(named, n_blk)
            select_row((b * fan + k) * 8, slot)
        select_row(q_own + b * 8, 4 * n_blk + b)
        own_sel[b * 8:(b + 1) * 8, :] = (lane_own == own_col + moves * (2 * b)).astype(F32).astype(BF16)
    sel_t = sel[:, 0:side].astype(F32) + sel[:, side:2 * side].astype(F32) + sel[:, 2 * side:].astype(F32)
    spread_sel[...] = jnp.transpose(jnp.concatenate([sel_t, jnp.zeros((384 - q_all, side), F32)], axis=0)).astype(BF16)
    terms[...] = jnp.zeros_like(terms)

    def split_block(b, carry):
        pltpu.make_async_copy(tiles_ref.at[b], stage.at[b], tile_sem.at[b]).wait()
        for k in range(fan):
            t = stage[b, k]
            hi = t.astype(BF16)
            thi[b, k] = hi
            tlo[b, k] = (t - hi.astype(F32)).astype(BF16)
        return carry

    lax.fori_loop(0, n_blk, split_block, 0)

    first_row = jnp.where(iota((rows, side), 0) == 0, 1.0, 0.0).astype(BF16)

    def grouped(c, v):
        return (v.reshape(q_own // 8, 8, side) * c[None]).reshape(q_own, side)

    def over_parts(v):
        return v + pltpu.roll(v, q_own - 2, 0) + pltpu.roll(v, q_own - 4, 0)

    def own_products(it, own):
        own_g[...] = nn_dot(own_sel[...], jnp.concatenate(split3(own) + (first_row,), axis=0))

        def one_block(b, carry):
            own_b = own_g[pl.ds(pl.multiple_of(b * 8, 8), 8), :].astype(BF16)
            for k in range(fan):
                q = pl.multiple_of((b * fan + k) * 8, 8)
                down = nn_dot(own_b, thi[b, k]) + nn_dot(own_b, tlo[b, k])
                down_sc[pl.ds(q, 8), :] = down
                if it == 0:
                    sums_sc[pl.ds(q, 8), :] = jnp.broadcast_to(down[6:7, :], (8, side))
            return carry

        lax.fori_loop(0, n_blk, one_block, 0, unroll=2)
        down_sum[it] = over_parts(down_sc[...])

    def gather_far(it):
        parts = jnp.concatenate(split3(xbuf[it]), axis=0)
        gath[...] = nn_dot(sel[0:q_own, :], parts)

    def apply(it, after_forward=None):
        forward_wait(it)
        if after_forward is not None:
            after_forward()
        gather_far(it)

        def one_block(b, carry):
            total = jnp.zeros((8, side), F32)
            for k in range(fan):
                q = pl.multiple_of((b * fan + k) * 8, 8)
                far_b = gath[pl.ds(q, 8), :].astype(BF16)
                total = total + nt_dot(far_b, thi[b, k]) + nt_dot(far_b, tlo[b, k])
            weight = total[6:7, :] + anchor_ref[pl.ds(b, 1), :]
            if it == 0:
                weight_sc[pl.ds(b, 1), :] = weight
            own = own_g[pl.ds(pl.multiple_of(b * 8, 8), 8), :]
            terms[pl.ds(pl.multiple_of(q_own + b * 8, 8), 8), :] = weight * own - total
            return carry

        lax.fori_loop(0, n_blk, one_block, 0, unroll=2)
        terms[0:q_own, :] = sums_sc[...] * gath[...] - down_sc[...]
        hi, mid, low = split3(terms[...])
        where_to = spread_sel[0:9 * rows, :]
        back[it] = nn_dot(where_to, hi) + nn_dot(where_to, mid) + nn_dot(where_to, low)
        backward(it)
        far_sum[it] = over_parts(gath[...])

    def applied(it):
        backward_wait(it)
        image = back[it, own_lo:own_lo + rows, :]
        for g in range(9):
            if g != 4:
                image = image + recv[it, g]
        return image

    def dots_start(it, pairs, more=None):
        lane = iota((8, 128), 1)
        tile = jnp.zeros((8, 128), F32)
        for d, (a, b) in enumerate(pairs):
            e = a * b
            e = e[0:8] + e[8:16]
            if d == 0 and more is not None:
                e = e + more
            tile = jnp.where(lane == d, jnp.sum(e, axis=1, keepdims=True), tile)
        ar_row[it, me_r] = tile
        for d in row_order:
            copy = remote(
                ar_row.at[it, me_r], ar_row.at[it, me_r], rs.at[it, d], rr.at[it, me_r],
                lax.rem(me_r + d, n_row), me_c,
            )
            copy.start()
            pending.append(copy)

    def dots_middle(it):
        for d in row_order:
            far = lax.rem(me_r + d, n_row)
            remote(ar_row.at[it, far], ar_row.at[it, far], rs.at[it, d], rr.at[it, far], me_r, me_c).wait_recv()
        ar_col[it, me_c] = jnp.sum(ar_row[it], axis=0)
        for d in col_order:
            copy = remote(
                ar_col.at[it, me_c], ar_col.at[it, me_c], cs.at[it, d], cr.at[it, me_c],
                me_r, lax.rem(me_c + d, n_col),
            )
            copy.start()
            pending.append(copy)

    def dots_end(it, n):
        for d in col_order:
            far = lax.rem(me_c + d, n_col)
            remote(ar_col.at[it, far], ar_col.at[it, far], cs.at[it, d], cr.at[it, far], me_r, me_c).wait_recv()
        t = jnp.sum(ar_col[it], axis=0)
        t = t + pltpu.roll(t, 4, 0)
        t = t + pltpu.roll(t, 2, 0)
        return [t[:, d:d + 1] for d in range(n)]

    def times(c, v):
        return jnp.concatenate([c] * (v.shape[0] // 8), axis=0) * v

    rank_of = iota((CAP, side), 0)

    def by_owner(values_of):
        total = None
        for b in range(n_blk):
            mine = rank_of == rank_sc[b:b + 1, :].astype(jnp.int32)
            placed = jnp.concatenate([jnp.where(mine, v, 0.0) for v in values_of(b)], axis=0)
            for part in split3(placed):
                more = nn_dot(part, own_hot[b])
                total = more if total is None else total + more
        return total

    def both(v):
        return lambda b: [v[2 * b:2 * b + 1, :], v[2 * b + 1:2 * b + 2, :]]

    def offsets(b):
        return [r[b * side:(b + 1) * side].reshape(1, side).astype(F32) for r in (roff_ref, coff_ref)]

    r0 = xbuf[0, own_lo:own_lo + rows, :]
    own_products(0, r0)
    apply(0)
    table_r0 = by_owner(both(r0))
    table_off = by_owner(offsets)
    w0 = applied(0)
    xbuf[1, own_lo:own_lo + rows, :] = w0
    forward(1)
    dots_start(0, [(r0, r0), (r0, w0)])
    own_products(1, w0)
    apply(1, lambda: dots_middle(0))
    table_w0 = by_owner(both(w0))
    gamma0, curve0 = dots_end(0, 2)
    alpha0 = gamma0 / curve0
    z0 = applied(1)
    w1 = w0 - times(alpha0, z0)
    xbuf[2, own_lo:own_lo + rows, :] = w1
    r1 = r0 - times(alpha0, w0)
    dots_start(1, [(r1, r1), (r1, w1), (r1, w0)])
    forward(2)

    table = jnp.concatenate([table_r0, table_w0, by_owner(both(w1)), table_off], axis=0)
    empty = iota((CAP, n_dev), 0).astype(F32) >= held
    table = jnp.concatenate(
        [table[0:6 * CAP], jnp.where(empty, NONE, table[6 * CAP:7 * CAP]), table[7 * CAP:]], axis=0
    )
    table = jnp.transpose(table)
    for o in range(n_dev):
        out_rows[o // n_col, o % n_col] = table[o:o + 1, :]
    keep = pltpu.make_async_copy(out_rows.at[me_r], mid_rows.at[:, me_r], keep_sem.at[0])
    keep.start()
    for d in row_order:
        far = lax.rem(me_r + d, n_row)
        copy = remote(out_rows.at[far], mid_rows.at[:, me_r], away1.at[d], got.at[me_r], far, me_c)
        copy.start()
        pending.append(copy)

    dots_middle(1)

    keep.wait()
    for d in row_order:
        far = lax.rem(me_r + d, n_row)
        remote(out_rows.at[far], mid_rows.at[:, far], away1.at[d], got.at[far], me_r, me_c).wait_recv()
    keep2 = pltpu.make_async_copy(mid_rows.at[me_c], end_rows.at[me_c], keep_sem.at[1])
    keep2.start()
    for d in col_order:
        far = lax.rem(me_c + d, n_col)
        copy = remote(mid_rows.at[far], end_rows.at[me_c], away2.at[d], land.at[me_c], me_r, far)
        copy.start()
        pending.append(copy)

    own_products(2, w1)
    forward_wait(2)
    gather_far(2)
    far_r1 = far_sum[0] - grouped(alpha0, far_sum[1])
    down_r1 = down_sum[0] - grouped(alpha0, down_sum[1])
    far_w1 = over_parts(gath[...])
    gamma1, r1w1, r1w0 = dots_end(1, 3)
    beta0 = gamma1 / gamma0
    curve1 = r1w1 + 2.0 * beta0 * r1w0 + beta0 * beta0 * curve0
    alpha1 = gamma1 / curve1
    p1 = r1 + times(beta0, r0)
    s1 = w1 + times(beta0, w0)
    r2 = r1 - times(alpha1, s1)

    far_r2 = far_r1 - grouped(alpha1, far_w1 + grouped(beta0, far_sum[1]))
    down_r2 = down_r1 - grouped(alpha1, down_sum[2] + grouped(beta0, down_sum[1]))
    cross = far_r2 * (sums_sc[...] * far_r2 - 2.0 * down_r2)
    cross = jnp.sum(cross.reshape(q_own // 8, 8, side), axis=0)
    cross = jnp.where(iota((8, side), 0) < 2, cross, 0.0)
    weights = weight_sc[...]
    weights = jnp.concatenate([weights[b:b + 1] for b in range(n_blk) for _ in (0, 1)], axis=0)
    dots_start(2, [(r2, weights * r2), (r2, r2), (r2, s1)], more=cross)

    keep2.wait()
    for d in col_order:
        far = lax.rem(me_c + d, n_col)
        remote(mid_rows.at[far], end_rows.at[far], away2.at[d], land.at[far], me_r, me_c).wait_recv()
    dots_middle(2)
    for o in range(n_dev):
        table_sc[o:o + 1, :] = end_rows[o // n_row, o % n_row]
    curve_r2, gamma2, r2s1 = dots_end(2, 3)
    beta1 = gamma2 / gamma1
    curve2 = curve_r2 + 2.0 * beta1 * r2s1 + beta1 * beta1 * curve1
    alpha2 = gamma2 / curve2

    of_b = alpha0 + alpha1 * (1.0 + beta0) + alpha2 * (1.0 + beta1 * (1.0 + beta0))
    of_w0 = -alpha1 * alpha0 - alpha2 * (alpha0 + alpha1 * beta0 + beta1 * alpha0)
    of_w1 = -alpha2 * alpha1
    lane = iota((1, 128), 1)

    def by_lane(first, second):
        return jnp.where(
            lane < CAP, first[0:1], jnp.where(lane < 2 * CAP, first[1:2], jnp.where(lane < 3 * CAP, second[0:1], second[1:2]))
        )

    near = table_sc[:, 0:128] * by_lane(of_b, of_w0)
    far = table_sc[:, 128:256]
    moved = near + pltpu.roll(near, 64, 1) + far * by_lane(of_w1, of_w1)
    pos_ref[...] = pltpu.roll(far, 64, 1) + 3.0 * jnp.tanh(moved)

    x = times(alpha0, r0) + times(alpha1, p1) + times(alpha2, r2 + times(beta1, p1))
    for b in range(n_blk):
        sol_ref[b] = x[2 * b:2 * b + 2, :]
    for copy in pending:
        copy.wait_send()


def solve(n_row, n_col, neighbours, right_side, anchor, owners, row_offset, col_offset, tiles):
    n_blk, fan, side, _ = tiles.shape
    rows = 2 * n_blk
    n_dev = n_row * n_col
    q_all = n_blk * fan * 8 + n_blk * 8
    vmem = pl.BlockSpec(memory_space=pltpu.VMEM)
    dma = pltpu.SemaphoreType.DMA
    return pl.pallas_call(
        functools.partial(solve_kernel, n_row, n_col),
        name="solve_and_route",
        out_shape=(
            jax.ShapeDtypeStruct(right_side.shape, F32),
            jax.ShapeDtypeStruct((n_dev, 128), F32),
        ),
        in_specs=[pl.BlockSpec(memory_space=pltpu.HBM)] * 7,
        out_specs=(vmem, vmem),
        scratch_shapes=[
            pltpu.VMEM(tiles.shape, F32),
            pltpu.VMEM(tiles.shape, BF16),
            pltpu.VMEM(tiles.shape, BF16),
            pltpu.VMEM((3, side, side), F32),
            pltpu.VMEM((q_all, 3 * side), BF16),
            pltpu.VMEM((side, 384), BF16),
            pltpu.VMEM((8 * n_blk * fan, side), F32),
            pltpu.VMEM((384, side), F32),
            pltpu.VMEM((2, 9 * rows, side), F32),
            pltpu.VMEM((2, 9, rows, side), F32),
            pltpu.VMEM((3, n_row, 8, 128), F32),
            pltpu.VMEM((3, n_col, 8, 128), F32),
            pltpu.VMEM((n_blk, side, n_dev), BF16),
            pltpu.VMEM((n_blk, side), F32),
            pltpu.VMEM((n_blk, side), F32),
            pltpu.VMEM((n_row, n_col, 1, 8 * CAP), F32),
            pltpu.VMEM((n_col, n_row, 1, 8 * CAP), F32),
            pltpu.VMEM((n_col, n_row, 1, 8 * CAP), F32),
            pltpu.VMEM((n_dev, 8 * CAP), F32),
            pltpu.VMEM((8 * n_blk, 4 * rows), BF16),
            pltpu.VMEM((8 * n_blk, side), F32),
            pltpu.VMEM((8 * n_blk * fan, side), F32),
            pltpu.VMEM((8 * n_blk * fan, side), F32),
            pltpu.VMEM((2, 8 * n_blk * fan, side), F32),
            pltpu.VMEM((3, 8 * n_blk * fan, side), F32),
            pltpu.SMEM((fan, n_blk), jnp.int32),
            pltpu.VMEM(right_side.shape, F32),
            pltpu.VMEM(anchor.shape, F32),
            pltpu.VMEM(owners.shape, jnp.int32),
            pltpu.VMEM(row_offset.shape, jnp.int32),
            pltpu.VMEM(col_offset.shape, jnp.int32),
            dma((6,)),
            dma((n_blk,)),
            dma((3, 9)), dma((3, 9)), dma((3, 9)), dma((3, 9)),
            dma((3, n_row)), dma((3, n_row)), dma((3, n_col)), dma((3, n_col)),
            dma((n_row,)), dma((n_row,)), dma((n_col,)), dma((n_col,)), dma((2,)),
        ],
        compiler_params=pltpu.CompilerParams(
            collective_id=0, has_side_effects=True, vmem_limit_bytes=48 * 2**20
        ),
        cost_estimate=pl.CostEstimate(flops=10**9, bytes_accessed=2**23, transcendentals=0),
    )(neighbours, right_side, anchor, owners, row_offset, col_offset, tiles)


def grid_kernel(
    n_row, n_col,
    pos_ref, macro_ref, out_ref,
    one, two, bell_col, left_sel, right_sel, low_part, high_part, place,
    top_s, bottom_s, west_s, east_s, up_r, down_r, west_r, east_r, keep_top, keep_bottom, side,
    in_sem, out_sem, ss, rs,
):
    length, width = macro_ref.shape
    n_dev = n_row * n_col
    n_slot = bell_col.shape[0]
    n_chunk = length // CHUNK
    me_r = lax.axis_index("row")
    me_c = lax.axis_index("col")
    log2e = 1.4426950408889634

    def at(dr, dc):
        return lax.rem(me_r + dr + n_row, n_row), lax.rem(me_c + dc + n_col, n_col)

    def load(i):
        return pltpu.make_async_copy(
            macro_ref.at[pl.ds(i * BAND, BAND)], one.at[pl.ds(8 + i * BAND, BAND)], in_sem.at[i]
        )

    def store(buf, i):
        return pltpu.make_async_copy(
            buf.at[pl.ds(8 + i * CHUNK, CHUNK)], out_ref.at[pl.ds(i * CHUNK, CHUNK)], out_sem.at[i]
        )

    barrier = pltpu.get_barrier_semaphore()
    around = sorted((g for g in range(9) if g != 4), key=lambda g: -abs(AROUND[g][0]) - 2 * abs(AROUND[g][1]))
    for g in around:
        row, col = at(*AROUND[g])
        pl.semaphore_signal(barrier, inc=1, device_id={"row": row, "col": col}, device_id_type=MESH)
    for i in range(length // BAND):
        load(i).start()
    rim = jnp.zeros((8, width), F32)
    for buf in (one, two):
        buf[0:8, :] = rim
        buf[length + 8:length + 16, :] = rim

    turned = jnp.transpose(pos_ref[...])
    at_row = turned[0:CAP]
    start = jnp.clip(jnp.floor(at_row) - 7.0, 0.0, length - 16.0)
    block = jnp.floor(start * (1.0 / 32.0))
    rows48 = iota((48, n_dev), 0).astype(F32)
    for j in range(CAP):
        u = rows48 + 32.0 * block[j:j + 1]
        d = u - at_row[j:j + 1]
        inside = jnp.abs(u - (start[j:j + 1] + 7.5)) < 8.0
        bell = jnp.where(inside, jnp.exp2(d * d * (-0.5 * log2e)), 0.0).astype(BF16)
        here = slice(j * n_dev, (j + 1) * n_dev)
        low_part[:, here] = bell[0:32]
        high_part[:, here] = jnp.concatenate([bell[32:48], jnp.zeros((16, n_dev), BF16)], axis=0)
        place[:, here] = jnp.broadcast_to(block[j:j + 1], (32, n_dev)).astype(BF16)

    all_pos = pos_ref[...]
    at_col = pltpu.roll(all_pos, 128 - CAP, 1)
    middle = jnp.clip(jnp.floor(at_col) - 7.0, 0.0, width - 16.0) + 7.5
    v = iota((1, width), 1).astype(F32)

    def some_columns(i, carry):
        p, m = carry
        for k in range(4):
            d = v - p[:, k:k + 1]
            inside = jnp.abs(v - m[:, k:k + 1]) < 8.0
            bell = jnp.where(inside, jnp.exp2(d * d * (-0.5 * log2e)), 0.0)
            bell_col[pl.ds(pl.multiple_of((i * 4 + k) * n_dev, n_dev), n_dev), :] = bell.astype(BF16)
        return pltpu.roll(p, 124, 1), pltpu.roll(m, 124, 1)

    lax.fori_loop(0, CAP // 4, some_columns, (at_col, middle))

    def build(dst, band):
        for sub in range(BAND // 32):
            block_id = (band * (BAND // 32) + sub).astype(F32)
            first = place[...] == jnp.full((32, n_slot), block_id, F32).astype(BF16)
            second = place[...] == jnp.full((32, n_slot), block_id - 1.0, F32).astype(BF16)
            zero = jnp.zeros((32, n_slot), BF16)
            dst[sub * 32:(sub + 1) * 32, :] = jnp.where(
                first, low_part[...], jnp.where(second, high_part[...], zero)
            )

    def product(src, band):
        load(band).wait()
        here = pl.ds(pl.multiple_of(8 + band * BAND, 8), BAND)
        one[here, :] = one[here, :] + nn_dot(src[...], bell_col[...])

    build(left_sel, jnp.int32(0))

    def two_bands(i, carry):
        build(right_sel, 2 * i + 1)
        product(left_sel, 2 * i)
        build(left_sel, jnp.minimum(2 * i + 2, length // BAND - 1))
        product(right_sel, 2 * i + 1)
        return carry

    lax.fori_loop(0, length // BAND // 2, two_bands, 0)

    top_s[...] = one[8:16, :]
    bottom_s[...] = one[length:length + 8, :]
    keep_top[...] = one[8:24, :]
    keep_bottom[...] = one[length - 8:length + 8, :]
    lane = iota((1, 128), 1)
    for i in range(length // 128):
        here = slice(8 + i * 128, 8 + (i + 1) * 128)
        tile = jnp.transpose(jnp.where(lane < 64, one[here, 0:128], one[here, width - 128:width]))
        west_s[:, i * 128:(i + 1) * 128] = tile[0:8]
        east_s[:, i * 128:(i + 1) * 128] = tile[120:128]

    pl.semaphore_wait(barrier, 8)
    first = (slice(None), pl.ds(0, 128))
    last = (slice(None), pl.ds(length - 128, 128))
    inner = (slice(None), pl.ds(128, length))
    above = (slice(None), pl.ds(0, 128))
    below = (slice(None), pl.ds(length + 128, 128))
    plan = {
        (-1, 0): (top_s, down_r),
        (1, 0): (bottom_s, up_r),
        (0, -1): (west_s, east_r.at[inner]),
        (0, 1): (east_s, west_r.at[inner]),
        (-1, -1): (west_s.at[first], east_r.at[below]),
        (-1, 1): (east_s.at[first], west_r.at[below]),
        (1, -1): (west_s.at[last], east_r.at[above]),
        (1, 1): (east_s.at[last], west_r.at[above]),
    }
    copies = []
    for g in around:
        src, dst = plan[AROUND[g]]
        row, col = at(*AROUND[g])
        copy = remote(src, dst, ss.at[g], rs.at[g], row, col)
        copy.start()
        copies.append(copy)

    def summed(src, begin, n):
        window = src[pl.ds(pl.multiple_of(begin - 8, 8), n + 16), :]
        centre = window[8:8 + n]
        return (
            (centre + window[7:7 + n]) + (window[9:9 + n] + pltpu.roll(centre, 1, 1)) + pltpu.roll(centre, width - 1, 1)
        )

    for src, dst in ((one, two), (two, one), (one, two)):

        def strip(i, carry, src=src, dst=dst):
            begin = pl.multiple_of(8 + i * CHUNK, 8)
            dst[pl.ds(begin, CHUNK), :] = summed(src, begin, CHUNK)
            return carry

        lax.fori_loop(0, n_chunk, strip, 0)

    for copy in copies:
        copy.wait_recv()
    not_first_row = (me_r > 0).astype(F32)
    not_last_row = (me_r < n_row - 1).astype(F32)
    not_first_col = (me_c > 0).astype(F32)
    not_last_col = (me_c < n_col - 1).astype(F32)
    scale = 0.2 ** STEPS

    def cross(t):
        n, m = t.shape
        return (t + pltpu.roll(t, 1, 0)) + (pltpu.roll(t, n - 1, 0) + pltpu.roll(t, 1, 1)) + pltpu.roll(t, m - 1, 1)

    pad = jnp.zeros((120, 128), F32)
    corners = []
    for halo, order in ((up_r, 0), (down_r, 1)):
        for part in (halo[:, 0:128], halo[:, width - 128:width]):
            corners.append(jnp.transpose(jnp.concatenate([pad, part] if order == 0 else [part, pad], axis=0)))
    own_west = jnp.concatenate([corners[0][0:8], west_s[...], corners[2][0:8]], axis=1)
    own_east = jnp.concatenate([corners[1][120:128], east_s[...], corners[3][120:128]], axis=1)
    t = jnp.concatenate([west_r[...], own_west, own_east, east_r[...]], axis=0)
    down32 = iota((32, 1), 0)
    along = iota((1, length + 256), 1)
    mask = jnp.where(down32 < 8, not_first_col, jnp.where(down32 >= 24, not_last_col, 1.0)) * jnp.where(
        along < 128, jnp.where(along >= 120, not_first_row, 0.0),
        jnp.where(along >= length + 128, jnp.where(along < length + 136, not_last_row, 0.0), 1.0),
    )
    t = t * mask
    for step in range(STEPS):
        t = cross(t)
        if step < STEPS - 1:
            t = t * mask
    side[...] = t * scale

    def rim_rows(halo, kept, keep, at_top):
        r = jnp.concatenate([halo * keep, kept] if at_top else [kept, halo * keep], axis=0)
        near = iota((24, 1), 0)
        flag = jnp.where((near < 8) if at_top else (near >= 16), keep, 1.0)
        for step in range(STEPS):
            r = cross(r)
            if step < STEPS - 1:
                r = r * flag
        return (r[8:16] if at_top else r[8:16]) * scale

    zero112 = jnp.zeros((112, 128), F32)

    def side_tile(i):
        here = pl.ds(pl.multiple_of((i + 1) * 128, 128), 128)
        return jnp.transpose(jnp.concatenate([side[8:16, here], zero112, side[16:24, here]], axis=0))

    def finish(i, carry):
        begin = pl.multiple_of(8 + i * CHUNK, 8)
        total = summed(two, begin, CHUNK) * scale
        for h in range(CHUNK // 128):
            rows_h = slice(h * 128, (h + 1) * 128)
            tile = side_tile(i * (CHUNK // 128) + h)
            here = pl.ds(pl.multiple_of(begin + h * 128, 8), 128)
            one[here, 0:128] = jnp.where(lane < 4, tile, total[rows_h, 0:128])
            one[here, 128:width - 128] = total[rows_h, 128:width - 128]
            one[here, width - 128:width] = jnp.where(lane >= 124, tile, total[rows_h, width - 128:width])
        return carry

    def start_store(i, carry):
        finish(i, carry)
        store(one, i).start()
        return carry

    lax.fori_loop(1, n_chunk - 1, start_store, 0)
    for i, at_row8, rim8 in (
        (0, 8, rim_rows(up_r[...], keep_top[...], not_first_row, True)),
        (n_chunk - 1, length, rim_rows(down_r[...], keep_bottom[...], not_last_row, False)),
    ):
        finish(jnp.int32(i), 0)
        one[at_row8:at_row8 + 8, 0:128] = jnp.where(lane < 4, one[at_row8:at_row8 + 8, 0:128], rim8[:, 0:128])
        one[at_row8:at_row8 + 8, 128:width - 128] = rim8[:, 128:width - 128]
        one[at_row8:at_row8 + 8, width - 128:width] = jnp.where(
            lane >= 124, one[at_row8:at_row8 + 8, width - 128:width], rim8[:, width - 128:width]
        )
        store(one, i).start()

    def finish_store(i, carry):
        store(one, i).wait()
        return carry

    lax.fori_loop(0, n_chunk, finish_store, 0)
    for copy in copies:
        copy.wait_send()


CHUNK = 256
BAND = 256


def spread_and_diffuse(n_row, n_col, positions, macro):
    length, width = macro.shape
    n_slot = n_row * n_col * CAP
    any_space = pl.BlockSpec(memory_space=pl.ANY)
    dma = pltpu.SemaphoreType.DMA
    return pl.pallas_call(
        functools.partial(grid_kernel, n_row, n_col),
        name="spread_and_diffuse",
        out_shape=jax.ShapeDtypeStruct(macro.shape, F32),
        in_specs=[pl.BlockSpec(memory_space=pltpu.VMEM), any_space],
        out_specs=any_space,
        scratch_shapes=[
            pltpu.VMEM((length + 16, width), F32),
            pltpu.VMEM((length + 16, width), F32),
            pltpu.VMEM((n_slot, width), BF16),
            pltpu.VMEM((BAND, n_slot), BF16),
            pltpu.VMEM((BAND, n_slot), BF16),
            pltpu.VMEM((32, n_slot), BF16),
            pltpu.VMEM((32, n_slot), BF16),
            pltpu.VMEM((32, n_slot), BF16),
            pltpu.VMEM((8, width), F32),
            pltpu.VMEM((8, width), F32),
            pltpu.VMEM((8, length), F32),
            pltpu.VMEM((8, length), F32),
            pltpu.VMEM((8, width), F32),
            pltpu.VMEM((8, width), F32),
            pltpu.VMEM((8, length + 256), F32),
            pltpu.VMEM((8, length + 256), F32),
            pltpu.VMEM((16, width), F32),
            pltpu.VMEM((16, width), F32),
            pltpu.VMEM((32, length + 256), F32),
            dma((length // BAND,)),
            dma((length // CHUNK,)),
            dma((9,)),
            dma((9,)),
        ],
        compiler_params=pltpu.CompilerParams(
            collective_id=1, has_side_effects=True, vmem_limit_bytes=48 * 2**20
        ),
        cost_estimate=pl.CostEstimate(flops=10**10, bytes_accessed=8 * length * width, transcendentals=0),
    )(positions, macro)


def per_device(right_side, anchor, tiles, neighbours, owners, row_offset, col_offset, macro_density):
    n_row, n_col = lax.axis_size("row"), lax.axis_size("col")
    solution, arrived = solve(
        n_row, n_col, neighbours.T, right_side, anchor, owners.T, row_offset, col_offset, tiles,
    )
    return solution, spread_and_diffuse(n_row, n_col, arrived, macro_density)


def solution(mesh):
    blocks = P(("row", "col"))
    return jax.shard_map(
        per_device,
        mesh=mesh,
        in_specs=(
            P(("row", "col"), None, None),
            P(("row", "col"), None),
            P(("row", "col"), None, None, None),
            P(("row", "col"), None),
            P(("row", "col"), None),
            blocks,
            blocks,
            P("row", "col"),
        ),
        out_specs=(P(("row", "col"), None, None), P("row", "col")),
        check_vma=False,
    )
```

```python
import functools

import jax
import jax.numpy as jnp
from jax import lax
from jax.experimental import pallas as pl
from jax.experimental.pallas import tpu as pltpu
from jax.sharding import PartitionSpec as P

MESH = pl.DeviceIdType.MESH
F32 = jnp.float32
BF16 = jnp.bfloat16
STEPS = 4
CAP = 32
NONE = -1000.0
AROUND = [(dr, dc) for dr in (-1, 0, 1) for dc in (-1, 0, 1)]


def nt_dot(a, b):
    return lax.dot_general(a, b, (((1,), (1,)), ((), ())), preferred_element_type=F32)


def nn_dot(a, b):
    return jnp.dot(a, b, preferred_element_type=F32)


def split3(x):
    hi = x.astype(BF16)
    rest = x - hi.astype(F32)
    mid = rest.astype(BF16)
    low = (rest - mid.astype(F32)).astype(BF16)
    return hi, mid, low


def iota(shape, dim):
    return lax.broadcasted_iota(jnp.int32, shape, dim)


def remote(src, dst, send, recv, row, col):
    return pltpu.make_async_remote_copy(
        src_ref=src, dst_ref=dst, send_sem=send, recv_sem=recv,
        device_id={"row": row, "col": col}, device_id_type=MESH,
    )


def solve_kernel(
    n_row, n_col,
    nbr_hbm, rhs_hbm, anchor_hbm, owner_hbm, roff_hbm, coff_hbm, tiles_ref,
    sol_ref, pos_ref,
    stage, thi, tlo, xbuf, sel, spread_sel, gath, terms, back, recv,
    ar_row, ar_col, own_hot, rank_sc, weight_sc, out_rows, mid_rows, end_rows, table_sc,
    own_sel, own_g, down_sc, sums_sc, far_sum, down_sum, nbr_sc, rhs_ref, anchor_ref, owner_ref, roff_ref, coff_ref, small_sem,
    tile_sem, fs, fr, bs, br, rs, rr, cs, cr, away1, got, away2, land, keep_sem,
):
    n_blk, fan, side, _ = thi.shape
    rows = 2 * n_blk
    q_own = n_blk * fan * 8
    q_all = q_own + n_blk * 8
    n_dev = n_row * n_col
    me_r = lax.axis_index("row")
    me_c = lax.axis_index("col")
    row_order = sorted(range(1, n_row), key=lambda d: -min(d, n_row - d))
    col_order = sorted(range(1, n_col), key=lambda d: -(min(d // 4, 4 - d // 4) + min(d % 4, 4 - d % 4)))
    around = sorted((g for g in range(9) if g != 4), key=lambda g: -abs(AROUND[g][0]) - 2 * abs(AROUND[g][1]))

    small = [
        pltpu.make_async_copy(src, dst, small_sem.at[i])
        for i, (src, dst) in enumerate((
            (rhs_hbm, rhs_ref), (owner_hbm, owner_ref), (nbr_hbm, nbr_sc),
            (anchor_hbm, anchor_ref), (roff_hbm, roff_ref), (coff_hbm, coff_ref),
        ))
    ]
    for copy in small:
        copy.start()
    for b in range(n_blk):
        pltpu.make_async_copy(tiles_ref.at[b], stage.at[b], tile_sem.at[b]).start()

    barrier = pltpu.get_barrier_semaphore()
    peers = [AROUND[g] for g in around if AROUND[g][0] and AROUND[g][1]]
    peers += [(0, d) for d in col_order] + [(d, 0) for d in row_order]
    for dr, dc in peers:
        pl.semaphore_signal(
            barrier, inc=1,
            device_id={"row": lax.rem(me_r + dr + n_row, n_row), "col": lax.rem(me_c + dc + n_col, n_col)},
            device_id_type=MESH,
        )

    own_lo = 4 * rows
    below = iota((side - 9 * rows, side), 0)
    for it in range(3):
        xbuf[it, 9 * rows:side, :] = jnp.where(below == 0, 1.0, 0.0)
    for copy in small[:2]:
        copy.wait()
    for b in range(n_blk):
        xbuf[0, own_lo + 2 * b:own_lo + 2 * b + 2, :] = rhs_ref[b]

    upper = (iota((side, side), 0) < iota((side, side), 1)).astype(F32).astype(BF16)
    count = jnp.zeros((n_dev, 1), F32)
    held = jnp.zeros((1, n_dev), F32)
    for b in range(n_blk):
        hot = (owner_ref[0:1, b * side:(b + 1) * side] == iota((n_dev, side), 0)).astype(F32)
        before = nn_dot(hot.astype(BF16), upper) + count
        rank_sc[b:b + 1, :] = jnp.sum(hot * before, axis=0, keepdims=True)
        count = count + jnp.sum(hot, axis=1, keepdims=True)
        turned = jnp.transpose(hot)
        own_hot[b] = turned.astype(BF16)
        held = held + jnp.sum(turned, axis=0, keepdims=True)

    ones_row = 9 * rows
    lane3 = iota((8, 3 * side), 1)
    part_row = iota((8, 1), 0)
    base_col = jnp.where(
        part_row < 6, (part_row // 2) * side + lax.rem(part_row, 2), jnp.where(part_row == 6, ones_row, -1)
    )
    moves = (part_row < 6).astype(jnp.int32)

    lane_own = iota((8, 4 * rows), 1)
    own_col = jnp.where(
        part_row < 6, (part_row // 2) * rows + lax.rem(part_row, 2), jnp.where(part_row == 6, 3 * rows, -1)
    )

    def select_row(q, slot):
        sel[q:q + 8, :] = (lane3 == base_col + moves * (2 * slot)).astype(F32).astype(BF16)

    for copy in small[2:]:
        copy.wait()
    for b in range(n_blk):
        for k in range(fan):
            named = nbr_sc[k, b]
            dev = named // n_blk
            slot = ((dev // n_col - me_r + 1) * 3 + (lax.rem(dev, n_col) - me_c + 1)) * n_blk + lax.rem(named, n_blk)
            select_row((b * fan + k) * 8, slot)
        select_row(q_own + b * 8, 4 * n_blk + b)
        own_sel[b * 8:(b + 1) * 8, :] = (lane_own == own_col + moves * (2 * b)).astype(F32).astype(BF16)
    sel_t = sel[:, 0:side].astype(F32) + sel[:, side:2 * side].astype(F32) + sel[:, 2 * side:].astype(F32)
    spread_sel[...] = jnp.transpose(jnp.concatenate([sel_t, jnp.zeros((384 - q_all, side), F32)], axis=0)).astype(BF16)
    terms[...] = jnp.zeros_like(terms)

    pl.semaphore_wait(barrier, len(peers))

    def x_rows(it, g):
        return xbuf.at[it, pl.ds(g * rows, rows)]

    pending = []

    def forward(it):
        for g in around:
            dr, dc = AROUND[g]
            copy = remote(
                x_rows(it, 4), x_rows(it, 8 - g), fs.at[it, g], fr.at[it, 8 - g],
                lax.rem(me_r + dr + n_row, n_row), lax.rem(me_c + dc + n_col, n_col),
            )
            copy.start()
            pending.append(copy)

    def forward_wait(it):
        for g in around:
            remote(x_rows(it, 4), x_rows(it, g), fs.at[it, g], fr.at[it, g], me_r, me_c).wait_recv()

    def backward(it):
        for g in around:
            dr, dc = AROUND[g]
            copy = remote(
                back.at[it, pl.ds(g * rows, rows)], recv.at[it, 8 - g], bs.at[it, g], br.at[it, 8 - g],
                lax.rem(me_r + dr + n_row, n_row), lax.rem(me_c + dc + n_col, n_col),
            )
            copy.start()
            pending.append(copy)

    def backward_wait(it):
        for g in around:
            remote(back.at[it, pl.ds(g * rows, rows)], recv.at[it, g], bs.at[it, g], br.at[it, g], me_r, me_c).wait_recv()

    forward(0)

    def split_block(b, carry):
        pltpu.make_async_copy(tiles_ref.at[b], stage.at[b], tile_sem.at[b]).wait()
        for k in range(fan):
            t = stage[b, k]
            hi = t.astype(BF16)
            thi[b, k] = hi
            tlo[b, k] = (t - hi.astype(F32)).astype(BF16)
        return carry

    lax.fori_loop(0, n_blk, split_block, 0)

    first_row = jnp.where(iota((rows, side), 0) == 0, 1.0, 0.0).astype(BF16)

    def grouped(c, v):
        return (v.reshape(q_own // 8, 8, side) * c[None]).reshape(q_own, side)

    def over_parts(v):
        return v + pltpu.roll(v, q_own - 2, 0) + pltpu.roll(v, q_own - 4, 0)

    def own_products(it, own):
        own_g[...] = nn_dot(own_sel[...], jnp.concatenate(split3(own) + (first_row,), axis=0))

        def one_block(b, carry):
            own_b = own_g[pl.ds(pl.multiple_of(b * 8, 8), 8), :].astype(BF16)
            for k in range(fan):
                q = pl.multiple_of((b * fan + k) * 8, 8)
                down = nn_dot(own_b, thi[b, k]) + nn_dot(own_b, tlo[b, k])
                down_sc[pl.ds(q, 8), :] = down
                if it == 0:
                    sums_sc[pl.ds(q, 8), :] = jnp.broadcast_to(down[6:7, :], (8, side))
            return carry

        lax.fori_loop(0, n_blk, one_block, 0, unroll=2)
        down_sum[it] = over_parts(down_sc[...])

    def gather_far(it):
        parts = jnp.concatenate(split3(xbuf[it]), axis=0)
        gath[...] = nn_dot(sel[0:q_own, :], parts)

    def apply(it, after_forward=None):
        forward_wait(it)
        if after_forward is not None:
            after_forward()
        gather_far(it)

        def one_block(b, carry):
            total = jnp.zeros((8, side), F32)
            for k in range(fan):
                q = pl.multiple_of((b * fan + k) * 8, 8)
                far_b = gath[pl.ds(q, 8), :].astype(BF16)
                total = total + nt_dot(far_b, thi[b, k]) + nt_dot(far_b, tlo[b, k])
            weight = total[6:7, :] + anchor_ref[pl.ds(b, 1), :]
            if it == 0:
                weight_sc[pl.ds(b, 1), :] = weight
            own = own_g[pl.ds(pl.multiple_of(b * 8, 8), 8), :]
            terms[pl.ds(pl.multiple_of(q_own + b * 8, 8), 8), :] = weight * own - total
            return carry

        lax.fori_loop(0, n_blk, one_block, 0, unroll=2)
        terms[0:q_own, :] = sums_sc[...] * gath[...] - down_sc[...]
        hi, mid, low = split3(terms[...])
        where_to = spread_sel[0:9 * rows, :]
        back[it] = nn_dot(where_to, hi) + nn_dot(where_to, mid) + nn_dot(where_to, low)
        backward(it)
        far_sum[it] = over_parts(gath[...])

    def applied(it):
        backward_wait(it)
        image = back[it, own_lo:own_lo + rows, :]
        for g in range(9):
            if g != 4:
                image = image + recv[it, g]
        return image

    def dots_start(it, pairs, more=None):
        lane = iota((8, 128), 1)
        tile = jnp.zeros((8, 128), F32)
        for d, (a, b) in enumerate(pairs):
            e = a * b
            e = e[0:8] + e[8:16]
            if d == 0 and more is not None:
                e = e + more
            tile = jnp.where(lane == d, jnp.sum(e, axis=1, keepdims=True), tile)
        ar_row[it, me_r] = tile
        for d in row_order:
            copy = remote(
                ar_row.at[it, me_r], ar_row.at[it, me_r], rs.at[it, d], rr.at[it, me_r],
                lax.rem(me_r + d, n_row), me_c,
            )
            copy.start()
            pending.append(copy)

    def dots_middle(it):
        for d in row_order:
            far = lax.rem(me_r + d, n_row)
            remote(ar_row.at[it, far], ar_row.at[it, far], rs.at[it, d], rr.at[it, far], me_r, me_c).wait_recv()
        ar_col[it, me_c] = jnp.sum(ar_row[it], axis=0)
        for d in col_order:
            copy = remote(
                ar_col.at[it, me_c], ar_col.at[it, me_c], cs.at[it, d], cr.at[it, me_c],
                me_r, lax.rem(me_c + d, n_col),
            )
            copy.start()
            pending.append(copy)

    def dots_end(it, n):
        for d in col_order:
            far = lax.rem(me_c + d, n_col)
            remote(ar_col.at[it, far], ar_col.at[it, far], cs.at[it, d], cr.at[it, far], me_r, me_c).wait_recv()
        t = jnp.sum(ar_col[it], axis=0)
        t = t + pltpu.roll(t, 4, 0)
        t = t + pltpu.roll(t, 2, 0)
        return [t[:, d:d + 1] for d in range(n)]

    def times(c, v):
        return jnp.concatenate([c] * (v.shape[0] // 8), axis=0) * v

    rank_of = iota((CAP, side), 0)

    def by_owner(values_of):
        total = None
        for b in range(n_blk):
            mine = rank_of == rank_sc[b:b + 1, :].astype(jnp.int32)
            placed = jnp.concatenate([jnp.where(mine, v, 0.0) for v in values_of(b)], axis=0)
            for part in split3(placed):
                more = nn_dot(part, own_hot[b])
                total = more if total is None else total + more
        return total

    def both(v):
        return lambda b: [v[2 * b:2 * b + 1, :], v[2 * b + 1:2 * b + 2, :]]

    def offsets(b):
        return [r[b * side:(b + 1) * side].reshape(1, side).astype(F32) for r in (roff_ref, coff_ref)]

    r0 = xbuf[0, own_lo:own_lo + rows, :]
    own_products(0, r0)
    apply(0)
    table_r0 = by_owner(both(r0))
    table_off = by_owner(offsets)
    w0 = applied(0)
    xbuf[1, own_lo:own_lo + rows, :] = w0
    forward(1)
    dots_start(0, [(r0, r0), (r0, w0)])
    own_products(1, w0)
    apply(1, lambda: dots_middle(0))
    table_w0 = by_owner(both(w0))
    gamma0, curve0 = dots_end(0, 2)
    alpha0 = gamma0 / curve0
    z0 = applied(1)
    w1 = w0 - times(alpha0, z0)
    xbuf[2, own_lo:own_lo + rows, :] = w1
    r1 = r0 - times(alpha0, w0)
    dots_start(1, [(r1, r1), (r1, w1), (r1, w0)])
    forward(2)

    table = jnp.concatenate([table_r0, table_w0, by_owner(both(w1)), table_off], axis=0)
    empty = iota((CAP, n_dev), 0).astype(F32) >= held
    table = jnp.concatenate(
        [table[0:6 * CAP], jnp.where(empty, NONE, table[6 * CAP:7 * CAP]), table[7 * CAP:]], axis=0
    )
    table = jnp.transpose(table)
    for o in range(n_dev):
        out_rows[o // n_col, o % n_col] = table[o:o + 1, :]
    keep = pltpu.make_async_copy(out_rows.at[me_r], mid_rows.at[:, me_r], keep_sem.at[0])
    keep.start()
    for d in row_order:
        far = lax.rem(me_r + d, n_row)
        copy = remote(out_rows.at[far], mid_rows.at[:, me_r], away1.at[d], got.at[me_r], far, me_c)
        copy.start()
        pending.append(copy)

    dots_middle(1)

    keep.wait()
    for d in row_order:
        far = lax.rem(me_r + d, n_row)
        remote(out_rows.at[far], mid_rows.at[:, far], away1.at[d], got.at[far], me_r, me_c).wait_recv()
    keep2 = pltpu.make_async_copy(mid_rows.at[me_c], end_rows.at[me_c], keep_sem.at[1])
    keep2.start()
    for d in col_order:
        far = lax.rem(me_c + d, n_col)
        copy = remote(mid_rows.at[far], end_rows.at[me_c], away2.at[d], land.at[me_c], me_r, far)
        copy.start()
        pending.append(copy)

    own_products(2, w1)
    forward_wait(2)
    gather_far(2)
    far_r1 = far_sum[0] - grouped(alpha0, far_sum[1])
    down_r1 = down_sum[0] - grouped(alpha0, down_sum[1])
    far_w1 = over_parts(gath[...])
    gamma1, r1w1, r1w0 = dots_end(1, 3)
    beta0 = gamma1 / gamma0
    curve1 = r1w1 + 2.0 * beta0 * r1w0 + beta0 * beta0 * curve0
    alpha1 = gamma1 / curve1
    p1 = r1 + times(beta0, r0)
    s1 = w1 + times(beta0, w0)
    r2 = r1 - times(alpha1, s1)

    far_r2 = far_r1 - grouped(alpha1, far_w1 + grouped(beta0, far_sum[1]))
    down_r2 = down_r1 - grouped(alpha1, down_sum[2] + grouped(beta0, down_sum[1]))
    cross = far_r2 * (sums_sc[...] * far_r2 - 2.0 * down_r2)
    cross = jnp.sum(cross.reshape(q_own // 8, 8, side), axis=0)
    cross = jnp.where(iota((8, side), 0) < 2, cross, 0.0)
    weights = weight_sc[...]
    weights = jnp.concatenate([weights[b:b + 1] for b in range(n_blk) for _ in (0, 1)], axis=0)
    dots_start(2, [(r2, weights * r2), (r2, r2), (r2, s1)], more=cross)

    keep2.wait()
    for d in col_order:
        far = lax.rem(me_c + d, n_col)
        remote(mid_rows.at[far], end_rows.at[far], away2.at[d], land.at[far], me_r, me_c).wait_recv()
    dots_middle(2)
    for o in range(n_dev):
        table_sc[o:o + 1, :] = end_rows[o // n_row, o % n_row]
    curve_r2, gamma2, r2s1 = dots_end(2, 3)
    beta1 = gamma2 / gamma1
    curve2 = curve_r2 + 2.0 * beta1 * r2s1 + beta1 * beta1 * curve1
    alpha2 = gamma2 / curve2

    of_b = alpha0 + alpha1 * (1.0 + beta0) + alpha2 * (1.0 + beta1 * (1.0 + beta0))
    of_w0 = -alpha1 * alpha0 - alpha2 * (alpha0 + alpha1 * beta0 + beta1 * alpha0)
    of_w1 = -alpha2 * alpha1
    lane = iota((1, 128), 1)

    def by_lane(first, second):
        return jnp.where(
            lane < CAP, first[0:1], jnp.where(lane < 2 * CAP, first[1:2], jnp.where(lane < 3 * CAP, second[0:1], second[1:2]))
        )

    near = table_sc[:, 0:128] * by_lane(of_b, of_w0)
    far = table_sc[:, 128:256]
    moved = near + pltpu.roll(near, 64, 1) + far * by_lane(of_w1, of_w1)
    pos_ref[...] = pltpu.roll(far, 64, 1) + 3.0 * jnp.tanh(moved)

    x = times(alpha0, r0) + times(alpha1, p1) + times(alpha2, r2 + times(beta1, p1))
    for b in range(n_blk):
        sol_ref[b] = x[2 * b:2 * b + 2, :]
    for copy in pending:
        copy.wait_send()


def solve(n_row, n_col, neighbours, right_side, anchor, owners, row_offset, col_offset, tiles):
    n_blk, fan, side, _ = tiles.shape
    rows = 2 * n_blk
    n_dev = n_row * n_col
    q_all = n_blk * fan * 8 + n_blk * 8
    vmem = pl.BlockSpec(memory_space=pltpu.VMEM)
    dma = pltpu.SemaphoreType.DMA
    return pl.pallas_call(
        functools.partial(solve_kernel, n_row, n_col),
        name="solve_and_route",
        out_shape=(
            jax.ShapeDtypeStruct(right_side.shape, F32),
            jax.ShapeDtypeStruct((n_dev, 128), F32),
        ),
        in_specs=[pl.BlockSpec(memory_space=pltpu.HBM)] * 7,
        out_specs=(vmem, vmem),
        scratch_shapes=[
            pltpu.VMEM(tiles.shape, F32),
            pltpu.VMEM(tiles.shape, BF16),
            pltpu.VMEM(tiles.shape, BF16),
            pltpu.VMEM((3, side, side), F32),
            pltpu.VMEM((q_all, 3 * side), BF16),
            pltpu.VMEM((side, 384), BF16),
            pltpu.VMEM((8 * n_blk * fan, side), F32),
            pltpu.VMEM((384, side), F32),
            pltpu.VMEM((2, 9 * rows, side), F32),
            pltpu.VMEM((2, 9, rows, side), F32),
            pltpu.VMEM((3, n_row, 8, 128), F32),
            pltpu.VMEM((3, n_col, 8, 128), F32),
            pltpu.VMEM((n_blk, side, n_dev), BF16),
            pltpu.VMEM((n_blk, side), F32),
            pltpu.VMEM((n_blk, side), F32),
            pltpu.VMEM((n_row, n_col, 1, 8 * CAP), F32),
            pltpu.VMEM((n_col, n_row, 1, 8 * CAP), F32),
            pltpu.VMEM((n_col, n_row, 1, 8 * CAP), F32),
            pltpu.VMEM((n_dev, 8 * CAP), F32),
            pltpu.VMEM((8 * n_blk, 4 * rows), BF16),
            pltpu.VMEM((8 * n_blk, side), F32),
            pltpu.VMEM((8 * n_blk * fan, side), F32),
            pltpu.VMEM((8 * n_blk * fan, side), F32),
            pltpu.VMEM((2, 8 * n_blk * fan, side), F32),
            pltpu.VMEM((3, 8 * n_blk * fan, side), F32),
            pltpu.SMEM((fan, n_blk), jnp.int32),
            pltpu.VMEM(right_side.shape, F32),
            pltpu.VMEM(anchor.shape, F32),
            pltpu.VMEM(owners.shape, jnp.int32),
            pltpu.VMEM(row_offset.shape, jnp.int32),
            pltpu.VMEM(col_offset.shape, jnp.int32),
            dma((6,)),
            dma((n_blk,)),
            dma((3, 9)), dma((3, 9)), dma((3, 9)), dma((3, 9)),
            dma((3, n_row)), dma((3, n_row)), dma((3, n_col)), dma((3, n_col)),
            dma((n_row,)), dma((n_row,)), dma((n_col,)), dma((n_col,)), dma((2,)),
        ],
        compiler_params=pltpu.CompilerParams(
            collective_id=0, has_side_effects=True, vmem_limit_bytes=63480000
        ),
        cost_estimate=pl.CostEstimate(flops=10**9, bytes_accessed=2**23, transcendentals=0),
    )(neighbours, right_side, anchor, owners, row_offset, col_offset, tiles)


def grid_kernel(
    n_row, n_col,
    pos_ref, macro_ref, two, side, rims,
    one, bell_col, left_sel, right_sel, low_part, high_part, place,
    top_s, bottom_s, west_s, east_s, up_r, down_r, west_r, east_r, keep_top, keep_bottom,
    in_sem, ss, rs,
):
    length, width = macro_ref.shape
    n_dev = n_row * n_col
    n_slot = bell_col.shape[0]
    n_chunk = length // CHUNK
    me_r = lax.axis_index("row")
    me_c = lax.axis_index("col")
    log2e = 1.4426950408889634

    def at(dr, dc):
        return lax.rem(me_r + dr + n_row, n_row), lax.rem(me_c + dc + n_col, n_col)

    def load(i):
        return pltpu.make_async_copy(
            macro_ref.at[pl.ds(i * BAND, BAND)], one.at[pl.ds(8 + i * BAND, BAND)], in_sem.at[i]
        )

    barrier = pltpu.get_barrier_semaphore()
    around = sorted((g for g in range(9) if g != 4), key=lambda g: -abs(AROUND[g][0]) - 2 * abs(AROUND[g][1]))
    for g in around:
        row, col = at(*AROUND[g])
        pl.semaphore_signal(barrier, inc=1, device_id={"row": row, "col": col}, device_id_type=MESH)
    for i in range(length // BAND):
        load(i).start()
    rim = jnp.zeros((8, width), F32)
    for buf in (one, two):
        buf[0:8, :] = rim
        buf[length + 8:length + 16, :] = rim

    turned = jnp.transpose(pos_ref[...])
    at_row = turned[0:CAP]
    start = jnp.clip(jnp.floor(at_row) - 7.0, 0.0, length - 16.0)
    block = jnp.floor(start * (1.0 / 32.0))
    rows48 = iota((48, n_dev), 0).astype(F32)
    for j in range(CAP):
        u = rows48 + 32.0 * block[j:j + 1]
        d = u - at_row[j:j + 1]
        inside = jnp.abs(u - (start[j:j + 1] + 7.5)) < 8.0
        bell = jnp.where(inside, jnp.exp2(d * d * (-0.5 * log2e)), 0.0).astype(BF16)
        here = slice(j * n_dev, (j + 1) * n_dev)
        low_part[:, here] = bell[0:32]
        high_part[:, here] = jnp.concatenate([bell[32:48], jnp.zeros((16, n_dev), BF16)], axis=0)
        place[:, here] = jnp.broadcast_to(block[j:j + 1], (32, n_dev)).astype(BF16)

    all_pos = pos_ref[...]
    at_col = pltpu.roll(all_pos, 128 - CAP, 1)
    middle = jnp.clip(jnp.floor(at_col) - 7.0, 0.0, width - 16.0) + 7.5
    v = iota((1, width), 1).astype(F32)

    def some_columns(i, carry):
        p, m = carry
        for k in range(4):
            d = v - p[:, k:k + 1]
            inside = jnp.abs(v - m[:, k:k + 1]) < 8.0
            bell = jnp.where(inside, jnp.exp2(d * d * (-0.5 * log2e)), 0.0)
            bell_col[pl.ds(pl.multiple_of((i * 4 + k) * n_dev, n_dev), n_dev), :] = bell.astype(BF16)
        return pltpu.roll(p, 124, 1), pltpu.roll(m, 124, 1)

    lax.fori_loop(0, CAP // 4, some_columns, (at_col, middle))

    def build(dst, band):
        for sub in range(BAND // 32):
            block_id = (band * (BAND // 32) + sub).astype(F32)
            first = place[...] == jnp.full((32, n_slot), block_id, F32).astype(BF16)
            second = place[...] == jnp.full((32, n_slot), block_id - 1.0, F32).astype(BF16)
            zero = jnp.zeros((32, n_slot), BF16)
            dst[sub * 32:(sub + 1) * 32, :] = jnp.where(
                first, low_part[...], jnp.where(second, high_part[...], zero)
            )

    def product(src, band):
        load(band).wait()
        here = pl.ds(pl.multiple_of(8 + band * BAND, 8), BAND)
        one[here, :] = one[here, :] + nn_dot(src[...], bell_col[...])

    build(left_sel, jnp.int32(0))

    def two_bands(i, carry):
        build(right_sel, 2 * i + 1)
        product(left_sel, 2 * i)
        build(left_sel, jnp.minimum(2 * i + 2, length // BAND - 1))
        product(right_sel, 2 * i + 1)
        return carry

    lax.fori_loop(0, length // BAND // 2, two_bands, 0)

    top_s[...] = one[8:16, :]
    bottom_s[...] = one[length:length + 8, :]
    keep_top[...] = one[8:24, :]
    keep_bottom[...] = one[length - 8:length + 8, :]
    lane = iota((1, 128), 1)
    for i in range(length // 128):
        here = slice(8 + i * 128, 8 + (i + 1) * 128)
        tile = jnp.transpose(jnp.where(lane < 64, one[here, 0:128], one[here, width - 128:width]))
        west_s[:, i * 128:(i + 1) * 128] = tile[0:8]
        east_s[:, i * 128:(i + 1) * 128] = tile[120:128]

    pl.semaphore_wait(barrier, 8)
    first = (slice(None), pl.ds(0, 128))
    last = (slice(None), pl.ds(length - 128, 128))
    inner = (slice(None), pl.ds(128, length))
    above = (slice(None), pl.ds(0, 128))
    below = (slice(None), pl.ds(length + 128, 128))
    plan = {
        (-1, 0): (top_s, down_r),
        (1, 0): (bottom_s, up_r),
        (0, -1): (west_s, east_r.at[inner]),
        (0, 1): (east_s, west_r.at[inner]),
        (-1, -1): (west_s.at[first], east_r.at[below]),
        (-1, 1): (east_s.at[first], west_r.at[below]),
        (1, -1): (west_s.at[last], east_r.at[above]),
        (1, 1): (east_s.at[last], west_r.at[above]),
    }
    copies = []
    for g in around:
        src, dst = plan[AROUND[g]]
        row, col = at(*AROUND[g])
        copy = remote(src, dst, ss.at[g], rs.at[g], row, col)
        copy.start()
        copies.append(copy)

    for src, dst in ((one, two), (two, one), (one, two)):

        def strip(i, carry, src=src, dst=dst):
            begin = pl.multiple_of(8 + i * CHUNK, 8)
            dst[pl.ds(begin, CHUNK), :] = summed(src, begin, CHUNK)
            return carry

        lax.fori_loop(0, n_chunk, strip, 0)

    for copy in copies:
        copy.wait_recv()
    not_first_row = (me_r > 0).astype(F32)
    not_last_row = (me_r < n_row - 1).astype(F32)
    not_first_col = (me_c > 0).astype(F32)
    not_last_col = (me_c < n_col - 1).astype(F32)
    scale = 0.2 ** STEPS

    def cross(t):
        n, m = t.shape
        return (t + pltpu.roll(t, 1, 0)) + (pltpu.roll(t, n - 1, 0) + pltpu.roll(t, 1, 1)) + pltpu.roll(t, m - 1, 1)

    pad = jnp.zeros((120, 128), F32)
    corners = []
    for halo, order in ((up_r, 0), (down_r, 1)):
        for part in (halo[:, 0:128], halo[:, width - 128:width]):
            corners.append(jnp.transpose(jnp.concatenate([pad, part] if order == 0 else [part, pad], axis=0)))
    own_west = jnp.concatenate([corners[0][0:8], west_s[...], corners[2][0:8]], axis=1)
    own_east = jnp.concatenate([corners[1][120:128], east_s[...], corners[3][120:128]], axis=1)
    t = jnp.concatenate([west_r[...], own_west, own_east, east_r[...]], axis=0)
    down32 = iota((32, 1), 0)
    along = iota((1, length + 256), 1)
    mask = jnp.where(down32 < 8, not_first_col, jnp.where(down32 >= 24, not_last_col, 1.0)) * jnp.where(
        along < 128, jnp.where(along >= 120, not_first_row, 0.0),
        jnp.where(along >= length + 128, jnp.where(along < length + 136, not_last_row, 0.0), 1.0),
    )
    t = t * mask
    for step in range(STEPS):
        t = cross(t)
        if step < STEPS - 1:
            t = t * mask
    side[...] = t * scale

    def rim_rows(halo, kept, keep, at_top):
        r = jnp.concatenate([halo * keep, kept] if at_top else [kept, halo * keep], axis=0)
        near = iota((24, 1), 0)
        flag = jnp.where((near < 8) if at_top else (near >= 16), keep, 1.0)
        for step in range(STEPS):
            r = cross(r)
            if step < STEPS - 1:
                r = r * flag
        return (r[8:16] if at_top else r[8:16]) * scale

    rims[0:8, :] = rim_rows(up_r[...], keep_top[...], not_first_row, True)
    rims[8:16, :] = rim_rows(down_r[...], keep_bottom[...], not_last_row, False)
    for copy in copies:
        copy.wait_send()


def summed(src, begin, n):
    width = src.shape[1]
    window = src[pl.ds(pl.multiple_of(begin - 8, 8), n + 16), :]
    centre = window[8:8 + n]
    return (
        (centre + window[7:7 + n]) + (window[9:9 + n] + pltpu.roll(centre, 1, 1)) + pltpu.roll(centre, width - 1, 1)
    )


def last_step_kernel(two, side, rims, out_ref, one, out_sem):
    length, width = out_ref.shape
    n_chunk = length // CHUNK
    scale = 0.2 ** STEPS
    lane = iota((1, 128), 1)

    def store(i):
        here = pl.ds(pl.multiple_of(i * CHUNK, CHUNK), CHUNK)
        return pltpu.make_async_copy(one.at[here], out_ref.at[here], out_sem.at[i])

    zero112 = jnp.zeros((112, 128), F32)

    def finish(i, carry):
        total = summed(two, pl.multiple_of(8 + i * CHUNK, 8), CHUNK) * scale
        for h in range(CHUNK // 128):
            rows_h = slice(h * 128, (h + 1) * 128)
            at_lane = pl.ds(pl.multiple_of(i * CHUNK + (h + 1) * 128, 128), 128)
            tile = jnp.transpose(jnp.concatenate([side[8:16, at_lane], zero112, side[16:24, at_lane]], axis=0))
            here = pl.ds(pl.multiple_of(i * CHUNK + h * 128, 8), 128)
            one[here, 0:128] = jnp.where(lane < 4, tile, total[rows_h, 0:128])
            one[here, 128:width - 128] = total[rows_h, 128:width - 128]
            one[here, width - 128:width] = jnp.where(lane >= 124, tile, total[rows_h, width - 128:width])
        return carry

    def rim(at_row, rim8):
        here = slice(at_row, at_row + 8)
        one[here, 0:128] = jnp.where(lane < 4, one[here, 0:128], rim8[:, 0:128])
        one[here, 128:width - 128] = rim8[:, 128:width - 128]
        one[here, width - 128:width] = jnp.where(lane >= 124, one[here, width - 128:width], rim8[:, width - 128:width])

    finish(jnp.int32(0), 0)
    rim(0, rims[0:8, :])
    store(0).start()

    def start_store(i, carry):
        finish(i, carry)
        store(i).start()
        return carry

    lax.fori_loop(1, n_chunk - 1, start_store, 0)
    finish(jnp.int32(n_chunk - 1), 0)
    rim(length - 8, rims[8:16, :])
    store(n_chunk - 1).start()

    def finish_store(i, carry):
        store(i).wait()
        return carry

    lax.fori_loop(0, n_chunk, finish_store, 0)


def last_step(three, side, rims):
    length, width = three.shape[0] - 16, three.shape[1]
    vmem = pl.BlockSpec(memory_space=pltpu.VMEM)
    return pl.pallas_call(
        last_step_kernel,
        name="last_step",
        out_shape=jax.ShapeDtypeStruct((length, width), F32),
        in_specs=[vmem] * 3,
        out_specs=pl.BlockSpec(memory_space=pl.ANY),
        scratch_shapes=[pltpu.VMEM((length, width), F32), pltpu.SemaphoreType.DMA((length // CHUNK,))],
        compiler_params=pltpu.CompilerParams(vmem_limit_bytes=16 * 2**20),
        cost_estimate=pl.CostEstimate(flops=5 * length * width, bytes_accessed=8 * length * width, transcendentals=0),
    )(three, side, rims)


CHUNK = 256
BAND = 256


def spread_and_diffuse(n_row, n_col, positions, macro):
    length, width = macro.shape
    n_slot = n_row * n_col * CAP
    any_space = pl.BlockSpec(memory_space=pl.ANY)
    vmem = pl.BlockSpec(memory_space=pltpu.VMEM)
    dma = pltpu.SemaphoreType.DMA
    return pl.pallas_call(
        functools.partial(grid_kernel, n_row, n_col),
        name="spread_and_diffuse",
        out_shape=(
            jax.ShapeDtypeStruct((length + 16, width), F32),
            jax.ShapeDtypeStruct((32, length + 256), F32),
            jax.ShapeDtypeStruct((16, width), F32),
        ),
        in_specs=[vmem, any_space],
        out_specs=(vmem,) * 3,
        scratch_shapes=[
            pltpu.VMEM((length + 16, width), F32),
            pltpu.VMEM((n_slot, width), BF16),
            pltpu.VMEM((BAND, n_slot), BF16),
            pltpu.VMEM((BAND, n_slot), BF16),
            pltpu.VMEM((32, n_slot), BF16),
            pltpu.VMEM((32, n_slot), BF16),
            pltpu.VMEM((32, n_slot), BF16),
            pltpu.VMEM((8, width), F32),
            pltpu.VMEM((8, width), F32),
            pltpu.VMEM((8, length), F32),
            pltpu.VMEM((8, length), F32),
            pltpu.VMEM((8, width), F32),
            pltpu.VMEM((8, width), F32),
            pltpu.VMEM((8, length + 256), F32),
            pltpu.VMEM((8, length + 256), F32),
            pltpu.VMEM((16, width), F32),
            pltpu.VMEM((16, width), F32),
            dma((length // BAND,)),
            dma((9,)),
            dma((9,)),
        ],
        compiler_params=pltpu.CompilerParams(
            collective_id=1, has_side_effects=True, vmem_limit_bytes=24 * 2**20
        ),
        cost_estimate=pl.CostEstimate(flops=10**10, bytes_accessed=8 * length * width, transcendentals=0),
    )(positions, macro)


def per_device(right_side, anchor, tiles, neighbours, owners, row_offset, col_offset, macro_density):
    n_row, n_col = lax.axis_size("row"), lax.axis_size("col")
    solution, arrived = solve(
        n_row, n_col, neighbours.T, right_side, anchor, owners.T, row_offset, col_offset, tiles,
    )
    return solution, last_step(*spread_and_diffuse(n_row, n_col, arrived, macro_density))


def solution(mesh):
    blocks = P(("row", "col"))
    return jax.shard_map(
        per_device,
        mesh=mesh,
        in_specs=(
            P(("row", "col"), None, None),
            P(("row", "col"), None),
            P(("row", "col"), None, None, None),
            P(("row", "col"), None),
            P(("row", "col"), None),
            blocks,
            blocks,
            P("row", "col"),
        ),
        out_specs=(P(("row", "col"), None, None), P("row", "col")),
        check_vma=False,
    )
```

```python
import functools

import jax
import jax.numpy as jnp
from jax import lax
from jax.experimental import pallas as pl
from jax.experimental.pallas import tpu as pltpu
from jax.sharding import PartitionSpec as P

MESH = pl.DeviceIdType.MESH
F32 = jnp.float32
BF16 = jnp.bfloat16
STEPS = 4
CAP = 32
NONE = -1000.0
AROUND = [(dr, dc) for dr in (-1, 0, 1) for dc in (-1, 0, 1)]


def nt_dot(a, b):
    return lax.dot_general(a, b, (((1,), (1,)), ((), ())), preferred_element_type=F32)


def nn_dot(a, b):
    return jnp.dot(a, b, preferred_element_type=F32)


def split3(x):
    hi = x.astype(BF16)
    rest = x - hi.astype(F32)
    mid = rest.astype(BF16)
    low = (rest - mid.astype(F32)).astype(BF16)
    return hi, mid, low


def iota(shape, dim):
    return lax.broadcasted_iota(jnp.int32, shape, dim)


def remote(src, dst, send, recv, row, col):
    return pltpu.make_async_remote_copy(
        src_ref=src, dst_ref=dst, send_sem=send, recv_sem=recv,
        device_id={"row": row, "col": col}, device_id_type=MESH,
    )


def solve_kernel(
    n_row, n_col,
    nbr_hbm, rhs_hbm, anchor_hbm, owner_hbm, roff_hbm, coff_hbm, tiles_ref,
    sol_ref, pos_ref,
    stage, thi, tlo, xbuf, sel, spread_sel, gath, terms, back, recv,
    ar_row, ar_col, own_hot, rank_sc, weight_sc, out_rows, mid_rows, end_rows, table_sc,
    own_sel, own_g, down_sc, sums_sc, far_sum, down_sum, nbr_sc, rhs_ref, anchor_ref, owner_ref, roff_ref, coff_ref, small_sem,
    tile_sem, fs, fr, bs, br, rs, rr, cs, cr, away1, got, away2, land, keep_sem,
):
    n_blk, fan, side, _ = thi.shape
    rows = 2 * n_blk
    q_own = n_blk * fan * 8
    q_all = q_own + n_blk * 8
    n_dev = n_row * n_col
    me_r = lax.axis_index("row")
    me_c = lax.axis_index("col")
    row_order = sorted(range(1, n_row), key=lambda d: -min(d, n_row - d))
    col_order = sorted(range(1, n_col), key=lambda d: -(min(d // 4, 4 - d // 4) + min(d % 4, 4 - d % 4)))
    around = sorted((g for g in range(9) if g != 4), key=lambda g: -abs(AROUND[g][0]) - 2 * abs(AROUND[g][1]))

    small = [
        pltpu.make_async_copy(src, dst, small_sem.at[i])
        for i, (src, dst) in enumerate((
            (rhs_hbm, rhs_ref), (owner_hbm, owner_ref), (nbr_hbm, nbr_sc),
            (anchor_hbm, anchor_ref), (roff_hbm, roff_ref), (coff_hbm, coff_ref),
        ))
    ]
    for copy in small:
        copy.start()
    for b in range(n_blk):
        pltpu.make_async_copy(tiles_ref.at[b], stage.at[b], tile_sem.at[b]).start()

    barrier = pltpu.get_barrier_semaphore()
    peers = [AROUND[g] for g in around if AROUND[g][0] and AROUND[g][1]]
    peers += [(0, d) for d in col_order] + [(d, 0) for d in row_order]
    for dr, dc in peers:
        pl.semaphore_signal(
            barrier, inc=1,
            device_id={"row": lax.rem(me_r + dr + n_row, n_row), "col": lax.rem(me_c + dc + n_col, n_col)},
            device_id_type=MESH,
        )

    own_lo = 4 * rows
    below = iota((side - 9 * rows, side), 0)
    for it in range(3):
        xbuf[it, 9 * rows:side, :] = jnp.where(below == 0, 1.0, 0.0)
    for copy in small[:2]:
        copy.wait()
    for b in range(n_blk):
        xbuf[0, own_lo + 2 * b:own_lo + 2 * b + 2, :] = rhs_ref[b]

    upper = (iota((side, side), 0) < iota((side, side), 1)).astype(F32).astype(BF16)
    count = jnp.zeros((n_dev, 1), F32)
    held = jnp.zeros((1, n_dev), F32)
    for b in range(n_blk):
        hot = (owner_ref[0:1, b * side:(b + 1) * side] == iota((n_dev, side), 0)).astype(F32)
        before = nn_dot(hot.astype(BF16), upper) + count
        rank_sc[b:b + 1, :] = jnp.sum(hot * before, axis=0, keepdims=True)
        count = count + jnp.sum(hot, axis=1, keepdims=True)
        turned = jnp.transpose(hot)
        own_hot[b] = turned.astype(BF16)
        held = held + jnp.sum(turned, axis=0, keepdims=True)

    ones_row = 9 * rows
    lane3 = iota((8, 3 * side), 1)
    part_row = iota((8, 1), 0)
    base_col = jnp.where(
        part_row < 6, (part_row // 2) * side + lax.rem(part_row, 2), jnp.where(part_row == 6, ones_row, -1)
    )
    moves = (part_row < 6).astype(jnp.int32)

    lane_own = iota((8, 4 * rows), 1)
    own_col = jnp.where(
        part_row < 6, (part_row // 2) * rows + lax.rem(part_row, 2), jnp.where(part_row == 6, 3 * rows, -1)
    )

    def select_row(q, slot):
        sel[q:q + 8, :] = (lane3 == base_col + moves * (2 * slot)).astype(F32).astype(BF16)

    for copy in small[2:]:
        copy.wait()
    for b in range(n_blk):
        for k in range(fan):
            named = nbr_sc[k, b]
            dev = named // n_blk
            slot = ((dev // n_col - me_r + 1) * 3 + (lax.rem(dev, n_col) - me_c + 1)) * n_blk + lax.rem(named, n_blk)
            select_row((b * fan + k) * 8, slot)
        select_row(q_own + b * 8, 4 * n_blk + b)
        own_sel[b * 8:(b + 1) * 8, :] = (lane_own == own_col + moves * (2 * b)).astype(F32).astype(BF16)
    sel_t = sel[:, 0:side].astype(F32) + sel[:, side:2 * side].astype(F32) + sel[:, 2 * side:].astype(F32)
    spread_sel[...] = jnp.transpose(jnp.concatenate([sel_t, jnp.zeros((384 - q_all, side), F32)], axis=0)).astype(BF16)
    terms[...] = jnp.zeros_like(terms)

    pl.semaphore_wait(barrier, len(peers))

    def x_rows(it, g):
        return xbuf.at[it, pl.ds(g * rows, rows)]

    pending = []

    def forward(it):
        for g in around:
            dr, dc = AROUND[g]
            copy = remote(
                x_rows(it, 4), x_rows(it, 8 - g), fs.at[it, g], fr.at[it, 8 - g],
                lax.rem(me_r + dr + n_row, n_row), lax.rem(me_c + dc + n_col, n_col),
            )
            copy.start()
            pending.append(copy)

    def forward_wait(it):
        for g in around:
            remote(x_rows(it, 4), x_rows(it, g), fs.at[it, g], fr.at[it, g], me_r, me_c).wait_recv()

    def backward(it):
        for g in around:
            dr, dc = AROUND[g]
            copy = remote(
                back.at[it, pl.ds(g * rows, rows)], recv.at[it, 8 - g], bs.at[it, g], br.at[it, 8 - g],
                lax.rem(me_r + dr + n_row, n_row), lax.rem(me_c + dc + n_col, n_col),
            )
            copy.start()
            pending.append(copy)

    def backward_wait(it):
        for g in around:
            remote(back.at[it, pl.ds(g * rows, rows)], recv.at[it, g], bs.at[it, g], br.at[it, g], me_r, me_c).wait_recv()

    forward(0)

    def split_block(b, carry):
        pltpu.make_async_copy(tiles_ref.at[b], stage.at[b], tile_sem.at[b]).wait()
        for k in range(fan):
            t = stage[b, k]
            hi = t.astype(BF16)
            thi[b, k] = hi
            tlo[b, k] = (t - hi.astype(F32)).astype(BF16)
        return carry

    lax.fori_loop(0, n_blk, split_block, 0, unroll=2)

    first_row = jnp.where(iota((rows, side), 0) == 0, 1.0, 0.0).astype(BF16)

    def grouped(c, v):
        return (v.reshape(q_own // 8, 8, side) * c[None]).reshape(q_own, side)

    def over_parts(v):
        return v + pltpu.roll(v, q_own - 2, 0) + pltpu.roll(v, q_own - 4, 0)

    def own_products(it, own):
        own_g[...] = nn_dot(own_sel[...], jnp.concatenate(split3(own) + (first_row,), axis=0))

        def one_block(b, carry):
            own_b = own_g[pl.ds(pl.multiple_of(b * 8, 8), 8), :].astype(BF16)
            for k in range(fan):
                q = pl.multiple_of((b * fan + k) * 8, 8)
                down = nn_dot(own_b, thi[b, k]) + nn_dot(own_b, tlo[b, k])
                down_sc[pl.ds(q, 8), :] = down
                if it == 0:
                    sums_sc[pl.ds(q, 8), :] = jnp.broadcast_to(down[6:7, :], (8, side))
            return carry

        lax.fori_loop(0, n_blk, one_block, 0, unroll=8)
        down_sum[it] = over_parts(down_sc[...])

    def gather_far(it):
        parts = jnp.concatenate(split3(xbuf[it]), axis=0)
        gath[...] = nn_dot(sel[0:q_own, :], parts)

    def apply(it, after_forward=None):
        forward_wait(it)
        if after_forward is not None:
            after_forward()
        gather_far(it)

        def one_block(b, carry):
            total = jnp.zeros((8, side), F32)
            for k in range(fan):
                q = pl.multiple_of((b * fan + k) * 8, 8)
                far_b = gath[pl.ds(q, 8), :].astype(BF16)
                total = total + nt_dot(far_b, thi[b, k]) + nt_dot(far_b, tlo[b, k])
            weight = total[6:7, :] + anchor_ref[pl.ds(b, 1), :]
            if it == 0:
                weight_sc[pl.ds(b, 1), :] = weight
            own = own_g[pl.ds(pl.multiple_of(b * 8, 8), 8), :]
            terms[pl.ds(pl.multiple_of(q_own + b * 8, 8), 8), :] = weight * own - total
            return carry

        lax.fori_loop(0, n_blk, one_block, 0, unroll=4)
        terms[0:q_own, :] = sums_sc[...] * gath[...] - down_sc[...]
        hi, mid, low = split3(terms[...])
        where_to = spread_sel[0:9 * rows, :]
        back[it] = nn_dot(where_to, hi) + nn_dot(where_to, mid) + nn_dot(where_to, low)
        backward(it)
        far_sum[it] = over_parts(gath[...])

    def applied(it):
        backward_wait(it)
        image = back[it, own_lo:own_lo + rows, :]
        for g in range(9):
            if g != 4:
                image = image + recv[it, g]
        return image

    def dots_start(it, pairs, more=None):
        lane = iota((8, 128), 1)
        tile = jnp.zeros((8, 128), F32)
        for d, (a, b) in enumerate(pairs):
            e = a * b
            e = e[0:8] + e[8:16]
            if d == 0 and more is not None:
                e = e + more
            tile = jnp.where(lane == d, jnp.sum(e, axis=1, keepdims=True), tile)
        ar_row[it, me_r] = tile
        for d in row_order:
            copy = remote(
                ar_row.at[it, me_r], ar_row.at[it, me_r], rs.at[it, d], rr.at[it, me_r],
                lax.rem(me_r + d, n_row), me_c,
            )
            copy.start()
            pending.append(copy)

    def dots_middle(it):
        for d in row_order:
            far = lax.rem(me_r + d, n_row)
            remote(ar_row.at[it, far], ar_row.at[it, far], rs.at[it, d], rr.at[it, far], me_r, me_c).wait_recv()
        ar_col[it, me_c] = jnp.sum(ar_row[it], axis=0)
        for d in col_order:
            copy = remote(
                ar_col.at[it, me_c], ar_col.at[it, me_c], cs.at[it, d], cr.at[it, me_c],
                me_r, lax.rem(me_c + d, n_col),
            )
            copy.start()
            pending.append(copy)

    def dots_end(it, n):
        for d in col_order:
            far = lax.rem(me_c + d, n_col)
            remote(ar_col.at[it, far], ar_col.at[it, far], cs.at[it, d], cr.at[it, far], me_r, me_c).wait_recv()
        t = jnp.sum(ar_col[it], axis=0)
        t = t + pltpu.roll(t, 4, 0)
        t = t + pltpu.roll(t, 2, 0)
        return [t[:, d:d + 1] for d in range(n)]

    def times(c, v):
        return jnp.concatenate([c] * (v.shape[0] // 8), axis=0) * v

    rank_of = iota((CAP, side), 0)

    def by_owner(values_of):
        total = None
        for b in range(n_blk):
            mine = rank_of == rank_sc[b:b + 1, :].astype(jnp.int32)
            placed = jnp.concatenate([jnp.where(mine, v, 0.0) for v in values_of(b)], axis=0)
            for part in split3(placed):
                more = nn_dot(part, own_hot[b])
                total = more if total is None else total + more
        return total

    def both(v):
        return lambda b: [v[2 * b:2 * b + 1, :], v[2 * b + 1:2 * b + 2, :]]

    def offsets(b):
        return [r[b * side:(b + 1) * side].reshape(1, side).astype(F32) for r in (roff_ref, coff_ref)]

    r0 = xbuf[0, own_lo:own_lo + rows, :]
    own_products(0, r0)
    apply(0)
    table_r0 = by_owner(both(r0))
    table_off = by_owner(offsets)
    w0 = applied(0)
    xbuf[1, own_lo:own_lo + rows, :] = w0
    forward(1)
    dots_start(0, [(r0, r0), (r0, w0)])
    own_products(1, w0)
    apply(1, lambda: dots_middle(0))
    table_w0 = by_owner(both(w0))
    gamma0, curve0 = dots_end(0, 2)
    alpha0 = gamma0 / curve0
    z0 = applied(1)
    w1 = w0 - times(alpha0, z0)
    xbuf[2, own_lo:own_lo + rows, :] = w1
    r1 = r0 - times(alpha0, w0)
    dots_start(1, [(r1, r1), (r1, w1), (r1, w0)])
    forward(2)

    table = jnp.concatenate([table_r0, table_w0, by_owner(both(w1)), table_off], axis=0)
    empty = iota((CAP, n_dev), 0).astype(F32) >= held
    table = jnp.concatenate(
        [table[0:6 * CAP], jnp.where(empty, NONE, table[6 * CAP:7 * CAP]), table[7 * CAP:]], axis=0
    )
    table = jnp.transpose(table)
    for o in range(n_dev):
        out_rows[o // n_col, o % n_col] = table[o:o + 1, :]
    keep = pltpu.make_async_copy(out_rows.at[me_r], mid_rows.at[:, me_r], keep_sem.at[0])
    keep.start()
    for d in row_order:
        far = lax.rem(me_r + d, n_row)
        copy = remote(out_rows.at[far], mid_rows.at[:, me_r], away1.at[d], got.at[me_r], far, me_c)
        copy.start()
        pending.append(copy)

    dots_middle(1)

    keep.wait()
    for d in row_order:
        far = lax.rem(me_r + d, n_row)
        remote(out_rows.at[far], mid_rows.at[:, far], away1.at[d], got.at[far], me_r, me_c).wait_recv()
    keep2 = pltpu.make_async_copy(mid_rows.at[me_c], end_rows.at[me_c], keep_sem.at[1])
    keep2.start()
    for d in col_order:
        far = lax.rem(me_c + d, n_col)
        copy = remote(mid_rows.at[far], end_rows.at[me_c], away2.at[d], land.at[me_c], me_r, far)
        copy.start()
        pending.append(copy)

    own_products(2, w1)
    forward_wait(2)
    gather_far(2)
    far_r1 = far_sum[0] - grouped(alpha0, far_sum[1])
    down_r1 = down_sum[0] - grouped(alpha0, down_sum[1])
    far_w1 = over_parts(gath[...])
    gamma1, r1w1, r1w0 = dots_end(1, 3)
    beta0 = gamma1 / gamma0
    curve1 = r1w1 + 2.0 * beta0 * r1w0 + beta0 * beta0 * curve0
    alpha1 = gamma1 / curve1
    p1 = r1 + times(beta0, r0)
    s1 = w1 + times(beta0, w0)
    r2 = r1 - times(alpha1, s1)

    far_r2 = far_r1 - grouped(alpha1, far_w1 + grouped(beta0, far_sum[1]))
    down_r2 = down_r1 - grouped(alpha1, down_sum[2] + grouped(beta0, down_sum[1]))
    cross = far_r2 * (sums_sc[...] * far_r2 - 2.0 * down_r2)
    cross = jnp.sum(cross.reshape(q_own // 8, 8, side), axis=0)
    cross = jnp.where(iota((8, side), 0) < 2, cross, 0.0)
    weights = weight_sc[...]
    weights = jnp.concatenate([weights[b:b + 1] for b in range(n_blk) for _ in (0, 1)], axis=0)
    dots_start(2, [(r2, weights * r2), (r2, r2), (r2, s1)], more=cross)

    keep2.wait()
    for d in col_order:
        far = lax.rem(me_c + d, n_col)
        remote(mid_rows.at[far], end_rows.at[far], away2.at[d], land.at[far], me_r, me_c).wait_recv()
    dots_middle(2)
    for o in range(n_dev):
        table_sc[o:o + 1, :] = end_rows[o // n_row, o % n_row]
    curve_r2, gamma2, r2s1 = dots_end(2, 3)
    beta1 = gamma2 / gamma1
    curve2 = curve_r2 + 2.0 * beta1 * r2s1 + beta1 * beta1 * curve1
    alpha2 = gamma2 / curve2

    of_b = alpha0 + alpha1 * (1.0 + beta0) + alpha2 * (1.0 + beta1 * (1.0 + beta0))
    of_w0 = -alpha1 * alpha0 - alpha2 * (alpha0 + alpha1 * beta0 + beta1 * alpha0)
    of_w1 = -alpha2 * alpha1
    lane = iota((1, 128), 1)

    def by_lane(first, second):
        return jnp.where(
            lane < CAP, first[0:1], jnp.where(lane < 2 * CAP, first[1:2], jnp.where(lane < 3 * CAP, second[0:1], second[1:2]))
        )

    near = table_sc[:, 0:128] * by_lane(of_b, of_w0)
    far = table_sc[:, 128:256]
    moved = near + pltpu.roll(near, 64, 1) + far * by_lane(of_w1, of_w1)
    pos_ref[...] = pltpu.roll(far, 64, 1) + 3.0 * jnp.tanh(moved)

    x = times(alpha0, r0) + times(alpha1, p1) + times(alpha2, r2 + times(beta1, p1))
    for b in range(n_blk):
        sol_ref[b] = x[2 * b:2 * b + 2, :]
    for copy in pending:
        copy.wait_send()


def solve(n_row, n_col, neighbours, right_side, anchor, owners, row_offset, col_offset, tiles):
    n_blk, fan, side, _ = tiles.shape
    rows = 2 * n_blk
    n_dev = n_row * n_col
    q_all = n_blk * fan * 8 + n_blk * 8
    vmem = pl.BlockSpec(memory_space=pltpu.VMEM)
    dma = pltpu.SemaphoreType.DMA
    return pl.pallas_call(
        functools.partial(solve_kernel, n_row, n_col),
        name="solve_and_route",
        out_shape=(
            jax.ShapeDtypeStruct(right_side.shape, F32),
            jax.ShapeDtypeStruct((n_dev, 128), F32),
        ),
        in_specs=[pl.BlockSpec(memory_space=pltpu.HBM)] * 7,
        out_specs=(vmem, vmem),
        scratch_shapes=[
            pltpu.VMEM(tiles.shape, F32),
            pltpu.VMEM(tiles.shape, BF16),
            pltpu.VMEM(tiles.shape, BF16),
            pltpu.VMEM((3, side, side), F32),
            pltpu.VMEM((q_all, 3 * side), BF16),
            pltpu.VMEM((side, 384), BF16),
            pltpu.VMEM((8 * n_blk * fan, side), F32),
            pltpu.VMEM((384, side), F32),
            pltpu.VMEM((2, 9 * rows, side), F32),
            pltpu.VMEM((2, 9, rows, side), F32),
            pltpu.VMEM((3, n_row, 8, 128), F32),
            pltpu.VMEM((3, n_col, 8, 128), F32),
            pltpu.VMEM((n_blk, side, n_dev), BF16),
            pltpu.VMEM((n_blk, side), F32),
            pltpu.VMEM((n_blk, side), F32),
            pltpu.VMEM((n_row, n_col, 1, 8 * CAP), F32),
            pltpu.VMEM((n_col, n_row, 1, 8 * CAP), F32),
            pltpu.VMEM((n_col, n_row, 1, 8 * CAP), F32),
            pltpu.VMEM((n_dev, 8 * CAP), F32),
            pltpu.VMEM((8 * n_blk, 4 * rows), BF16),
            pltpu.VMEM((8 * n_blk, side), F32),
            pltpu.VMEM((8 * n_blk * fan, side), F32),
            pltpu.VMEM((8 * n_blk * fan, side), F32),
            pltpu.VMEM((2, 8 * n_blk * fan, side), F32),
            pltpu.VMEM((3, 8 * n_blk * fan, side), F32),
            pltpu.SMEM((fan, n_blk), jnp.int32),
            pltpu.VMEM(right_side.shape, F32),
            pltpu.VMEM(anchor.shape, F32),
            pltpu.VMEM(owners.shape, jnp.int32),
            pltpu.VMEM(row_offset.shape, jnp.int32),
            pltpu.VMEM(col_offset.shape, jnp.int32),
            dma((6,)),
            dma((n_blk,)),
            dma((3, 9)), dma((3, 9)), dma((3, 9)), dma((3, 9)),
            dma((3, n_row)), dma((3, n_row)), dma((3, n_col)), dma((3, n_col)),
            dma((n_row,)), dma((n_row,)), dma((n_col,)), dma((n_col,)), dma((2,)),
        ],
        compiler_params=pltpu.CompilerParams(
            collective_id=0, has_side_effects=True, vmem_limit_bytes=63480000
        ),
        cost_estimate=pl.CostEstimate(flops=10**9, bytes_accessed=2**23, transcendentals=0),
    )(neighbours, right_side, anchor, owners, row_offset, col_offset, tiles)


def grid_kernel(
    n_row, n_col,
    pos_ref, macro_ref, two, side, rims,
    one, bell_col, left_sel, right_sel, low_part, high_part, place,
    top_s, bottom_s, west_s, east_s, up_r, down_r, west_r, east_r, keep_top, keep_bottom,
    in_sem, ss, rs,
):
    length, width = macro_ref.shape
    n_dev = n_row * n_col
    n_slot = bell_col.shape[0]
    n_chunk = length // CHUNK
    me_r = lax.axis_index("row")
    me_c = lax.axis_index("col")
    log2e = 1.4426950408889634

    def at(dr, dc):
        return lax.rem(me_r + dr + n_row, n_row), lax.rem(me_c + dc + n_col, n_col)

    def load(i):
        return pltpu.make_async_copy(
            macro_ref.at[pl.ds(i * BAND, BAND)], one.at[pl.ds(8 + i * BAND, BAND)], in_sem.at[i]
        )

    barrier = pltpu.get_barrier_semaphore()
    around = sorted((g for g in range(9) if g != 4), key=lambda g: -abs(AROUND[g][0]) - 2 * abs(AROUND[g][1]))
    for g in around:
        row, col = at(*AROUND[g])
        pl.semaphore_signal(barrier, inc=1, device_id={"row": row, "col": col}, device_id_type=MESH)
    for i in range(length // BAND):
        load(i).start()
    rim = jnp.zeros((8, width), F32)
    for buf in (one, two):
        buf[0:8, :] = rim
        buf[length + 8:length + 16, :] = rim

    turned = jnp.transpose(pos_ref[...])
    at_row = turned[0:CAP]
    start = jnp.clip(jnp.floor(at_row) - 7.0, 0.0, length - 16.0)
    block = jnp.floor(start * (1.0 / 32.0))
    rows48 = iota((48, n_dev), 0).astype(F32)
    for j in range(CAP):
        u = rows48 + 32.0 * block[j:j + 1]
        d = u - at_row[j:j + 1]
        inside = jnp.abs(u - (start[j:j + 1] + 7.5)) < 8.0
        bell = jnp.where(inside, jnp.exp2(d * d * (-0.5 * log2e)), 0.0).astype(BF16)
        here = slice(j * n_dev, (j + 1) * n_dev)
        low_part[:, here] = bell[0:32]
        high_part[:, here] = jnp.concatenate([bell[32:48], jnp.zeros((16, n_dev), BF16)], axis=0)
        place[:, here] = jnp.broadcast_to(block[j:j + 1], (32, n_dev)).astype(BF16)

    all_pos = pos_ref[...]
    at_col = pltpu.roll(all_pos, 128 - CAP, 1)
    middle = jnp.clip(jnp.floor(at_col) - 7.0, 0.0, width - 16.0) + 7.5
    v = iota((1, width), 1).astype(F32)

    def some_columns(i, carry):
        p, m = carry
        for k in range(8):
            d = v - p[:, k:k + 1]
            inside = jnp.abs(v - m[:, k:k + 1]) < 8.0
            bell = jnp.where(inside, jnp.exp2(d * d * (-0.5 * log2e)), 0.0)
            bell_col[pl.ds(pl.multiple_of((i * 8 + k) * n_dev, n_dev), n_dev), :] = bell.astype(BF16)
        return pltpu.roll(p, 120, 1), pltpu.roll(m, 120, 1)

    lax.fori_loop(0, CAP // 8, some_columns, (at_col, middle))

    def build(dst, band):
        for sub in range(BAND // 32):
            block_id = (band * (BAND // 32) + sub).astype(F32)
            first = place[...] == jnp.full((32, n_slot), block_id, F32).astype(BF16)
            second = place[...] == jnp.full((32, n_slot), block_id - 1.0, F32).astype(BF16)
            zero = jnp.zeros((32, n_slot), BF16)
            dst[sub * 32:(sub + 1) * 32, :] = jnp.where(
                first, low_part[...], jnp.where(second, high_part[...], zero)
            )

    def product(src, band):
        load(band).wait()
        here = pl.ds(pl.multiple_of(8 + band * BAND, 8), BAND)
        one[here, :] = one[here, :] + nn_dot(src[...], bell_col[...])

    build(left_sel, jnp.int32(0))

    def two_bands(i, carry):
        build(right_sel, 2 * i + 1)
        product(left_sel, 2 * i)
        build(left_sel, jnp.minimum(2 * i + 2, length // BAND - 1))
        product(right_sel, 2 * i + 1)
        return carry

    lax.fori_loop(0, length // BAND // 2, two_bands, 0)

    top_s[...] = one[8:16, :]
    bottom_s[...] = one[length:length + 8, :]
    keep_top[...] = one[8:24, :]
    keep_bottom[...] = one[length - 8:length + 8, :]
    lane = iota((1, 128), 1)
    for i in range(length // 128):
        here = slice(8 + i * 128, 8 + (i + 1) * 128)
        tile = jnp.transpose(jnp.where(lane < 64, one[here, 0:128], one[here, width - 128:width]))
        west_s[:, i * 128:(i + 1) * 128] = tile[0:8]
        east_s[:, i * 128:(i + 1) * 128] = tile[120:128]

    pl.semaphore_wait(barrier, 8)
    first = (slice(None), pl.ds(0, 128))
    last = (slice(None), pl.ds(length - 128, 128))
    inner = (slice(None), pl.ds(128, length))
    above = (slice(None), pl.ds(0, 128))
    below = (slice(None), pl.ds(length + 128, 128))
    plan = {
        (-1, 0): (top_s, down_r),
        (1, 0): (bottom_s, up_r),
        (0, -1): (west_s, east_r.at[inner]),
        (0, 1): (east_s, west_r.at[inner]),
        (-1, -1): (west_s.at[first], east_r.at[below]),
        (-1, 1): (east_s.at[first], west_r.at[below]),
        (1, -1): (west_s.at[last], east_r.at[above]),
        (1, 1): (east_s.at[last], west_r.at[above]),
    }
    copies = []
    for g in around:
        src, dst = plan[AROUND[g]]
        row, col = at(*AROUND[g])
        copy = remote(src, dst, ss.at[g], rs.at[g], row, col)
        copy.start()
        copies.append(copy)

    for src, dst in ((one, two), (two, one), (one, two)):

        def strip(i, carry, src=src, dst=dst):
            begin = pl.multiple_of(8 + i * STRIP, 8)
            dst[pl.ds(begin, STRIP), :] = summed(src, begin, STRIP)
            return carry

        lax.fori_loop(0, length // STRIP, strip, 0)

    for copy in copies:
        copy.wait_recv()
    not_first_row = (me_r > 0).astype(F32)
    not_last_row = (me_r < n_row - 1).astype(F32)
    not_first_col = (me_c > 0).astype(F32)
    not_last_col = (me_c < n_col - 1).astype(F32)
    scale = 0.2 ** STEPS

    def cross(t):
        n, m = t.shape
        return (t + pltpu.roll(t, 1, 0)) + (pltpu.roll(t, n - 1, 0) + pltpu.roll(t, 1, 1)) + pltpu.roll(t, m - 1, 1)

    pad = jnp.zeros((120, 128), F32)
    corners = []
    for halo, order in ((up_r, 0), (down_r, 1)):
        for part in (halo[:, 0:128], halo[:, width - 128:width]):
            corners.append(jnp.transpose(jnp.concatenate([pad, part] if order == 0 else [part, pad], axis=0)))
    own_west = jnp.concatenate([corners[0][0:8], west_s[...], corners[2][0:8]], axis=1)
    own_east = jnp.concatenate([corners[1][120:128], east_s[...], corners[3][120:128]], axis=1)
    t = jnp.concatenate([west_r[...], own_west, own_east, east_r[...]], axis=0)
    down32 = iota((32, 1), 0)
    along = iota((1, length + 256), 1)
    mask = jnp.where(down32 < 8, not_first_col, jnp.where(down32 >= 24, not_last_col, 1.0)) * jnp.where(
        along < 128, jnp.where(along >= 120, not_first_row, 0.0),
        jnp.where(along >= length + 128, jnp.where(along < length + 136, not_last_row, 0.0), 1.0),
    )
    t = t * mask
    for step in range(STEPS):
        t = cross(t)
        if step < STEPS - 1:
            t = t * mask
    side[...] = t * scale

    def rim_rows(halo, kept, keep, at_top):
        r = jnp.concatenate([halo * keep, kept] if at_top else [kept, halo * keep], axis=0)
        near = iota((24, 1), 0)
        flag = jnp.where((near < 8) if at_top else (near >= 16), keep, 1.0)
        for step in range(STEPS):
            r = cross(r)
            if step < STEPS - 1:
                r = r * flag
        return (r[8:16] if at_top else r[8:16]) * scale

    rims[0:8, :] = rim_rows(up_r[...], keep_top[...], not_first_row, True)
    rims[8:16, :] = rim_rows(down_r[...], keep_bottom[...], not_last_row, False)
    for copy in copies:
        copy.wait_send()


def summed(src, begin, n):
    width = src.shape[1]
    window = src[pl.ds(pl.multiple_of(begin - 8, 8), n + 16), :]
    centre = window[8:8 + n]
    return (
        (centre + window[7:7 + n]) + (window[9:9 + n] + pltpu.roll(centre, 1, 1)) + pltpu.roll(centre, width - 1, 1)
    )


def last_step_kernel(two, side, rims, out_ref, one, out_sem):
    length, width = out_ref.shape
    n_chunk = length // CHUNK
    scale = 0.2 ** STEPS
    lane = iota((1, 128), 1)

    def store(i):
        here = pl.ds(pl.multiple_of(i * CHUNK, CHUNK), CHUNK)
        return pltpu.make_async_copy(one.at[here], out_ref.at[here], out_sem.at[i])

    zero112 = jnp.zeros((112, 128), F32)

    def finish(i, carry):
        total = summed(two, pl.multiple_of(8 + i * CHUNK, 8), CHUNK) * scale
        for h in range(CHUNK // 128):
            rows_h = slice(h * 128, (h + 1) * 128)
            at_lane = pl.ds(pl.multiple_of(i * CHUNK + (h + 1) * 128, 128), 128)
            tile = jnp.transpose(jnp.concatenate([side[8:16, at_lane], zero112, side[16:24, at_lane]], axis=0))
            here = pl.ds(pl.multiple_of(i * CHUNK + h * 128, 8), 128)
            one[here, 0:128] = jnp.where(lane < 4, tile, total[rows_h, 0:128])
            one[here, 128:width - 128] = total[rows_h, 128:width - 128]
            one[here, width - 128:width] = jnp.where(lane >= 124, tile, total[rows_h, width - 128:width])
        return carry

    def rim(at_row, rim8):
        here = slice(at_row, at_row + 8)
        one[here, 0:128] = jnp.where(lane < 4, one[here, 0:128], rim8[:, 0:128])
        one[here, 128:width - 128] = rim8[:, 128:width - 128]
        one[here, width - 128:width] = jnp.where(lane >= 124, one[here, width - 128:width], rim8[:, width - 128:width])

    finish(jnp.int32(0), 0)
    rim(0, rims[0:8, :])
    store(0).start()

    def start_store(i, carry):
        finish(i, carry)
        store(i).start()
        return carry

    lax.fori_loop(1, n_chunk - 1, start_store, 0)
    finish(jnp.int32(n_chunk - 1), 0)
    rim(length - 8, rims[8:16, :])
    store(n_chunk - 1).start()

    def finish_store(i, carry):
        store(i).wait()
        return carry

    lax.fori_loop(0, n_chunk, finish_store, 0)


def last_step(three, side, rims):
    length, width = three.shape[0] - 16, three.shape[1]
    vmem = pl.BlockSpec(memory_space=pltpu.VMEM)
    return pl.pallas_call(
        last_step_kernel,
        name="last_step",
        out_shape=jax.ShapeDtypeStruct((length, width), F32),
        in_specs=[vmem] * 3,
        out_specs=pl.BlockSpec(memory_space=pl.ANY),
        scratch_shapes=[pltpu.VMEM((length, width), F32), pltpu.SemaphoreType.DMA((length // CHUNK,))],
        compiler_params=pltpu.CompilerParams(vmem_limit_bytes=16 * 2**20),
        cost_estimate=pl.CostEstimate(flops=5 * length * width, bytes_accessed=8 * length * width, transcendentals=0),
    )(three, side, rims)


CHUNK = 256
STRIP = 512
BAND = 256


def spread_and_diffuse(n_row, n_col, positions, macro):
    length, width = macro.shape
    n_slot = n_row * n_col * CAP
    any_space = pl.BlockSpec(memory_space=pl.ANY)
    vmem = pl.BlockSpec(memory_space=pltpu.VMEM)
    dma = pltpu.SemaphoreType.DMA
    return pl.pallas_call(
        functools.partial(grid_kernel, n_row, n_col),
        name="spread_and_diffuse",
        out_shape=(
            jax.ShapeDtypeStruct((length + 16, width), F32),
            jax.ShapeDtypeStruct((32, length + 256), F32),
            jax.ShapeDtypeStruct((16, width), F32),
        ),
        in_specs=[vmem, any_space],
        out_specs=(vmem,) * 3,
        scratch_shapes=[
            pltpu.VMEM((length + 16, width), F32),
            pltpu.VMEM((n_slot, width), BF16),
            pltpu.VMEM((BAND, n_slot), BF16),
            pltpu.VMEM((BAND, n_slot), BF16),
            pltpu.VMEM((32, n_slot), BF16),
            pltpu.VMEM((32, n_slot), BF16),
            pltpu.VMEM((32, n_slot), BF16),
            pltpu.VMEM((8, width), F32),
            pltpu.VMEM((8, width), F32),
            pltpu.VMEM((8, length), F32),
            pltpu.VMEM((8, length), F32),
            pltpu.VMEM((8, width), F32),
            pltpu.VMEM((8, width), F32),
            pltpu.VMEM((8, length + 256), F32),
            pltpu.VMEM((8, length + 256), F32),
            pltpu.VMEM((16, width), F32),
            pltpu.VMEM((16, width), F32),
            dma((length // BAND,)),
            dma((9,)),
            dma((9,)),
        ],
        compiler_params=pltpu.CompilerParams(
            collective_id=1, has_side_effects=True, vmem_limit_bytes=24 * 2**20
        ),
        cost_estimate=pl.CostEstimate(flops=10**10, bytes_accessed=8 * length * width, transcendentals=0),
    )(positions, macro)


def per_device(right_side, anchor, tiles, neighbours, owners, row_offset, col_offset, macro_density):
    n_row, n_col = lax.axis_size("row"), lax.axis_size("col")
    solution, arrived = solve(
        n_row, n_col, neighbours.T, right_side, anchor, owners.T, row_offset, col_offset, tiles,
    )
    return solution, last_step(*spread_and_diffuse(n_row, n_col, arrived, macro_density))


def solution(mesh):
    blocks = P(("row", "col"))
    return jax.shard_map(
        per_device,
        mesh=mesh,
        in_specs=(
            P(("row", "col"), None, None),
            P(("row", "col"), None),
            P(("row", "col"), None, None, None),
            P(("row", "col"), None),
            P(("row", "col"), None),
            blocks,
            blocks,
            P("row", "col"),
        ),
        out_specs=(P(("row", "col"), None, None), P("row", "col")),
        check_vma=False,
    )
```

```python
import functools

import jax
import jax.numpy as jnp
from jax import lax
from jax.experimental import pallas as pl
from jax.experimental.pallas import tpu as pltpu
from jax.sharding import PartitionSpec as P

MESH = pl.DeviceIdType.MESH
F32 = jnp.float32
BF16 = jnp.bfloat16
STEPS = 4
CAP = 32
NONE = -1000.0
AROUND = [(dr, dc) for dr in (-1, 0, 1) for dc in (-1, 0, 1)]


def nt_dot(a, b):
    return lax.dot_general(a, b, (((1,), (1,)), ((), ())), preferred_element_type=F32)


def nn_dot(a, b):
    return jnp.dot(a, b, preferred_element_type=F32)


def split3(x):
    hi = x.astype(BF16)
    rest = x - hi.astype(F32)
    mid = rest.astype(BF16)
    low = (rest - mid.astype(F32)).astype(BF16)
    return hi, mid, low


def iota(shape, dim):
    return lax.broadcasted_iota(jnp.int32, shape, dim)


def remote(src, dst, send, recv, row, col):
    return pltpu.make_async_remote_copy(
        src_ref=src, dst_ref=dst, send_sem=send, recv_sem=recv,
        device_id={"row": row, "col": col}, device_id_type=MESH,
    )


def solve_kernel(
    n_row, n_col,
    nbr_hbm, rhs_hbm, anchor_hbm, owner_hbm, roff_hbm, coff_hbm, tiles_ref,
    sol_ref, pos_ref,
    stage, thi, tlo, xbuf, sel, spread_sel, gath, terms, back, recv,
    ar_row, ar_col, own_hot, rank_sc, weight_sc, out_rows, mid_rows, end_rows, table_sc,
    own_sel, own_g, down_sc, sums_sc, far_sum, down_sum, nbr_sc, rhs_ref, anchor_ref, owner_ref, roff_ref, coff_ref, small_sem,
    tile_sem, fs, fr, bs, br, rs, rr, cs, cr, away1, got, away2, land, keep_sem,
):
    n_blk, fan, side, _ = thi.shape
    rows = 2 * n_blk
    q_own = n_blk * fan * 8
    q_all = q_own + n_blk * 8
    n_dev = n_row * n_col
    me_r = lax.axis_index("row")
    me_c = lax.axis_index("col")
    row_order = sorted(range(1, n_row), key=lambda d: -min(d, n_row - d))
    col_order = sorted(range(1, n_col), key=lambda d: -(min(d // 4, 4 - d // 4) + min(d % 4, 4 - d % 4)))
    around = sorted((g for g in range(9) if g != 4), key=lambda g: -abs(AROUND[g][0]) - 2 * abs(AROUND[g][1]))

    small = [
        pltpu.make_async_copy(src, dst, small_sem.at[i])
        for i, (src, dst) in enumerate((
            (rhs_hbm, rhs_ref), (owner_hbm, owner_ref), (nbr_hbm, nbr_sc),
            (anchor_hbm, anchor_ref), (roff_hbm, roff_ref), (coff_hbm, coff_ref),
        ))
    ]
    for copy in small:
        copy.start()
    for b in range(n_blk):
        pltpu.make_async_copy(tiles_ref.at[b], stage.at[b], tile_sem.at[b]).start()

    barrier = pltpu.get_barrier_semaphore()
    peers = [AROUND[g] for g in around if AROUND[g][0] and AROUND[g][1]]
    peers += [(0, d) for d in col_order] + [(d, 0) for d in row_order]
    for dr, dc in peers:
        pl.semaphore_signal(
            barrier, inc=1,
            device_id={"row": lax.rem(me_r + dr + n_row, n_row), "col": lax.rem(me_c + dc + n_col, n_col)},
            device_id_type=MESH,
        )

    own_lo = 4 * rows
    below = iota((side - 9 * rows, side), 0)
    for it in range(3):
        xbuf[it, 9 * rows:side, :] = jnp.where(below == 0, 1.0, 0.0)
    for copy in small[:2]:
        copy.wait()
    for b in range(n_blk):
        xbuf[0, own_lo + 2 * b:own_lo + 2 * b + 2, :] = rhs_ref[b]

    upper = (iota((side, side), 0) < iota((side, side), 1)).astype(F32).astype(BF16)
    count = jnp.zeros((n_dev, 1), F32)
    held = jnp.zeros((1, n_dev), F32)
    for b in range(n_blk):
        hot = (owner_ref[0:1, b * side:(b + 1) * side] == iota((n_dev, side), 0)).astype(F32)
        before = nn_dot(hot.astype(BF16), upper) + count
        rank_sc[b:b + 1, :] = jnp.sum(hot * before, axis=0, keepdims=True)
        count = count + jnp.sum(hot, axis=1, keepdims=True)
        turned = jnp.transpose(hot)
        own_hot[b] = turned.astype(BF16)
        held = held + jnp.sum(turned, axis=0, keepdims=True)

    ones_row = 9 * rows
    lane3 = iota((8, 3 * side), 1)
    part_row = iota((8, 1), 0)
    base_col = jnp.where(
        part_row < 6, (part_row // 2) * side + lax.rem(part_row, 2), jnp.where(part_row == 6, ones_row, -1)
    )
    moves = (part_row < 6).astype(jnp.int32)

    lane_own = iota((8, 4 * rows), 1)
    own_col = jnp.where(
        part_row < 6, (part_row // 2) * rows + lax.rem(part_row, 2), jnp.where(part_row == 6, 3 * rows, -1)
    )

    def select_row(q, slot):
        sel[q:q + 8, :] = (lane3 == base_col + moves * (2 * slot)).astype(F32).astype(BF16)

    for copy in small[2:]:
        copy.wait()
    for b in range(n_blk):
        for k in range(fan):
            named = nbr_sc[k, b]
            dev = named // n_blk
            slot = ((dev // n_col - me_r + 1) * 3 + (lax.rem(dev, n_col) - me_c + 1)) * n_blk + lax.rem(named, n_blk)
            select_row((b * fan + k) * 8, slot)
        select_row(q_own + b * 8, 4 * n_blk + b)
        own_sel[b * 8:(b + 1) * 8, :] = (lane_own == own_col + moves * (2 * b)).astype(F32).astype(BF16)
    sel_t = sel[:, 0:side].astype(F32) + sel[:, side:2 * side].astype(F32) + sel[:, 2 * side:].astype(F32)
    spread_sel[...] = jnp.transpose(jnp.concatenate([sel_t, jnp.zeros((384 - q_all, side), F32)], axis=0)).astype(BF16)
    terms[...] = jnp.zeros_like(terms)

    pl.semaphore_wait(barrier, len(peers))

    def x_rows(it, g):
        return xbuf.at[it, pl.ds(g * rows, rows)]

    pending = []

    def forward(it):
        for g in around:
            dr, dc = AROUND[g]
            copy = remote(
                x_rows(it, 4), x_rows(it, 8 - g), fs.at[it, g], fr.at[it, 8 - g],
                lax.rem(me_r + dr + n_row, n_row), lax.rem(me_c + dc + n_col, n_col),
            )
            copy.start()
            pending.append(copy)

    def forward_wait(it):
        for g in around:
            remote(x_rows(it, 4), x_rows(it, g), fs.at[it, g], fr.at[it, g], me_r, me_c).wait_recv()

    def backward(it):
        for g in around:
            dr, dc = AROUND[g]
            copy = remote(
                back.at[it, pl.ds(g * rows, rows)], recv.at[it, 8 - g], bs.at[it, g], br.at[it, 8 - g],
                lax.rem(me_r + dr + n_row, n_row), lax.rem(me_c + dc + n_col, n_col),
            )
            copy.start()
            pending.append(copy)

    def backward_wait(it):
        for g in around:
            remote(back.at[it, pl.ds(g * rows, rows)], recv.at[it, g], bs.at[it, g], br.at[it, g], me_r, me_c).wait_recv()

    forward(0)

    def split_block(b, carry):
        pltpu.make_async_copy(tiles_ref.at[b], stage.at[b], tile_sem.at[b]).wait()
        for k in range(fan):
            t = stage[b, k]
            hi = t.astype(BF16)
            thi[b, k] = hi
            tlo[b, k] = (t - hi.astype(F32)).astype(BF16)
        return carry

    lax.fori_loop(0, n_blk, split_block, 0, unroll=2)

    first_row = jnp.where(iota((rows, side), 0) == 0, 1.0, 0.0).astype(BF16)

    def grouped(c, v):
        return (v.reshape(q_own // 8, 8, side) * c[None]).reshape(q_own, side)

    def over_parts(v):
        return v + pltpu.roll(v, q_own - 2, 0) + pltpu.roll(v, q_own - 4, 0)

    def own_products(it, own):
        own_g[...] = nn_dot(own_sel[...], jnp.concatenate(split3(own) + (first_row,), axis=0))

        def one_block(b, carry):
            own_b = own_g[pl.ds(pl.multiple_of(b * 8, 8), 8), :].astype(BF16)
            for k in range(fan):
                q = pl.multiple_of((b * fan + k) * 8, 8)
                down = nn_dot(own_b, thi[b, k]) + nn_dot(own_b, tlo[b, k])
                down_sc[pl.ds(q, 8), :] = down
                if it == 0:
                    sums_sc[pl.ds(q, 8), :] = jnp.broadcast_to(down[6:7, :], (8, side))
            return carry

        lax.fori_loop(0, n_blk, one_block, 0, unroll=8)
        down_sum[it] = over_parts(down_sc[...])

    def gather_far(it):
        parts = jnp.concatenate(split3(xbuf[it]), axis=0)
        gath[...] = nn_dot(sel[0:q_own, :], parts)

    def apply(it, after_forward=None):
        forward_wait(it)
        if after_forward is not None:
            after_forward()
        gather_far(it)

        def one_block(b, carry):
            total = jnp.zeros((8, side), F32)
            for k in range(fan):
                q = pl.multiple_of((b * fan + k) * 8, 8)
                far_b = gath[pl.ds(q, 8), :].astype(BF16)
                total = total + nt_dot(far_b, thi[b, k]) + nt_dot(far_b, tlo[b, k])
            weight = total[6:7, :] + anchor_ref[pl.ds(b, 1), :]
            if it == 0:
                weight_sc[pl.ds(b, 1), :] = weight
            own = own_g[pl.ds(pl.multiple_of(b * 8, 8), 8), :]
            terms[pl.ds(pl.multiple_of(q_own + b * 8, 8), 8), :] = weight * own - total
            return carry

        lax.fori_loop(0, n_blk, one_block, 0, unroll=4)
        terms[0:q_own, :] = sums_sc[...] * gath[...] - down_sc[...]
        hi, mid, low = split3(terms[...])
        where_to = spread_sel[0:9 * rows, :]
        back[it] = nn_dot(where_to, hi) + nn_dot(where_to, mid) + nn_dot(where_to, low)
        backward(it)
        far_sum[it] = over_parts(gath[...])

    def applied(it):
        backward_wait(it)
        image = back[it, own_lo:own_lo + rows, :]
        for g in range(9):
            if g != 4:
                image = image + recv[it, g]
        return image

    def dots_start(it, pairs, more=None):
        lane = iota((8, 128), 1)
        tile = jnp.zeros((8, 128), F32)
        for d, (a, b) in enumerate(pairs):
            e = a * b
            e = e[0:8] + e[8:16]
            if d == 0 and more is not None:
                e = e + more
            tile = jnp.where(lane == d, jnp.sum(e, axis=1, keepdims=True), tile)
        ar_row[it, me_r] = tile
        for d in row_order:
            copy = remote(
                ar_row.at[it, me_r], ar_row.at[it, me_r], rs.at[it, d], rr.at[it, me_r],
                lax.rem(me_r + d, n_row), me_c,
            )
            copy.start()
            pending.append(copy)

    def dots_middle(it):
        for d in row_order:
            far = lax.rem(me_r + d, n_row)
            remote(ar_row.at[it, far], ar_row.at[it, far], rs.at[it, d], rr.at[it, far], me_r, me_c).wait_recv()
        ar_col[it, me_c] = jnp.sum(ar_row[it], axis=0)
        for d in col_order:
            copy = remote(
                ar_col.at[it, me_c], ar_col.at[it, me_c], cs.at[it, d], cr.at[it, me_c],
                me_r, lax.rem(me_c + d, n_col),
            )
            copy.start()
            pending.append(copy)

    def dots_end(it, n):
        for d in col_order:
            far = lax.rem(me_c + d, n_col)
            remote(ar_col.at[it, far], ar_col.at[it, far], cs.at[it, d], cr.at[it, far], me_r, me_c).wait_recv()
        t = jnp.sum(ar_col[it], axis=0)
        t = t + pltpu.roll(t, 4, 0)
        t = t + pltpu.roll(t, 2, 0)
        return [t[:, d:d + 1] for d in range(n)]

    def times(c, v):
        return jnp.concatenate([c] * (v.shape[0] // 8), axis=0) * v

    rank_of = iota((CAP, side), 0)

    def by_owner(values_of):
        total = None
        for b in range(n_blk):
            mine = rank_of == rank_sc[b:b + 1, :].astype(jnp.int32)
            placed = jnp.concatenate([jnp.where(mine, v, 0.0) for v in values_of(b)], axis=0)
            for part in split3(placed):
                more = nn_dot(part, own_hot[b])
                total = more if total is None else total + more
        return total

    def both(v):
        return lambda b: [v[2 * b:2 * b + 1, :], v[2 * b + 1:2 * b + 2, :]]

    def offsets(b):
        return [r[b * side:(b + 1) * side].reshape(1, side).astype(F32) for r in (roff_ref, coff_ref)]

    r0 = xbuf[0, own_lo:own_lo + rows, :]
    own_products(0, r0)
    apply(0)
    table_r0 = by_owner(both(r0))
    table_off = by_owner(offsets)
    w0 = applied(0)
    xbuf[1, own_lo:own_lo + rows, :] = w0
    forward(1)
    dots_start(0, [(r0, r0), (r0, w0)])
    own_products(1, w0)
    apply(1, lambda: dots_middle(0))
    early = jnp.transpose(jnp.concatenate([table_r0, by_owner(both(w0))], axis=0))
    for o in range(n_dev):
        out_rows[o // n_col, o % n_col, :, 0:4 * CAP] = early[o:o + 1, :]
    empty = iota((CAP, n_dev), 0).astype(F32) >= held
    table_off = jnp.concatenate([jnp.where(empty, NONE, table_off[0:CAP]), table_off[CAP:]], axis=0)
    gamma0, curve0 = dots_end(0, 2)
    alpha0 = gamma0 / curve0
    z0 = applied(1)
    w1 = w0 - times(alpha0, z0)
    xbuf[2, own_lo:own_lo + rows, :] = w1
    r1 = r0 - times(alpha0, w0)
    dots_start(1, [(r1, r1), (r1, w1), (r1, w0)])
    forward(2)

    late = jnp.transpose(jnp.concatenate([by_owner(both(w1)), table_off], axis=0))
    for o in range(n_dev):
        out_rows[o // n_col, o % n_col, :, 4 * CAP:8 * CAP] = late[o:o + 1, :]
    keep = pltpu.make_async_copy(out_rows.at[me_r], mid_rows.at[:, me_r], keep_sem.at[0])
    keep.start()
    for d in row_order:
        far = lax.rem(me_r + d, n_row)
        copy = remote(out_rows.at[far], mid_rows.at[:, me_r], away1.at[d], got.at[me_r], far, me_c)
        copy.start()
        pending.append(copy)

    dots_middle(1)

    keep.wait()
    for d in row_order:
        far = lax.rem(me_r + d, n_row)
        remote(out_rows.at[far], mid_rows.at[:, far], away1.at[d], got.at[far], me_r, me_c).wait_recv()
    keep2 = pltpu.make_async_copy(mid_rows.at[me_c], end_rows.at[me_c], keep_sem.at[1])
    keep2.start()
    for d in col_order:
        far = lax.rem(me_c + d, n_col)
        copy = remote(mid_rows.at[far], end_rows.at[me_c], away2.at[d], land.at[me_c], me_r, far)
        copy.start()
        pending.append(copy)

    own_products(2, w1)
    forward_wait(2)
    gather_far(2)
    far_r1 = far_sum[0] - grouped(alpha0, far_sum[1])
    down_r1 = down_sum[0] - grouped(alpha0, down_sum[1])
    far_w1 = over_parts(gath[...])
    weights = weight_sc[...]
    weights = jnp.concatenate([weights[b:b + 1] for b in range(n_blk) for _ in (0, 1)], axis=0)
    gamma1, r1w1, r1w0 = dots_end(1, 3)
    beta0 = gamma1 / gamma0
    curve1 = r1w1 + 2.0 * beta0 * r1w0 + beta0 * beta0 * curve0
    alpha1 = gamma1 / curve1
    p1 = r1 + times(beta0, r0)
    s1 = w1 + times(beta0, w0)
    r2 = r1 - times(alpha1, s1)

    far_r2 = far_r1 - grouped(alpha1, far_w1 + grouped(beta0, far_sum[1]))
    down_r2 = down_r1 - grouped(alpha1, down_sum[2] + grouped(beta0, down_sum[1]))
    cross = far_r2 * (sums_sc[...] * far_r2 - 2.0 * down_r2)
    cross = jnp.sum(cross.reshape(q_own // 8, 8, side), axis=0)
    cross = jnp.where(iota((8, side), 0) < 2, cross, 0.0)
    dots_start(2, [(r2, weights * r2), (r2, r2), (r2, s1)], more=cross)

    keep2.wait()
    for d in col_order:
        far = lax.rem(me_c + d, n_col)
        remote(mid_rows.at[far], end_rows.at[far], away2.at[d], land.at[far], me_r, me_c).wait_recv()
    dots_middle(2)
    for o in range(n_dev):
        table_sc[o:o + 1, :] = end_rows[o // n_row, o % n_row]
    curve_r2, gamma2, r2s1 = dots_end(2, 3)
    beta1 = gamma2 / gamma1
    curve2 = curve_r2 + 2.0 * beta1 * r2s1 + beta1 * beta1 * curve1
    alpha2 = gamma2 / curve2

    of_b = alpha0 + alpha1 * (1.0 + beta0) + alpha2 * (1.0 + beta1 * (1.0 + beta0))
    of_w0 = -alpha1 * alpha0 - alpha2 * (alpha0 + alpha1 * beta0 + beta1 * alpha0)
    of_w1 = -alpha2 * alpha1
    lane = iota((1, 128), 1)

    def by_lane(first, second):
        return jnp.where(
            lane < CAP, first[0:1], jnp.where(lane < 2 * CAP, first[1:2], jnp.where(lane < 3 * CAP, second[0:1], second[1:2]))
        )

    near = table_sc[:, 0:128] * by_lane(of_b, of_w0)
    far = table_sc[:, 128:256]
    moved = near + pltpu.roll(near, 64, 1) + far * by_lane(of_w1, of_w1)
    pos_ref[...] = pltpu.roll(far, 64, 1) + 3.0 * jnp.tanh(moved)

    x = times(alpha0, r0) + times(alpha1, p1) + times(alpha2, r2 + times(beta1, p1))
    for b in range(n_blk):
        sol_ref[b] = x[2 * b:2 * b + 2, :]
    for copy in pending:
        copy.wait_send()


def solve(n_row, n_col, neighbours, right_side, anchor, owners, row_offset, col_offset, tiles):
    n_blk, fan, side, _ = tiles.shape
    rows = 2 * n_blk
    n_dev = n_row * n_col
    q_all = n_blk * fan * 8 + n_blk * 8
    vmem = pl.BlockSpec(memory_space=pltpu.VMEM)
    dma = pltpu.SemaphoreType.DMA
    return pl.pallas_call(
        functools.partial(solve_kernel, n_row, n_col),
        name="solve_and_route",
        out_shape=(
            jax.ShapeDtypeStruct(right_side.shape, F32),
            jax.ShapeDtypeStruct((n_dev, 128), F32),
        ),
        in_specs=[pl.BlockSpec(memory_space=pltpu.HBM)] * 7,
        out_specs=(vmem, vmem),
        scratch_shapes=[
            pltpu.VMEM(tiles.shape, F32),
            pltpu.VMEM(tiles.shape, BF16),
            pltpu.VMEM(tiles.shape, BF16),
            pltpu.VMEM((3, side, side), F32),
            pltpu.VMEM((q_all, 3 * side), BF16),
            pltpu.VMEM((side, 384), BF16),
            pltpu.VMEM((8 * n_blk * fan, side), F32),
            pltpu.VMEM((384, side), F32),
            pltpu.VMEM((2, 9 * rows, side), F32),
            pltpu.VMEM((2, 9, rows, side), F32),
            pltpu.VMEM((3, n_row, 8, 128), F32),
            pltpu.VMEM((3, n_col, 8, 128), F32),
            pltpu.VMEM((n_blk, side, n_dev), BF16),
            pltpu.VMEM((n_blk, side), F32),
            pltpu.VMEM((n_blk, side), F32),
            pltpu.VMEM((n_row, n_col, 1, 8 * CAP), F32),
            pltpu.VMEM((n_col, n_row, 1, 8 * CAP), F32),
            pltpu.VMEM((n_col, n_row, 1, 8 * CAP), F32),
            pltpu.VMEM((n_dev, 8 * CAP), F32),
            pltpu.VMEM((8 * n_blk, 4 * rows), BF16),
            pltpu.VMEM((8 * n_blk, side), F32),
            pltpu.VMEM((8 * n_blk * fan, side), F32),
            pltpu.VMEM((8 * n_blk * fan, side), F32),
            pltpu.VMEM((2, 8 * n_blk * fan, side), F32),
            pltpu.VMEM((3, 8 * n_blk * fan, side), F32),
            pltpu.SMEM((fan, n_blk), jnp.int32),
            pltpu.VMEM(right_side.shape, F32),
            pltpu.VMEM(anchor.shape, F32),
            pltpu.VMEM(owners.shape, jnp.int32),
            pltpu.VMEM(row_offset.shape, jnp.int32),
            pltpu.VMEM(col_offset.shape, jnp.int32),
            dma((6,)),
            dma((n_blk,)),
            dma((3, 9)), dma((3, 9)), dma((3, 9)), dma((3, 9)),
            dma((3, n_row)), dma((3, n_row)), dma((3, n_col)), dma((3, n_col)),
            dma((n_row,)), dma((n_row,)), dma((n_col,)), dma((n_col,)), dma((2,)),
        ],
        compiler_params=pltpu.CompilerParams(
            collective_id=0, has_side_effects=True, vmem_limit_bytes=63480000
        ),
        cost_estimate=pl.CostEstimate(flops=10**9, bytes_accessed=2**23, transcendentals=0),
    )(neighbours, right_side, anchor, owners, row_offset, col_offset, tiles)


def grid_kernel(
    n_row, n_col,
    pos_ref, macro_ref, two, side, rims,
    one, bell_col, left_sel, right_sel, low_part, high_part, place,
    top_s, bottom_s, west_s, east_s, up_r, down_r, west_r, east_r, keep_top, keep_bottom,
    in_sem, ss, rs,
):
    length, width = macro_ref.shape
    n_dev = n_row * n_col
    n_slot = bell_col.shape[0]
    n_chunk = length // CHUNK
    me_r = lax.axis_index("row")
    me_c = lax.axis_index("col")
    log2e = 1.4426950408889634

    def at(dr, dc):
        return lax.rem(me_r + dr + n_row, n_row), lax.rem(me_c + dc + n_col, n_col)

    def load(i):
        return pltpu.make_async_copy(
            macro_ref.at[pl.ds(i * BAND, BAND)], one.at[pl.ds(8 + i * BAND, BAND)], in_sem.at[i]
        )

    barrier = pltpu.get_barrier_semaphore()
    around = sorted((g for g in range(9) if g != 4), key=lambda g: -abs(AROUND[g][0]) - 2 * abs(AROUND[g][1]))
    for g in around:
        row, col = at(*AROUND[g])
        pl.semaphore_signal(barrier, inc=1, device_id={"row": row, "col": col}, device_id_type=MESH)
    for i in range(length // BAND):
        load(i).start()
    rim = jnp.zeros((8, width), F32)
    for buf in (one, two):
        buf[0:8, :] = rim
        buf[length + 8:length + 16, :] = rim

    turned = jnp.transpose(pos_ref[...])
    at_row = turned[0:CAP]
    start = jnp.clip(jnp.floor(at_row) - 7.0, 0.0, length - 16.0)
    block = jnp.floor(start * (1.0 / 32.0))
    rows48 = iota((48, n_dev), 0).astype(F32)
    for j in range(CAP):
        u = rows48 + 32.0 * block[j:j + 1]
        d = u - at_row[j:j + 1]
        inside = jnp.abs(u - (start[j:j + 1] + 7.5)) < 8.0
        bell = jnp.where(inside, jnp.exp2(d * d * (-0.5 * log2e)), 0.0).astype(BF16)
        here = slice(j * n_dev, (j + 1) * n_dev)
        low_part[:, here] = bell[0:32]
        high_part[:, here] = jnp.concatenate([bell[32:48], jnp.zeros((16, n_dev), BF16)], axis=0)
        place[:, here] = jnp.broadcast_to(block[j:j + 1], (32, n_dev)).astype(BF16)

    all_pos = pos_ref[...]
    at_col = pltpu.roll(all_pos, 128 - CAP, 1)
    middle = jnp.clip(jnp.floor(at_col) - 7.0, 0.0, width - 16.0) + 7.5
    v = iota((1, width), 1).astype(F32)

    def some_columns(i, carry):
        p, m = carry
        for k in range(8):
            d = v - p[:, k:k + 1]
            inside = jnp.abs(v - m[:, k:k + 1]) < 8.0
            bell = jnp.where(inside, jnp.exp2(d * d * (-0.5 * log2e)), 0.0)
            bell_col[pl.ds(pl.multiple_of((i * 8 + k) * n_dev, n_dev), n_dev), :] = bell.astype(BF16)
        return pltpu.roll(p, 120, 1), pltpu.roll(m, 120, 1)

    lax.fori_loop(0, CAP // 8, some_columns, (at_col, middle))

    def build(dst, band):
        for sub in range(BAND // 32):
            block_id = (band * (BAND // 32) + sub).astype(F32)
            first = place[...] == jnp.full((32, n_slot), block_id, F32).astype(BF16)
            second = place[...] == jnp.full((32, n_slot), block_id - 1.0, F32).astype(BF16)
            zero = jnp.zeros((32, n_slot), BF16)
            dst[sub * 32:(sub + 1) * 32, :] = jnp.where(
                first, low_part[...], jnp.where(second, high_part[...], zero)
            )

    def product(src, band):
        load(band).wait()
        here = pl.ds(pl.multiple_of(8 + band * BAND, 8), BAND)
        one[here, :] = one[here, :] + nn_dot(src[...], bell_col[...])

    build(left_sel, jnp.int32(0))

    def two_bands(i, carry):
        build(right_sel, 2 * i + 1)
        product(left_sel, 2 * i)
        build(left_sel, jnp.minimum(2 * i + 2, length // BAND - 1))
        product(right_sel, 2 * i + 1)
        return carry

    lax.fori_loop(0, length // BAND // 2, two_bands, 0)

    top_s[...] = one[8:16, :]
    bottom_s[...] = one[length:length + 8, :]
    keep_top[...] = one[8:24, :]
    keep_bottom[...] = one[length - 8:length + 8, :]
    lane = iota((1, 128), 1)
    for i in range(length // 128):
        here = slice(8 + i * 128, 8 + (i + 1) * 128)
        tile = jnp.transpose(jnp.where(lane < 64, one[here, 0:128], one[here, width - 128:width]))
        west_s[:, i * 128:(i + 1) * 128] = tile[0:8]
        east_s[:, i * 128:(i + 1) * 128] = tile[120:128]

    pl.semaphore_wait(barrier, 8)
    first = (slice(None), pl.ds(0, 128))
    last = (slice(None), pl.ds(length - 128, 128))
    inner = (slice(None), pl.ds(128, length))
    above = (slice(None), pl.ds(0, 128))
    below = (slice(None), pl.ds(length + 128, 128))
    plan = {
        (-1, 0): (top_s, down_r),
        (1, 0): (bottom_s, up_r),
        (0, -1): (west_s, east_r.at[inner]),
        (0, 1): (east_s, west_r.at[inner]),
        (-1, -1): (west_s.at[first], east_r.at[below]),
        (-1, 1): (east_s.at[first], west_r.at[below]),
        (1, -1): (west_s.at[last], east_r.at[above]),
        (1, 1): (east_s.at[last], west_r.at[above]),
    }
    copies = []
    for g in around:
        src, dst = plan[AROUND[g]]
        row, col = at(*AROUND[g])
        copy = remote(src, dst, ss.at[g], rs.at[g], row, col)
        copy.start()
        copies.append(copy)

    for src, dst in ((one, two), (two, one), (one, two)):

        def strip(i, carry, src=src, dst=dst):
            begin = pl.multiple_of(8 + i * STRIP, 8)
            dst[pl.ds(begin, STRIP), :] = summed(src, begin, STRIP)
            return carry

        lax.fori_loop(0, length // STRIP, strip, 0)

    for copy in copies:
        copy.wait_recv()
    not_first_row = (me_r > 0).astype(F32)
    not_last_row = (me_r < n_row - 1).astype(F32)
    not_first_col = (me_c > 0).astype(F32)
    not_last_col = (me_c < n_col - 1).astype(F32)
    scale = 0.2 ** STEPS

    def cross(t):
        n, m = t.shape
        return (t + pltpu.roll(t, 1, 0)) + (pltpu.roll(t, n - 1, 0) + pltpu.roll(t, 1, 1)) + pltpu.roll(t, m - 1, 1)

    pad = jnp.zeros((120, 128), F32)
    corners = []
    for halo, order in ((up_r, 0), (down_r, 1)):
        for part in (halo[:, 0:128], halo[:, width - 128:width]):
            corners.append(jnp.transpose(jnp.concatenate([pad, part] if order == 0 else [part, pad], axis=0)))
    own_west = jnp.concatenate([corners[0][0:8], west_s[...], corners[2][0:8]], axis=1)
    own_east = jnp.concatenate([corners[1][120:128], east_s[...], corners[3][120:128]], axis=1)
    t = jnp.concatenate([west_r[...], own_west, own_east, east_r[...]], axis=0)
    down32 = iota((32, 1), 0)
    along = iota((1, length + 256), 1)
    mask = jnp.where(down32 < 8, not_first_col, jnp.where(down32 >= 24, not_last_col, 1.0)) * jnp.where(
        along < 128, jnp.where(along >= 120, not_first_row, 0.0),
        jnp.where(along >= length + 128, jnp.where(along < length + 136, not_last_row, 0.0), 1.0),
    )
    t = t * mask
    for step in range(STEPS):
        t = cross(t)
        if step < STEPS - 1:
            t = t * mask
    side[...] = t * scale

    def rim_rows(halo, kept, keep, at_top):
        r = jnp.concatenate([halo * keep, kept] if at_top else [kept, halo * keep], axis=0)
        near = iota((24, 1), 0)
        flag = jnp.where((near < 8) if at_top else (near >= 16), keep, 1.0)
        for step in range(STEPS):
            r = cross(r)
            if step < STEPS - 1:
                r = r * flag
        return (r[8:16] if at_top else r[8:16]) * scale

    rims[0:8, :] = rim_rows(up_r[...], keep_top[...], not_first_row, True)
    rims[8:16, :] = rim_rows(down_r[...], keep_bottom[...], not_last_row, False)
    for copy in copies:
        copy.wait_send()


def summed(src, begin, n):
    width = src.shape[1]
    window = src[pl.ds(pl.multiple_of(begin - 8, 8), n + 16), :]
    centre = window[8:8 + n]
    return (
        (centre + window[7:7 + n]) + (window[9:9 + n] + pltpu.roll(centre, 1, 1)) + pltpu.roll(centre, width - 1, 1)
    )


def last_step_kernel(two, side, rims, out_ref, one, out_sem):
    length, width = out_ref.shape
    n_chunk = length // CHUNK
    scale = 0.2 ** STEPS
    lane = iota((1, 128), 1)

    def store(i):
        here = pl.ds(pl.multiple_of(i * CHUNK, CHUNK), CHUNK)
        return pltpu.make_async_copy(one.at[here], out_ref.at[here], out_sem.at[i])

    zero112 = jnp.zeros((112, 128), F32)

    def finish(i, carry):
        total = summed(two, pl.multiple_of(8 + i * CHUNK, 8), CHUNK) * scale
        for h in range(CHUNK // 128):
            rows_h = slice(h * 128, (h + 1) * 128)
            at_lane = pl.ds(pl.multiple_of(i * CHUNK + (h + 1) * 128, 128), 128)
            tile = jnp.transpose(jnp.concatenate([side[8:16, at_lane], zero112, side[16:24, at_lane]], axis=0))
            here = pl.ds(pl.multiple_of(i * CHUNK + h * 128, 8), 128)
            one[here, 0:128] = jnp.where(lane < 4, tile, total[rows_h, 0:128])
            one[here, 128:width - 128] = total[rows_h, 128:width - 128]
            one[here, width - 128:width] = jnp.where(lane >= 124, tile, total[rows_h, width - 128:width])
        return carry

    def rim(at_row, rim8):
        here = slice(at_row, at_row + 8)
        one[here, 0:128] = jnp.where(lane < 4, one[here, 0:128], rim8[:, 0:128])
        one[here, 128:width - 128] = rim8[:, 128:width - 128]
        one[here, width - 128:width] = jnp.where(lane >= 124, one[here, width - 128:width], rim8[:, width - 128:width])

    finish(jnp.int32(0), 0)
    rim(0, rims[0:8, :])
    store(0).start()

    def start_store(i, carry):
        finish(i, carry)
        store(i).start()
        return carry

    lax.fori_loop(1, n_chunk - 1, start_store, 0)
    finish(jnp.int32(n_chunk - 1), 0)
    rim(length - 8, rims[8:16, :])
    store(n_chunk - 1).start()

    def finish_store(i, carry):
        store(i).wait()
        return carry

    lax.fori_loop(0, n_chunk, finish_store, 0)


def last_step(three, side, rims):
    length, width = three.shape[0] - 16, three.shape[1]
    vmem = pl.BlockSpec(memory_space=pltpu.VMEM)
    return pl.pallas_call(
        last_step_kernel,
        name="last_step",
        out_shape=jax.ShapeDtypeStruct((length, width), F32),
        in_specs=[vmem] * 3,
        out_specs=pl.BlockSpec(memory_space=pl.ANY),
        scratch_shapes=[pltpu.VMEM((length, width), F32), pltpu.SemaphoreType.DMA((length // CHUNK,))],
        compiler_params=pltpu.CompilerParams(vmem_limit_bytes=16 * 2**20),
        cost_estimate=pl.CostEstimate(flops=5 * length * width, bytes_accessed=8 * length * width, transcendentals=0),
    )(three, side, rims)


CHUNK = 256
STRIP = 512
BAND = 256


def spread_and_diffuse(n_row, n_col, positions, macro):
    length, width = macro.shape
    n_slot = n_row * n_col * CAP
    any_space = pl.BlockSpec(memory_space=pl.ANY)
    vmem = pl.BlockSpec(memory_space=pltpu.VMEM)
    dma = pltpu.SemaphoreType.DMA
    return pl.pallas_call(
        functools.partial(grid_kernel, n_row, n_col),
        name="spread_and_diffuse",
        out_shape=(
            jax.ShapeDtypeStruct((length + 16, width), F32),
            jax.ShapeDtypeStruct((32, length + 256), F32),
            jax.ShapeDtypeStruct((16, width), F32),
        ),
        in_specs=[vmem, any_space],
        out_specs=(vmem,) * 3,
        scratch_shapes=[
            pltpu.VMEM((length + 16, width), F32),
            pltpu.VMEM((n_slot, width), BF16),
            pltpu.VMEM((BAND, n_slot), BF16),
            pltpu.VMEM((BAND, n_slot), BF16),
            pltpu.VMEM((32, n_slot), BF16),
            pltpu.VMEM((32, n_slot), BF16),
            pltpu.VMEM((32, n_slot), BF16),
            pltpu.VMEM((8, width), F32),
            pltpu.VMEM((8, width), F32),
            pltpu.VMEM((8, length), F32),
            pltpu.VMEM((8, length), F32),
            pltpu.VMEM((8, width), F32),
            pltpu.VMEM((8, width), F32),
            pltpu.VMEM((8, length + 256), F32),
            pltpu.VMEM((8, length + 256), F32),
            pltpu.VMEM((16, width), F32),
            pltpu.VMEM((16, width), F32),
            dma((length // BAND,)),
            dma((9,)),
            dma((9,)),
        ],
        compiler_params=pltpu.CompilerParams(
            collective_id=1, has_side_effects=True, vmem_limit_bytes=24 * 2**20
        ),
        cost_estimate=pl.CostEstimate(flops=10**10, bytes_accessed=8 * length * width, transcendentals=0),
    )(positions, macro)


def per_device(right_side, anchor, tiles, neighbours, owners, row_offset, col_offset, macro_density):
    n_row, n_col = lax.axis_size("row"), lax.axis_size("col")
    solution, arrived = solve(
        n_row, n_col, neighbours.T, right_side, anchor, owners.T, row_offset, col_offset, tiles,
    )
    return solution, last_step(*spread_and_diffuse(n_row, n_col, arrived, macro_density))


def solution(mesh):
    blocks = P(("row", "col"))
    return jax.shard_map(
        per_device,
        mesh=mesh,
        in_specs=(
            P(("row", "col"), None, None),
            P(("row", "col"), None),
            P(("row", "col"), None, None, None),
            P(("row", "col"), None),
            P(("row", "col"), None),
            blocks,
            blocks,
            P("row", "col"),
        ),
        out_specs=(P(("row", "col"), None, None), P("row", "col")),
        check_vma=False,
    )
```
